128 devices in a mesh: gx: 8 (over x_lo, z), gy: 16 (over y, x_hi, core).
Axes of the slice: x: 4 (x_hi: 2, x_lo: 2; x = x_hi * 2 + x_lo), y: 4, z: 4, core: 2. Of those that a mesh axis runs over, the one named last changes fastest.
Arguments:
- ice_force: float32 [2, 11, 256, 2048], P(None, None, 'gx', 'gy'), may hold values from -6 to 6
- ice_visc: float32 [10, 256, 2048], P(None, 'gx', 'gy'), may hold values from 0.2 to 5
- ice_drag: float32 [256, 2048], P('gx', 'gy'), may hold values from 0.5 to 5
- ice_mask: int32 [256, 2048], P('gx', 'gy'), may hold values 0 or 1
- ice_thick: float32 [256, 2048], P('gx', 'gy'), may hold values from 0.1 to 1.5
- ice_target: int32 [4096], P(('gx', 'gy')), may hold values from -1 to 4095, as said below
- ocean_temp: float32 [80, 256, 2048], P(None, 'gx', 'gy'), may hold values from -2 to 1
- ocean_salt: float32 [80, 256, 2048], P(None, 'gx', 'gy'), may hold values from -2 to 2
- ocean_diff: float32 [256, 2048], P('gx', 'gy'), may hold values from 0.05 to 0.2
- ocean_mask: int32 [256, 2048], P('gx', 'gy'), may hold values 0 or 1
- ocean_source: int32 [4096], P(('gx', 'gy')), may hold values from 0 to 4095, as said below
Outputs:
- ice_velocity: float32 [2, 11, 256, 2048], P(None, None, 'gx', 'gy')
- ice_thick_new: float32 [256, 2048], P('gx', 'gy')
- ocean_temp_new: float32 [80, 256, 2048], P(None, 'gx', 'gy')
- ocean_salt_new: float32 [80, 256, 2048], P(None, 'gx', 'gy')
The draws below stay inside these ranges and needn't reach their ends.
Inputs may be any that keep to these rules, and one draw needn't show every extreme that they name: ice_target and ocean_source are inverse lists: every ocean block has exactly one ice block above it, no ice block feeds two; each ocean device takes exactly 1 block from each of its 32 source devices, so at most 1 block pass between any two devices and that bound is reached. `ice_target`: -1 for ice blocks over no cavity; each device has exactly 32 coupled blocks.
All inputs are finite; a program needn't handle non-finite values. No bound on the sum of `ice_mask` or of `ocean_mask` on one device may be relied on, other than what follows from the above.
Results may differ from the reference program's by a relative error of at most 0.0001.
Values sent between devices are 32-bit elements; how exact they have to be, the bound alone decides.
A program may use at most 128 MiB of HBM per device.

```python
import math
import jax
import jax.numpy as jnp
import numpy as np
from jax import lax

IX = 32
COLS = 128
OX = 32
LAYERS = 10
ZO = 80
SUBSTEPS = 4
MATVECS = 3
CAP = 1
NLEV = 11
NX = 256
NY = 2048
NXO = 256
NIB = 4096
NOB = 4096
N_GX = 8
N_GY = 16


def shuffled_rows(keys, count):
    return jax.vmap(partial_permutation(count))(keys)


def partial_permutation(count):

    def permuted(subkey):
        return jax.random.permutation(subkey, count)
    return permuted


def coupling_maps(key):
    device_count = N_GX * N_GY
    picks = OX // CAP
    key_offsets, key_ice, key_ocean = jax.random.split(key, 3)
    ranking = jax.random.permutation(key_offsets, device_count).astype(jnp.int32)
    every_offset = jnp.arange(device_count, dtype=jnp.int32)
    scores = jnp.where(every_offset == 1, -3, jnp.where(every_offset == device_count - 1, -2, jnp.where(every_offset == device_count // 2, -1, ranking)))
    offsets = jnp.argsort(scores, stable=True)[:picks].astype(jnp.int32)
    ice_perm = shuffled_rows(jax.random.split(key_ice, device_count), IX)
    ocean_perm = shuffled_rows(jax.random.split(key_ocean, device_count), OX)
    owner = jnp.arange(device_count, dtype=jnp.int32)[:, None]
    ranks = jnp.arange(OX, dtype=jnp.int32)[None, :]
    source_dev = (owner + offsets[ranks // CAP]) % device_count
    source_ids = source_dev * IX + ice_perm[source_dev, jnp.broadcast_to(ranks, source_dev.shape)]
    ocean_ids = owner * OX + ocean_perm[jnp.broadcast_to(owner, source_dev.shape), jnp.broadcast_to(ranks, source_dev.shape)]
    return (source_ids.reshape(-1).astype(jnp.int32), ocean_ids.reshape(-1).astype(jnp.int32))


def draw_ocean_source(key, part):
    source_ids, ocean_ids = coupling_maps(key)
    return jnp.zeros((NOB,), jnp.int32).at[ocean_ids].set(source_ids)


def draw_ice_target(key, part):
    source_ids, ocean_ids = coupling_maps(key)
    return jnp.full((NIB,), -1, jnp.int32).at[source_ids].set(ocean_ids)


def with_ends(drawn, stream_key, least, high):
    dims = drawn.shape
    place = [jax.random.randint(jax.random.fold_in(stream_key, axis), (), 0, dims[axis]) for axis in range(len(dims))]
    drawn = drawn.at[tuple(place)].set(least)
    longest = dims.index(max(dims))
    place[longest] = (place[longest] + 1) % dims[longest]
    return drawn.at[tuple(place)].set(high)


def block_scale(rng, shape, shards, least, top_value):
    level = 1.0
    for dim, blocks in shards:
        draws = jax.random.uniform(jax.random.fold_in(jax.random.fold_in(rng, 6), dim), (blocks,), jnp.float32, least / len(shards), top_value / len(shards))
        level = level * jnp.repeat(jnp.exp(draws), shape[dim] // blocks).reshape((-1,) + (1,) * (len(shape) - 1 - dim))
    return level


def noise(rng, extent, spread, most, cuts=(), kind=jnp.bfloat16):
    array = jax.random.normal(rng, extent, jnp.float32) * spread
    if len(cuts) > 0:
        array = block_scale(rng, extent, cuts, -0.22, 0.18) * array
    return jnp.clip(array, min=-most, max=most).astype(kind)


def setup_inputs(seed: int = 0) -> dict:
    key_of = jax.random.split(jax.random.key(seed), 12)
    return {
        "ice_force": noise(key_of[0], (2, NLEV, NX, NY), 1.0, 6.0, ((2, 8), (3, 16)), jnp.float32),
        "ice_visc": jnp.clip(jnp.exp(math.log(5.0) - 3.218876 * jax.random.uniform(key_of[1], (LAYERS, NX, NY), jnp.float32) ** block_scale(key_of[1], (LAYERS, NX, NY), ((1, 8), (2, 16)), -0.2, 0.2)), 0.2, 5.0),
        "ice_drag": jnp.clip(jnp.exp(math.log(5.0) - 2.3025851 * jax.random.uniform(key_of[2], (NX, NY), jnp.float32) ** block_scale(key_of[2], (NX, NY), ((0, 8), (1, 16)), -0.2, 0.2)), 0.5, 5.0),
        "ice_mask": with_ends((jax.random.randint(key_of[3], (NX, NY), 0, 4) < 3).astype(jnp.int32), jax.random.fold_in(key_of[3], 1), 0, 1),
        "ice_thick": jnp.clip(jnp.exp(math.log(1.5) - 2.7080502 * jax.random.uniform(key_of[4], (NX, NY), jnp.float32) ** block_scale(key_of[4], (NX, NY), ((0, 8), (1, 16)), -0.2, 0.2)), 0.1, 1.5),
        "ice_target": draw_ice_target(jax.random.fold_in(key_of[11], 71), 0),
        "ocean_temp": jnp.clip(-2.0 + 3.0 * jax.random.uniform(key_of[6], (ZO, NXO, NY), jnp.float32) ** block_scale(key_of[6], (ZO, NXO, NY), ((1, 8), (2, 16)), -0.2, 0.2), -2.0, 1.0),
        "ocean_salt": noise(key_of[7], (ZO, NXO, NY), 0.3, 2.0, ((1, 8), (2, 16)), jnp.float32),
        "ocean_diff": jnp.clip(jnp.exp(math.log(0.2) - 1.3862944 * jax.random.uniform(key_of[8], (NXO, NY), jnp.float32) ** block_scale(key_of[8], (NXO, NY), ((0, 8), (1, 16)), -0.2, 0.2)), 0.05, 0.2),
        "ocean_mask": with_ends((jax.random.randint(key_of[9], (NXO, NY), 0, 5) < 4).astype(jnp.int32), jax.random.fold_in(key_of[9], 1), 0, 1),
        "ocean_source": draw_ocean_source(jax.random.fold_in(key_of[11], 71), 0),
    }


relax_weight = 0.6
shift_term = 0.2
vert_mix = 0.1
heat_gamma = 0.5
heat_factor = 0.05
salt_factor = 0.05
salt_ref = 34.5
freeze_slope = -0.0573
freeze_base = 0.0832
freeze_depth = 0.761
melt_factor = 0.2
draft_ratio = 0.89

def element_table():
    gauss = [0.5 - 0.5 / np.sqrt(3.0), 0.5 + 0.5 / np.sqrt(3.0)]
    element_matrix = np.zeros((16, 16))
    for point_z in gauss:
        for point_x in gauss:
            for point_y in gauss:
                gradients = np.zeros((8, 3))
                for corner in range(8):
                    depth_off = corner // 4
                    row_off = corner // 2 % 2
                    col_off = corner % 2
                    shape_z = point_z if depth_off else 1.0 - point_z
                    shape_x = point_x if row_off else 1.0 - point_x
                    shape_y = point_y if col_off else 1.0 - point_y
                    sign_z = 1.0 if depth_off else -1.0
                    sign_x = 1.0 if row_off else -1.0
                    sign_y = 1.0 if col_off else -1.0
                    gradients[corner] = [sign_x * shape_y * shape_z, sign_y * shape_x * shape_z, sign_z * shape_x * shape_y]
                for first in range(8):
                    for second in range(8):
                        grad_a = gradients[first]
                        grad_b = gradients[second]
                        element_matrix[first, second] += 0.125 * (4 * grad_a[0] * grad_b[0] + grad_a[1] * grad_b[1] + grad_a[2] * grad_b[2])
                        element_matrix[first, 8 + second] += 0.125 * (2 * grad_a[0] * grad_b[1] + grad_a[1] * grad_b[0])
                        element_matrix[8 + first, second] += 0.125 * (2 * grad_a[1] * grad_b[0] + grad_a[0] * grad_b[1])
                        element_matrix[8 + first, 8 + second] += 0.125 * (4 * grad_a[1] * grad_b[1] + grad_a[0] * grad_b[0] + grad_a[2] * grad_b[2])
    return element_matrix.astype(np.float32)

def corner_stack(nodes):
    layer_count = nodes.shape[1] - 1
    row_count = nodes.shape[2] - 2
    col_count = nodes.shape[3] - 2
    portions = []
    for component in range(2):
        for corner in range(8):
            depth_off = corner // 4
            row_off = corner // 2 % 2
            col_off = corner % 2
            portions.append(nodes[component, depth_off:depth_off + layer_count, row_off:row_off + row_count + 1, col_off:col_off + col_count + 1])
    return jnp.stack(portions)

def scatter_owned(values, row_count, col_count):
    components = []
    zero_level = jnp.zeros((1, row_count, col_count), jnp.float32)
    for component in range(2):
        summed = None
        for corner in range(8):
            depth_off = corner // 4
            row_off = corner // 2 % 2
            col_off = corner % 2
            portion = values[component * 8 + corner, :, 1 - row_off:1 - row_off + row_count, 1 - col_off:1 - col_off + col_count]
            if depth_off:
                portion = jnp.concatenate([zero_level, portion], 0)
            else:
                portion = jnp.concatenate([portion, zero_level], 0)
            summed = portion if summed is None else summed + portion
        components.append(summed)
    return jnp.stack(components)

def apply_operator(nodes, weights_ext, element_matrix):
    row_count = nodes.shape[2] - 2
    col_count = nodes.shape[3] - 2
    stacked = corner_stack(nodes)
    products = jnp.einsum('ab,bkij->akij', element_matrix, stacked, precision=lax.Precision.HIGHEST)
    products = products * weights_ext[None, :, :row_count + 1, :col_count + 1]
    return scatter_owned(products, row_count, col_count)

def ice_solve(force, weights_ext, drag, element_matrix, extend):
    levels = force.shape[1]
    row_count = force.shape[2]
    col_count = force.shape[3]
    diag_extra = shift_term + jnp.concatenate([drag[None], jnp.zeros((levels - 1, row_count, col_count), jnp.float32)], 0)
    diag_values = jnp.diagonal(element_matrix)[:, None, None, None] * weights_ext[None, :, :row_count + 1, :col_count + 1]
    diagonal = scatter_owned(diag_values, row_count, col_count) + diag_extra[None]
    velocity = relax_weight * force / diagonal
    for iteration in range(MATVECS):
        applied = apply_operator(extend(velocity), weights_ext, element_matrix) + diag_extra[None] * velocity
        velocity = velocity + relax_weight * (force - applied) / diagonal
    return velocity

def freezing(salt_top, draft):
    return freeze_slope * (salt_ref + salt_top) + freeze_base - freeze_depth * draft

def ocean_substep(fields, static):
    row_count = fields.shape[2] - 2
    col_count = fields.shape[3] - 2
    center = fields[:, :, 1:-1, 1:-1]
    diff_mid = static[0, 1:-1, 1:-1]
    wet_mid = static[1, 1:-1, 1:-1]
    draft_mid = static[2, 1:-1, 1:-1]
    lateral = jnp.zeros_like(center)
    for row_start, col_start in ((0, 1), (2, 1), (1, 0), (1, 2)):
        diff_near = static[0, row_start:row_start + row_count, col_start:col_start + col_count]
        wet_near = static[1, row_start:row_start + row_count, col_start:col_start + col_count]
        near = fields[:, :, row_start:row_start + row_count, col_start:col_start + col_count]
        lateral = lateral + 0.5 * (diff_mid + diff_near) * wet_mid * wet_near * (near - center)
    vert_flux = vert_mix * (center[:, 1:] - center[:, :-1])
    zero_level = jnp.zeros((2, 1, row_count, col_count), jnp.float32)
    vertical = jnp.concatenate([vert_flux, zero_level], 1) - jnp.concatenate([zero_level, vert_flux], 1)
    updated = center + lateral + wet_mid * vertical
    temp_top = updated[0, 0]
    salt_top = updated[1, 0]
    melt_rate = heat_gamma * (temp_top - freezing(salt_top, draft_mid)) * wet_mid
    updated = updated.at[0, 0].set(temp_top - heat_factor * melt_rate)
    updated = updated.at[1, 0].set(salt_top - salt_factor * melt_rate * (salt_ref + salt_top) / salt_ref)
    return updated

def to_blocks(field, row_count):
    return field.reshape(N_GX, row_count, N_GY, COLS).transpose(0, 2, 1, 3).reshape(N_GX * N_GY * row_count, COLS)

def from_blocks(blocks, row_count):
    return blocks.reshape(N_GX, N_GY, row_count, COLS).transpose(0, 2, 1, 3).reshape(N_GX * row_count, N_GY * COLS)

def pad_nodes(velocity):
    return jnp.pad(velocity, ((0, 0), (0, 0), (1, 1), (1, 1)))

def reference(ice_force, ice_visc, ice_drag, ice_mask, ice_thick, ice_target, ocean_temp, ocean_salt, ocean_diff, ocean_mask, ocean_source):
    element_matrix = jnp.asarray(element_table())
    ice_wet = ice_mask.astype(jnp.float32)
    weights = ice_visc * ice_wet[None]
    weights_ext = jnp.pad(weights, ((0, 0), (1, 1), (1, 1)))
    velocity = ice_solve(ice_force, weights_ext, ice_drag, element_matrix, pad_nodes)
    draft_blocks = to_blocks(draft_ratio * ice_thick, IX)
    ocean_draft = from_blocks(draft_blocks[ocean_source], OX)
    wet = ocean_mask.astype(jnp.float32)
    static = jnp.stack([ocean_diff, wet, ocean_draft])
    static_ext = jnp.pad(static, ((0, 0), (1, 1), (1, 1)))
    fields = jnp.stack([ocean_temp, ocean_salt])
    for substep_index in range(SUBSTEPS):
        fields = ocean_substep(jnp.pad(fields, ((0, 0), (0, 0), (1, 1), (1, 1))), static_ext)
    melt_rate = heat_gamma * (fields[0, 0] - freezing(fields[1, 0], ocean_draft)) * wet
    melt_blocks = to_blocks(melt_rate, OX)
    coupled = ice_target >= 0
    ice_melt_blocks = jnp.where(coupled[:, None], melt_blocks[jnp.where(coupled, ice_target, 0)], 0.0)
    ice_melt = from_blocks(ice_melt_blocks, IX)
    ice_thick_new = ice_thick - melt_factor * ice_melt * ice_wet
    return (velocity, ice_thick_new, fields[0], fields[1])
```

```python
import jax
import jax.numpy as jnp
from jax import lax
from jax.experimental import pallas as pl
from jax.experimental.pallas import tpu as pltpu
from jax.sharding import PartitionSpec as P

MESH = pl.DeviceIdType.MESH
F32 = jnp.float32

LANES = 128
SUB = 8
ROWS = 32
TILES = ROWS // SUB
ZO = 80
NODES = 11
CELLS = 10
STEPS = 4
SWEEPS = 3
CHUNK = 8
FBASE = 8
FSPAN = (ZO + 2) * ROWS
FROWS = 2 * FBASE + 2 * FSPAN
VSPAN = 40
VROWS = (NODES + 16) * VSPAN

relax_weight = 0.6
shift_term = 0.2
vert_mix = 0.1
heat_gamma = 0.5
heat_factor = 0.05
salt_factor = 0.05
salt_ref = 34.5
freeze_slope = -0.0573
freeze_base = 0.0832
freeze_depth = 0.761
melt_factor = 0.2
draft_ratio = 0.89

MASS = {"s": 1.0 / 4.0, "d": 1.0 / 12.0}


def same_weight(z, x, y, along):
    wx, wy = (4.0, 1.0) if along == 0 else (1.0, 4.0)
    total = 0.0
    if x == "d":
        total += wx * MASS[y] * MASS[z]
    if y == "d":
        total += wy * MASS[x] * MASS[z]
    if z == "d":
        total += MASS[x] * MASS[y]
    return total


DIAGONAL = 2.0 / 3.0


def iota(shape, axis):
    return lax.broadcasted_iota(jnp.int32, shape, axis)


def roll(value, shift, axis):
    size = value.shape[axis]
    if isinstance(shift, int):
        shift = shift % size
        if shift == 0:
            return value
    return pltpu.roll(value, shift, axis)


def plane_sums(lo, lo_right, hi, hi_right):
    ls, ld = lo + lo_right, lo_right - lo
    hs, hd = hi + hi_right, hi_right - hi
    return {"ss": ls + hs, "sd": ld + hd, "ds": hs - ls, "dd": hd - ld}


def element_forces(u_low, u_high, v_low, v_high, mu):
    u, v = {}, {}
    for xy in ("ss", "sd", "ds", "dd"):
        if xy != "ss":
            u["s" + xy] = u_low[xy] + u_high[xy]
            v["s" + xy] = v_low[xy] + v_high[xy]
        u["d" + xy] = u_high[xy] - u_low[xy]
        v["d" + xy] = v_high[xy] - v_low[xy]
    scaled = {}

    def times_mu(factor):
        if factor not in scaled:
            scaled[factor] = mu * factor
        return scaled[factor]

    fu, fv = {}, {}
    for key in u:
        z, xy = key[0], key[1:]
        for along, mine, other, out in ((0, u, v, fu), (1, v, u, fv)):
            own = same_weight(z, xy[0], xy[1], along)
            if xy in ("ds", "sd"):
                first = xy == "ds"
                double = first if along == 0 else not first
                cross = MASS[z] * (2.0 if double else 1.0) / 4.0
                swapped = z + ("sd" if first else "ds")
                out[key] = times_mu(own) * (mine[key] + (cross / own) * other[swapped])
            else:
                out[key] = times_mu(own) * mine[key]
    return fu, fv


def lower_part(f):
    out = {xy: f["s" + xy] - f["d" + xy] for xy in ("sd", "ds", "dd")}
    out["ss"] = -f["dss"]
    return out


def upper_part(f):
    out = {xy: f["s" + xy] + f["d" + xy] for xy in ("sd", "ds", "dd")}
    out["ss"] = f["dss"]
    return out


def packed_place(field, chunk):
    return field + (chunk // 8) * (2 - field), (chunk % 8) * 16 + (chunk // 8) * (32 * field)


def kernel(
    force, visc, drag, imask, thick, target, temp, salt, diff, omask, source,
    vel_out, thick_out, temp_out, salt_out,
    fa, fb, coef, opack, orow, rpack, rrow, merged,
    va, vb, mu, rdiag, ipack, imsg, rside, rmsg, rcorner,
    edge_e, col_lo, col_hi, col_mu, col_q, row_q, row_mu,
    wpack, wmsg, rwpack, rwmsg, rwcorner,
    pad_in, draft, tbl, mid, fwd, got,
    in_sem, o_send, o_recv, i_send, i_recv, w_send, w_recv, a_send, a_recv, b_send, b_recv,
):
    gx, gy = lax.axis_index("gx"), lax.axis_index("gy")
    nx, ny = lax.axis_size("gx"), lax.axis_size("gy")

    def at(dx, dy):
        return (lax.rem(gx + (dx + nx), nx), lax.rem(gy + (dy + ny), ny))

    north, south, west, east = at(-1, 0), at(1, 0), at(0, -1), at(0, 1)
    corners = (at(-1, -1), at(-1, 1), at(1, -1), at(1, 1))

    lane8 = iota((SUB, LANES), 1)
    sub8 = iota((SUB, LANES), 0)
    pair8 = lane8 // 2

    loads = []
    for field, ref in ((0, temp), (1, salt)):
        start = FBASE + field * FSPAN + ROWS
        loads.append(pltpu.make_async_copy(ref, fa.at[pl.ds(start, ZO * ROWS)], in_sem.at[field]))
    for copy in loads:
        copy.start()
    barrier = pltpu.get_barrier_semaphore()
    peers = [north, south, *corners]
    peers += [at(0, q) for q in range(1, ny)] + [at(p, 0) for p in range(2, nx - 1)]
    for peer in peers:
        pl.semaphore_signal(barrier, inc=1, device_id=peer, device_id_type=MESH)

    has_n = (gx > 0).astype(F32)
    has_s = (gx < nx - 1).astype(F32)
    has_w = (gy > 0).astype(F32)
    has_e = (gy < ny - 1).astype(F32)

    sends = []

    def send(src, dst, ssem, rsem, device):
        copy = pltpu.make_async_remote_copy(
            src_ref=src, dst_ref=dst, send_sem=ssem, recv_sem=rsem, device_id=device, device_id_type=MESH
        )
        copy.start()
        sends.append(copy)
        return copy

    wet_ice = imask[...].astype(F32)
    wmsg[...] = jnp.zeros_like(wmsg)
    va[...] = jnp.zeros_like(va)
    vb[...] = jnp.zeros_like(vb)
    edge_e[...] = jnp.zeros_like(edge_e)
    col_lo[...] = jnp.zeros_like(col_lo)
    col_hi[...] = jnp.zeros_like(col_hi)
    col_mu[...] = jnp.zeros_like(col_mu)
    for t in range(TILES):
        acc = jnp.zeros((SUB, LANES), F32)
        wet_t = wet_ice[t * SUB : (t + 1) * SUB]
        for k in range(CELLS):
            rows = pl.ds(k * ROWS + t * SUB, SUB)
            weight = visc[rows] * wet_t
            mu[pl.ds(SUB + k * ROWS + t * SUB, SUB)] = weight
            acc = jnp.where(pair8 == k, roll(weight, 2 * k + 1, 1), acc)
        wpack[pl.ds(t * SUB, SUB)] = acc
    wmsg[pl.ds(0, 8)] = mu[pl.ds(SUB + ROWS - 1, 8, stride=ROWS)]
    wmsg[pl.ds(8, 2)] = mu[pl.ds(SUB + 8 * ROWS + ROWS - 1, 2, stride=ROWS)]
    wmsg[pl.ds(16, 1)] = wpack[pl.ds(ROWS - 1, 1)]

    lane1 = iota((SUB, LANES), 1)
    to_row = jnp.full((SUB, LANES), -1, jnp.int32)
    from_row = jnp.full((SUB, LANES), -1, jnp.int32)
    to_col = [jnp.full((SUB, LANES), -1, jnp.int32) for _ in range(TILES)]
    from_col = [jnp.full((SUB, LANES), -1, jnp.int32) for _ in range(TILES)]
    for i in range(ROWS):
        to_row = jnp.where(lane1 == i, target[i], to_row)
        from_row = jnp.where(lane1 == i, source[i], from_row)
        to_col[i // SUB] = jnp.where(sub8 == i % SUB, target[i], to_col[i // SUB])
        from_col[i // SUB] = jnp.where(sub8 == i % SUB, source[i], from_col[i // SUB])

    def slot_of(ids):
        device = ids >> 5
        return jnp.where(ids >= 0, (device & (ny - 1)) * nx + (device >> 4), -1)

    def by_slot(row):
        slots = slot_of(row)
        return jnp.concatenate(
            [(sub8 + n * SUB == slots).astype(F32) for n in range(LANES // SUB)], axis=0
        )

    def by_device(cols):
        return jnp.concatenate(
            [((lane8 == (ids >> 5)) & (ids >= 0)).astype(F32) for ids in cols], axis=0
        )

    def pick(one_hot, values):
        return jnp.dot(one_hot, values, precision=lax.Precision.HIGHEST, preferred_element_type=F32)

    pad_in[...] = jnp.zeros_like(pad_in)
    pad_in[pl.ds(0, ROWS)] = draft_ratio * thick[...]
    tbl[0] = pick(by_slot(to_row), pad_in[...])

    for copy in loads:
        copy.wait()

    def guard(ref):
        for field in range(2):
            base = FBASE + field * FSPAN
            ref[pl.ds(base, ROWS)] = ref[pl.ds(base + ROWS, ROWS)]
            ref[pl.ds(base + (ZO + 1) * ROWS, ROWS)] = ref[pl.ds(base + ZO * ROWS, ROWS)]

    def put_pack(r, field, chunk, t, acc):
        vec, lane = packed_place(field, chunk)
        rows = pl.ds(pl.multiple_of(vec * ROWS + t * SUB, SUB), SUB)
        shifted = pltpu.roll(acc, lane, 1)
        mine = (lane8 >= lane) & (lane8 < lane + 16)
        opack[r, rows] = jnp.where(mine, shifted, opack[r, rows])

    def put_rows(r, ref, field, chunk):
        base = FBASE + field * FSPAN + ROWS + chunk * (CHUNK * ROWS)
        rows = pl.ds(pl.multiple_of(field * ZO + chunk * CHUNK, SUB), SUB)
        orow[r, 0, rows] = ref[pl.ds(base, SUB, stride=ROWS)]
        orow[r, 1, rows] = ref[pl.ds(base + ROWS - 1, SUB, stride=ROWS)]

    opack[...] = jnp.zeros_like(opack)
    orow[...] = jnp.zeros_like(orow)

    def first_edges(chunk, carry):
        for field in range(2):
            base = FBASE + field * FSPAN + ROWS + chunk * (CHUNK * ROWS)
            for t in range(TILES):
                acc = jnp.zeros((SUB, LANES), F32)
                for j in range(CHUNK):
                    value = fa[pl.ds(pl.multiple_of(base + j * ROWS + t * SUB, SUB), SUB)]
                    acc = jnp.where(pair8 == j, roll(value, 2 * j + 1, 1), acc)
                put_pack(0, field, chunk, t, acc)
            put_rows(0, fa, field, chunk)
        return carry

    lax.fori_loop(0, ZO // CHUNK, first_edges, 0)
    guard(fa)
    wet = omask[...].astype(F32)
    diffusion = diff[...]
    orow[0, 0, pl.ds(2 * ZO, 1)] = diffusion[0:1]
    orow[0, 0, pl.ds(2 * ZO + 1, 1)] = wet[0:1]
    orow[0, 1, pl.ds(2 * ZO, 1)] = diffusion[ROWS - 1 :]
    orow[0, 1, pl.ds(2 * ZO + 1, 1)] = wet[ROWS - 1 :]
    for t in range(TILES):
        rows = pl.ds(2 * ROWS + t * SUB, SUB)
        acc = opack[0, rows]
        acc = jnp.where(pair8 == 32, roll(diffusion[t * SUB : (t + 1) * SUB], 65, 1), acc)
        acc = jnp.where(pair8 == 33, roll(wet[t * SUB : (t + 1) * SUB], 67, 1), acc)
        opack[0, rows] = acc

    pl.semaphore_wait(barrier, len(peers))

    def send_ocean(r):
        return [
            send(orow.at[r, 0], rrow.at[r, 1], o_send.at[r, 0], o_recv.at[r, 0], north),
            send(orow.at[r, 1], rrow.at[r, 0], o_send.at[r, 1], o_recv.at[r, 1], south),
            send(opack.at[r], rpack.at[r, 1], o_send.at[r, 2], o_recv.at[r, 2], west),
            send(opack.at[r], rpack.at[r, 0], o_send.at[r, 3], o_recv.at[r, 3], east),
        ]

    def scatter_first(n):
        copies = []
        for q in range(1, ny):
            peer = at(0, q)
            copies.append(
                send(
                    tbl.at[n, pl.ds(pl.multiple_of(peer[1] * nx, nx), nx)],
                    mid.at[n, pl.ds(pl.multiple_of(gy * nx, nx), nx)],
                    a_send.at[n, q], a_recv.at[n, q], peer,
                )
            )
        own = pl.ds(pl.multiple_of(gy * nx, nx), nx)
        mid[n, own] = tbl[n, own]
        return copies

    def scatter_second(n, copies):
        for copy in copies:
            copy.wait_recv()
        for p in range(nx):
            fwd[n, pl.ds(p * ny, ny)] = mid[n, pl.ds(p, ny, stride=nx)]
        copies = []
        for p in range(1, nx):
            peer = at(p, 0)
            copies.append(
                send(
                    fwd.at[n, pl.ds(pl.multiple_of(peer[0] * ny, ny), ny)],
                    got.at[n, pl.ds(pl.multiple_of(gx * ny, ny), ny)],
                    b_send.at[n, p], b_recv.at[n, p], peer,
                )
            )
        own = pl.ds(pl.multiple_of(gx * ny, ny), ny)
        got[n, own] = fwd[n, own]
        return copies

    weights = [
        send(wmsg, rwmsg, w_send.at[0], w_recv.at[0], south),
        send(wpack, rwpack, w_send.at[1], w_recv.at[1], east),
        send(wmsg.at[pl.ds(16, 8)], rwcorner, w_send.at[2], w_recv.at[2], corners[3]),
    ]
    ocean = send_ocean(0)
    coupling = scatter_first(0)

    for copy in weights:
        copy.wait_recv()
    row_mu[...] = rwmsg[pl.ds(0, 16)] * has_n
    even = (lane8 & 1) == 0
    for t in range(TILES):
        col_mu[pl.ds(SUB + t * SUB, SUB)] = jnp.where(even, rwpack[pl.ds(t * SUB, SUB)] * has_w, 0.0)
    even1 = (iota((1, LANES), 1) & 1) == 0
    col_mu[pl.ds(SUB - 1, 1)] = jnp.where(even1, rwcorner[pl.ds(0, 1)] * (has_w * has_n), 0.0)

    def put_ice_edges(r, ref):
        for c in range(2):
            for edge in range(2):
                start = c * NODES * VSPAN + edge * (ROWS - 1)
                imsg[r, edge, pl.ds(c * 16, 16)] = ref[pl.ds(start, 16, stride=VSPAN)]
        imsg[r, 0, pl.ds(32, 1)] = ipack[r, pl.ds(0, 1)]
        imsg[r, 1, pl.ds(32, 1)] = ipack[r, pl.ds(ROWS - 1, 1)]

    def send_ice(r):
        copies = [
            send(imsg.at[r, 0], rmsg.at[r, 1], i_send.at[r, 0], i_recv.at[r, 0], north),
            send(imsg.at[r, 1], rmsg.at[r, 0], i_send.at[r, 1], i_recv.at[r, 1], south),
            send(ipack.at[r], rside.at[r, 1], i_send.at[r, 2], i_recv.at[r, 2], west),
            send(ipack.at[r], rside.at[r, 0], i_send.at[r, 3], i_recv.at[r, 3], east),
        ]
        for n, device in enumerate(corners):
            src = imsg.at[r, n // 2, pl.ds(32, 8)]
            copies.append(send(src, rcorner.at[r, 3 - n], i_send.at[r, 4 + n], i_recv.at[r, 4 + n], device))
        return copies

    imsg[...] = jnp.zeros_like(imsg)
    for t in range(TILES):
        cols = col_mu[pl.ds(SUB + t * SUB, SUB)] + col_mu[pl.ds(SUB - 1 + t * SUB, SUB)]
        cols = cols + roll(cols, 2, 1)
        acc = jnp.zeros((SUB, LANES), F32)
        below = None
        for k in range(NODES):
            layer = None
            if k < CELLS:
                start = SUB + k * ROWS + t * SUB
                up = mu[pl.ds(start - 1, SUB)]
                if t == 0:
                    up = jnp.where(sub8 == 0, row_mu[pl.ds(k, 1)], up)
                layer = mu[pl.ds(start, SUB)] + up
            total = layer if below is None else (below if layer is None else layer + below)
            below = layer
            left = jnp.where(lane8 == 0, roll(cols, -2 * k, 1), roll(total, 1, 1))
            diagonal = DIAGONAL * (total + left) + shift_term
            if k == 0:
                diagonal = diagonal + drag[pl.ds(t * SUB, SUB)]
            factor = relax_weight / diagonal
            rdiag[pl.ds(k * ROWS + t * SUB, SUB)] = factor
            for c in range(2):
                value = force[pl.ds((c * NODES + k) * ROWS + t * SUB, SUB)] * factor
                va[pl.ds((c * NODES + k) * VSPAN + t * SUB, SUB)] = value
                acc = jnp.where(pair8 == 32 * c + k, roll(value, 64 * c + 2 * k + 1, 1), acc)
        ipack[0, pl.ds(t * SUB, SUB)] = acc
    put_ice_edges(0, va)
    ice = send_ice(0)

    def take_ocean(r, copies):
        for copy in copies:
            copy.wait_recv()
        for n in range(3 * TILES):
            rows = pl.ds(n * SUB, SUB)
            from_e = roll(rpack[r, 1, rows], -1, 1)
            from_w = roll(rpack[r, 0, rows], 1, 1)
            merged[rows] = jnp.where(even, from_e, from_w)

    take_ocean(0, ocean)
    for t in range(TILES):
        rows = slice(t * SUB, (t + 1) * SUB)
        d, w = diffusion[rows], wet[rows]

        def around(mine, plane, n):
            whole = plane
            up = roll(mine, 1, 0)
            above = rrow[0, 0, pl.ds(2 * ZO + n, 1)] if t == 0 else whole[t * SUB - 1 : t * SUB]
            up = jnp.where(sub8 == 0, above, up)
            down = roll(mine, -1, 0)
            below = rrow[0, 1, pl.ds(2 * ZO + n, 1)] if t == TILES - 1 else whole[(t + 1) * SUB : (t + 1) * SUB + 1]
            down = jnp.where(sub8 == SUB - 1, below, down)
            edge = roll(merged[pl.ds(2 * ROWS + t * SUB, SUB)], 127 - 64 - 2 * n, 1)
            left = jnp.where(lane8 == 0, edge, roll(mine, 1, 1))
            right = jnp.where(lane8 == LANES - 1, edge, roll(mine, -1, 1))
            return up, down, left, right

        near_d = around(d, diffusion, 0)
        up_w, down_w, left_w, right_w = around(w, wet, 1)
        if t == 0:
            up_w = jnp.where(sub8 == 0, up_w * has_n, up_w)
        if t == TILES - 1:
            down_w = jnp.where(sub8 == SUB - 1, down_w * has_s, down_w)
        left_w = jnp.where(lane8 == 0, left_w * has_w, left_w)
        right_w = jnp.where(lane8 == LANES - 1, right_w * has_e, right_w)
        total = 2.0 * vert_mix * w
        for n, (near, near_w) in enumerate(zip(near_d, (up_w, down_w, left_w, right_w))):
            face = 0.5 * (d + near) * w * near_w
            coef[pl.ds((n + 1) * ROWS + t * SUB, SUB)] = face
            total = total + face
        coef[pl.ds(t * SUB, SUB)] = 1.0 - total
        coef[pl.ds(5 * ROWS + t * SUB, SUB)] = vert_mix * w

    def melt_of(temp_top, salt_top, t):
        freezing = freeze_slope * (salt_ref + salt_top) + freeze_base - freeze_depth * draft[pl.ds(t * SUB, SUB)]
        return heat_gamma * (temp_top - freezing) * (10.0 * coef[pl.ds(5 * ROWS + t * SUB, SUB)])

    def ocean_chunk(s, chunk, src, dst, top):
        for t in range(TILES):
            cs = [coef[pl.ds(n * ROWS + t * SUB, SUB)] for n in range(6)]
            first = []
            for field in range(2):
                base = FBASE + field * FSPAN + ROWS + chunk * (CHUNK * ROWS) + t * SUB
                if not isinstance(base, int):
                    base = pl.multiple_of(base, SUB)
                vec, lane = packed_place(field, chunk)
                packed = merged[pl.ds(pl.multiple_of(vec * ROWS + t * SUB, SUB), SUB)]
                packed = pltpu.roll(packed, lax.rem(LANES - lane, LANES), 1)
                acc = jnp.zeros((SUB, LANES), F32)
                prev = src[pl.ds(base - ROWS, SUB)]
                cur = src[pl.ds(base, SUB)]
                news = []
                for j in range(CHUNK):
                    row = base + j * ROWS
                    nxt = src[pl.ds(row + ROWS, SUB)]
                    up = src[pl.ds(row - 1, SUB)]
                    down = src[pl.ds(row + 1, SUB)]
                    level = field * ZO + chunk * CHUNK + j
                    if t == 0:
                        up = jnp.where(sub8 == 0, rrow[s, 0, pl.ds(level, 1)], up)
                    if t == TILES - 1:
                        down = jnp.where(sub8 == SUB - 1, rrow[s, 1, pl.ds(level, 1)], down)
                    edge = roll(packed, 127 - 2 * j, 1)
                    left = jnp.where(lane8 == 0, edge, roll(cur, 1, 1))
                    right = jnp.where(lane8 == LANES - 1, edge, roll(cur, -1, 1))
                    new = (
                        cs[0] * cur
                        + (cs[1] * up + cs[2] * down)
                        + (cs[3] * left + cs[4] * right)
                        + cs[5] * (prev + nxt)
                    )
                    news.append(new)
                    prev, cur = cur, nxt
                first.append(news)
            if top:
                temp_top, salt_top = first[0][0], first[1][0]
                rate = melt_of(temp_top, salt_top, t)
                first[0][0] = temp_top - heat_factor * rate
                first[1][0] = salt_top - salt_factor * rate * (salt_ref + salt_top) / salt_ref
            for field in range(2):
                acc = jnp.zeros((SUB, LANES), F32)
                for j in range(CHUNK):
                    new = first[field][j]
                    if s < STEPS - 1:
                        row = FBASE + field * FSPAN + ROWS + chunk * (CHUNK * ROWS) + t * SUB + j * ROWS
                        if not isinstance(row, int):
                            row = pl.multiple_of(row, SUB)
                        dst[pl.ds(row, SUB)] = new
                        acc = jnp.where(pair8 == j, roll(new, 2 * j + 1, 1), acc)
                    else:
                        row = chunk * (CHUNK * ROWS) + j * ROWS + t * SUB
                        if not isinstance(row, int):
                            row = pl.multiple_of(row, SUB)
                        dst[field][pl.ds(row, SUB)] = new
                if s < STEPS - 1:
                    put_pack(s + 1, field, chunk, t, acc)
        if s < STEPS - 1:
            for field in range(2):
                put_rows(s + 1, dst, field, chunk)

    def ocean_rest(s, src, dst):
        def body(chunk, carry):
            ocean_chunk(s, chunk, src, dst, False)
            return carry

        lax.fori_loop(1, ZO // CHUNK, body, 0)

    def ice_sweep(r, copies, src, dst):
        last = r == SWEEPS - 1
        for copy in copies:
            copy.wait_recv()
        for c in range(2):
            for k in range(NODES):
                src[pl.ds((c * NODES + k) * VSPAN + ROWS, 1)] = rmsg[r, 1, pl.ds(c * 16 + k, 1)] * has_s
        for t in range(TILES):
            rows = pl.ds(t * SUB, SUB)
            edge_e[rows] = rside[r, 1, rows] * has_e
            col_lo[pl.ds(SUB + t * SUB, SUB)] = rside[r, 0, rows] * has_w
            col_hi[pl.ds(SUB + t * SUB, SUB)] = roll(ipack[r, rows], -1, 1)
        edge_e[pl.ds(ROWS, 1)] = rcorner[r, 3, pl.ds(0, 1)] * (has_e * has_s)
        col_lo[pl.ds(SUB - 1, 1)] = rcorner[r, 0, pl.ds(0, 1)] * (has_w * has_n)
        col_lo[pl.ds(SUB + ROWS, 1)] = rcorner[r, 2, pl.ds(0, 1)] * (has_w * has_s)
        col_hi[pl.ds(SUB - 1, 1)] = roll(rmsg[r, 0, pl.ds(32, 1)] * has_n, -1, 1)
        col_hi[pl.ds(SUB + ROWS, 1)] = roll(rmsg[r, 1, pl.ds(32, 1)] * has_s, -1, 1)
        for t in range(TILES + 1):
            start = SUB - 1 + t * SUB
            if t == TILES:
                start = ROWS
            lo0, lo1 = col_lo[pl.ds(start, SUB)], col_lo[pl.ds(start + 1, SUB)]
            hi0, hi1 = col_hi[pl.ds(start, SUB)], col_hi[pl.ds(start + 1, SUB)]
            planes = []
            for c in range(2):
                parts = [roll(value, 64 * c, 1) for value in (lo0, hi0, lo1, hi1)]
                low = plane_sums(*parts)
                planes += [low, {key: roll(value, -2, 1) for key, value in low.items()}]
            fu, fv = element_forces(*planes, col_mu[pl.ds(start, SUB)])
            for c, f in enumerate((fu, fv)):
                low, high = lower_part(f), upper_part(f)
                node = {key: low[key] + roll(high[key], 2, 1) for key in low}
                col_q[2 * c, pl.ds(start - SUB + 1, SUB)] = node["ss"] + node["sd"]
                col_q[2 * c + 1, pl.ds(start - SUB + 1, SUB)] = node["ds"] + node["dd"]
        lane16, sub16 = iota((16, LANES), 1), iota((16, LANES), 0)

        def upright(row, offset):
            chosen = jnp.where(lane16 == 2 * sub16 + offset, row, 0.0)
            return jnp.sum(chosen, axis=1, keepdims=True)

        planes = []
        for c in range(2):
            lo = rmsg[r, 0, pl.ds(c * 16, 16)]
            hi = imsg[r, 0, pl.ds(c * 16, 16)]
            lo_end = upright(rcorner[r, 1, pl.ds(0, 1)] * (has_e * has_n), 64 * c + 1)
            hi_end = upright(edge_e[pl.ds(0, 1)], 64 * c + 1)
            lo_right = jnp.where(lane16 == LANES - 1, lo_end, roll(lo, -1, 1))
            hi_right = jnp.where(lane16 == LANES - 1, hi_end, roll(hi, -1, 1))
            low = plane_sums(lo, lo_right, hi, hi_right)
            planes += [low, {key: roll(value, -1, 0) for key, value in low.items()}]
        fu, fv = element_forces(*planes, row_mu[...])
        for c, f in enumerate((fu, fv)):
            low, high = lower_part(f), upper_part(f)
            node = {key: low[key] + roll(high[key], 1, 0) for key in low}
            ends = []
            for n, x in enumerate("sd"):
                behind = upright(col_q[2 * c + n, pl.ds(0, 1)], 0)
                shifted = roll(node[x + "s"] + node[x + "d"], 1, 1)
                ends.append(node[x + "s"] - node[x + "d"] + jnp.where(lane16 == 0, behind, shifted))
            row_q[pl.ds(c * 16, 16)] = ends[0] + ends[1]
        pass_down = [[None] * NODES, [None] * NODES]
        for t in range(TILES):
            here, next_row = edge_e[pl.ds(t * SUB, SUB)], edge_e[pl.ds(t * SUB + 1, SUB)]
            strips = [[col_q[2 * c + n, pl.ds(1 + t * SUB, SUB)] for n in range(2)] for c in range(2)]
            acc = jnp.zeros((SUB, LANES), F32)
            below, carried = None, None
            for k in range(NODES + 1):
                planes = None
                if k < NODES:
                    planes = []
                    for c in range(2):
                        start = (c * NODES + k) * VSPAN + t * SUB
                        lo, hi = src[pl.ds(start, SUB)], src[pl.ds(start + 1, SUB)]
                        shift = 127 - (64 * c + 2 * k + 1)
                        lo_right = jnp.where(lane8 == LANES - 1, roll(here, shift, 1), roll(lo, -1, 1))
                        hi_right = jnp.where(lane8 == LANES - 1, roll(next_row, shift, 1), roll(hi, -1, 1))
                        planes.append(plane_sums(lo, lo_right, hi, hi_right))
                if k >= 1:
                    level = k - 1
                    nodes, ups = [None, None], [None, None]
                    if level < CELLS:
                        weight = mu[pl.ds(SUB + level * ROWS + t * SUB, SUB)]
                        forces = element_forces(below[0], planes[0], below[1], planes[1], weight)
                        for c in range(2):
                            nodes[c], ups[c] = lower_part(forces[c]), upper_part(forces[c])
                            if carried is not None:
                                nodes[c] = {key: nodes[c][key] + carried[c][key] for key in nodes[c]}
                    else:
                        nodes = carried
                    carried = ups
                    factor = rdiag[pl.ds(level * ROWS + t * SUB, SUB)]
                    for c in range(2):
                        node = nodes[c]
                        shift = -(2 * level)
                        sides = []
                        for n, x in enumerate("sd"):
                            before = jnp.where(
                                lane8 == 0,
                                roll(strips[c][n], shift, 1),
                                roll(node[x + "s"] + node[x + "d"], 1, 1),
                            )
                            sides.append(node[x + "s"] - node[x + "d"] + before)
                        down = roll(sides[0] + sides[1], 1, 0)
                        over = row_q[pl.ds(c * 16 + level, 1)] if t == 0 else pass_down[c][level]
                        pass_down[c][level] = down[0:1]
                        applied = sides[0] - sides[1] + jnp.where(sub8 == 0, over, down)
                        value = src[pl.ds((c * NODES + level) * VSPAN + t * SUB, SUB)]
                        extra = shift_term
                        if level == 0:
                            extra = shift_term + drag[pl.ds(t * SUB, SUB)]
                        applied = applied + extra * value
                        row = (c * NODES + level) * ROWS + t * SUB
                        value = value + (force[pl.ds(row, SUB)] - applied) * factor
                        if last:
                            dst[pl.ds(row, SUB)] = value
                        else:
                            dst[pl.ds((c * NODES + level) * VSPAN + t * SUB, SUB)] = value
                            place = 64 * c + 2 * level + 1
                            acc = jnp.where(pair8 == 32 * c + level, roll(value, place, 1), acc)
                below = planes
            if not last:
                ipack[r + 1, pl.ds(t * SUB, SUB)] = acc
        if last:
            return None
        put_ice_edges(r + 1, dst)
        return send_ice(r + 1)

    coupling = scatter_second(0, coupling)
    ocean_rest(0, fa, fb)
    for copy in coupling:
        copy.wait_recv()
    draft[...] = pick(by_device(from_col), got[0])
    ocean_chunk(0, 0, fa, fb, True)
    guard(fb)
    ocean = send_ocean(1)
    ice = ice_sweep(0, ice, va, vb)

    take_ocean(1, ocean)
    ocean_chunk(1, 0, fb, fa, True)
    ocean_rest(1, fb, fa)
    guard(fa)
    ocean = send_ocean(2)
    ice = ice_sweep(1, ice, vb, va)

    take_ocean(2, ocean)
    ocean_chunk(2, 0, fa, fb, True)
    ocean_rest(2, fa, fb)
    guard(fb)
    ocean = send_ocean(3)
    take_ocean(3, ocean)
    ocean_chunk(3, 0, fb, (temp_out, salt_out), True)
    for t in range(TILES):
        rows = pl.ds(t * SUB, SUB)
        pad_in[rows] = melt_of(temp_out[rows], salt_out[rows], t)
    tbl[1] = pick(by_slot(from_row), pad_in[...])
    coupling = scatter_first(1)
    ice_sweep(2, ice, va, vel_out)
    coupling = scatter_second(1, coupling)
    ocean_rest(3, fb, (temp_out, salt_out))
    for copy in coupling:
        copy.wait_recv()
    melt = pick(by_device(to_col), got[1])
    thick_out[...] = thick[...] - melt_factor * melt * wet_ice
    for copy in sends:
        copy.wait_send()


def per_device(
    ice_force, ice_visc, ice_drag, ice_mask, ice_thick, ice_target,
    ocean_temp, ocean_salt, ocean_diff, ocean_mask, ocean_source,
):
    def flat(array):
        return array.reshape(-1, LANES)

    vmem = pl.BlockSpec(memory_space=pltpu.VMEM)
    smem = pl.BlockSpec(memory_space=pltpu.SMEM)
    hbm = pl.BlockSpec(memory_space=pl.ANY)
    dma = pltpu.SemaphoreType.DMA

    def buf(*shape):
        return pltpu.VMEM((*shape, LANES), F32)

    nx, ny = lax.axis_size("gx"), lax.axis_size("gy")
    scratch = [
        buf(FROWS), buf(FROWS), buf(6 * ROWS), buf(STEPS, 3 * ROWS), buf(STEPS, 2, 2 * ZO + SUB),
        buf(STEPS, 2, 3 * ROWS), buf(STEPS, 2, 2 * ZO + SUB), buf(3 * ROWS),
        buf(VROWS), buf(VROWS), buf(2 * SUB + CELLS * ROWS), buf(NODES * ROWS),
        buf(SWEEPS, ROWS), buf(SWEEPS, 2, 40), buf(SWEEPS, 2, ROWS), buf(SWEEPS, 2, 40), buf(SWEEPS, 4, SUB),
        buf(ROWS + SUB), buf(ROWS + 2 * SUB), buf(ROWS + 2 * SUB), buf(ROWS + 2 * SUB),
        buf(4, ROWS + SUB), buf(32), buf(16),
        buf(ROWS), buf(24), buf(ROWS), buf(24), buf(SUB),
        buf(LANES), buf(ROWS), buf(2, LANES), buf(2, LANES), buf(2, LANES), buf(2, LANES),
        dma((2,)), dma((STEPS, 4)), dma((STEPS, 4)), dma((SWEEPS, 8)), dma((SWEEPS, 8)),
        dma((3,)), dma((3,)), dma((2, ny)), dma((2, ny)), dma((2, nx)), dma((2, nx)),
    ]
    velocity, thickness, temp, salt = pl.pallas_call(
        kernel,
        out_shape=[
            jax.ShapeDtypeStruct((2 * NODES * ROWS, LANES), F32),
            jax.ShapeDtypeStruct((ROWS, LANES), F32),
            jax.ShapeDtypeStruct((ZO * ROWS, LANES), F32),
            jax.ShapeDtypeStruct((ZO * ROWS, LANES), F32),
        ],
        in_specs=[vmem, vmem, vmem, vmem, vmem, smem, hbm, hbm, vmem, vmem, smem],
        out_specs=[vmem] * 4,
        scratch_shapes=scratch,
        compiler_params=pltpu.CompilerParams(
            collective_id=0, has_side_effects=True, vmem_limit_bytes=40 * 1024 * 1024
        ),
    )(
        flat(ice_force), flat(ice_visc), ice_drag, ice_mask, ice_thick, ice_target,
        flat(ocean_temp), flat(ocean_salt), ocean_diff, ocean_mask, ocean_source,
    )
    return (
        velocity.reshape(ice_force.shape),
        thickness,
        temp.reshape(ocean_temp.shape),
        salt.reshape(ocean_salt.shape),
    )


def solution(mesh):
    in_specs = (
        P(None, None, "gx", "gy"),
        P(None, "gx", "gy"),
        P("gx", "gy"),
        P("gx", "gy"),
        P("gx", "gy"),
        P(("gx", "gy")),
        P(None, "gx", "gy"),
        P(None, "gx", "gy"),
        P("gx", "gy"),
        P("gx", "gy"),
        P(("gx", "gy")),
    )
    out_specs = (P(None, None, "gx", "gy"), P("gx", "gy"), P(None, "gx", "gy"), P(None, "gx", "gy"))
    return jax.shard_map(per_device, mesh=mesh, in_specs=in_specs, out_specs=out_specs, check_vma=False)
```

```python
import jax
import jax.numpy as jnp
from jax import lax
from jax.experimental import pallas as pl
from jax.experimental.pallas import tpu as pltpu
from jax.sharding import PartitionSpec as P

MESH = pl.DeviceIdType.MESH
F32 = jnp.float32

LANES = 128
SUB = 8
ROWS = 32
TILES = ROWS // SUB
ZO = 80
NODES = 11
CELLS = 10
STEPS = 4
SWEEPS = 3
CHUNK = 8
FBASE = 8
FSPAN = (ZO + 2) * ROWS
FROWS = 2 * FBASE + 2 * FSPAN
VSPAN = 40
VROWS = (NODES + 16) * VSPAN

relax_weight = 0.6
shift_term = 0.2
vert_mix = 0.1
heat_gamma = 0.5
heat_factor = 0.05
salt_factor = 0.05
salt_ref = 34.5
freeze_slope = -0.0573
freeze_base = 0.0832
freeze_depth = 0.761
melt_factor = 0.2
draft_ratio = 0.89

MASS = {"s": 1.0 / 4.0, "d": 1.0 / 12.0}


def same_weight(z, x, y, along):
    wx, wy = (4.0, 1.0) if along == 0 else (1.0, 4.0)
    total = 0.0
    if x == "d":
        total += wx * MASS[y] * MASS[z]
    if y == "d":
        total += wy * MASS[x] * MASS[z]
    if z == "d":
        total += MASS[x] * MASS[y]
    return total


DIAGONAL = 2.0 / 3.0


def iota(shape, axis):
    return lax.broadcasted_iota(jnp.int32, shape, axis)


def roll(value, shift, axis):
    size = value.shape[axis]
    if isinstance(shift, int):
        shift = shift % size
        if shift == 0:
            return value
    return pltpu.roll(value, shift, axis)


def plane_sums(lo, lo_right, hi, hi_right):
    ls, ld = lo + lo_right, lo_right - lo
    hs, hd = hi + hi_right, hi_right - hi
    return {"ss": ls + hs, "sd": ld + hd, "ds": hs - ls, "dd": hd - ld}


def element_forces(u_low, u_high, v_low, v_high, mu):
    u, v = {}, {}
    for xy in ("ss", "sd", "ds", "dd"):
        if xy != "ss":
            u["s" + xy] = u_low[xy] + u_high[xy]
            v["s" + xy] = v_low[xy] + v_high[xy]
        u["d" + xy] = u_high[xy] - u_low[xy]
        v["d" + xy] = v_high[xy] - v_low[xy]
    scaled = {}

    def times_mu(factor):
        if factor not in scaled:
            scaled[factor] = mu * factor
        return scaled[factor]

    fu, fv = {}, {}
    for key in u:
        z, xy = key[0], key[1:]
        for along, mine, other, out in ((0, u, v, fu), (1, v, u, fv)):
            own = same_weight(z, xy[0], xy[1], along)
            if xy in ("ds", "sd"):
                first = xy == "ds"
                double = first if along == 0 else not first
                cross = MASS[z] * (2.0 if double else 1.0) / 4.0
                swapped = z + ("sd" if first else "ds")
                out[key] = times_mu(own) * (mine[key] + (cross / own) * other[swapped])
            else:
                out[key] = times_mu(own) * mine[key]
    return fu, fv


def lower_part(f):
    out = {xy: f["s" + xy] - f["d" + xy] for xy in ("sd", "ds", "dd")}
    out["ss"] = -f["dss"]
    return out


def upper_part(f):
    out = {xy: f["s" + xy] + f["d" + xy] for xy in ("sd", "ds", "dd")}
    out["ss"] = f["dss"]
    return out


def packed_place(field, chunk):
    return field + (chunk // 8) * (2 - field), (chunk % 8) * 16 + (chunk // 8) * (32 * field)


def kernel(
    force_in, visc_in, drag_in, imask_in, thick_in, target_in, temp_in, salt_in, diff_in, omask_in, source_in,
    vel_out, thick_out, temp_out, salt_out,
    force, visc, drag, imask, thick, target, diff, omask, source,
    fa, fb, coef, opack, orow, rpack, rrow, merged,
    va, vb, mu, rdiag, ipack, imsg, rside, rmsg, rcorner,
    vright, low_y, high_y, shifts, sides,
    edge_e, col_lo, col_hi, col_mu, col_q, row_q, row_mu,
    wpack, wmsg, rwpack, rwmsg, rwcorner,
    pad_in, draft, tbl, mid, fwd, got,
    in_sem, o_send, o_recv, i_send, i_recv, w_send, w_recv, a_send, a_recv, b_send, b_recv,
):
    gx, gy = lax.axis_index("gx"), lax.axis_index("gy")
    nx, ny = lax.axis_size("gx"), lax.axis_size("gy")

    def at(dx, dy):
        return (lax.rem(gx + (dx + nx), nx), lax.rem(gy + (dy + ny), ny))

    north, south, west, east = at(-1, 0), at(1, 0), at(0, -1), at(0, 1)
    corners = (at(-1, -1), at(-1, 1), at(1, -1), at(1, 1))

    lane8 = iota((SUB, LANES), 1)
    sub8 = iota((SUB, LANES), 0)
    pair8 = lane8 // 2

    pairs = [(visc_in, visc), (imask_in, imask), (thick_in, thick), (target_in, target), (source_in, source)]
    for field, ref in ((0, temp_in), (1, salt_in)):
        start = FBASE + field * FSPAN + ROWS
        pairs.append((ref, fa.at[pl.ds(start, ZO * ROWS)]))
    pairs += [(diff_in, diff), (omask_in, omask), (drag_in, drag), (force_in, force)]
    loads = [pltpu.make_async_copy(src, dst, in_sem.at[n]) for n, (src, dst) in enumerate(pairs)]
    for copy in loads:
        copy.start()
    barrier = pltpu.get_barrier_semaphore()
    peers = [north, south, *corners]
    peers += [at(0, q) for q in range(1, ny)] + [at(p, 0) for p in range(2, nx - 1)]
    for peer in peers:
        pl.semaphore_signal(barrier, inc=1, device_id=peer, device_id_type=MESH)

    has_n = (gx > 0).astype(F32)
    has_s = (gx < nx - 1).astype(F32)
    has_w = (gy > 0).astype(F32)
    has_e = (gy < ny - 1).astype(F32)

    sends = []

    def send(src, dst, ssem, rsem, device):
        copy = pltpu.make_async_remote_copy(
            src_ref=src, dst_ref=dst, send_sem=ssem, recv_sem=rsem, device_id=device, device_id_type=MESH
        )
        copy.start()
        sends.append(copy)
        return copy

    wmsg[...] = jnp.zeros_like(wmsg)
    va[...] = jnp.zeros_like(va)
    vb[...] = jnp.zeros_like(vb)
    edge_e[...] = jnp.zeros_like(edge_e)
    col_lo[...] = jnp.zeros_like(col_lo)
    col_hi[...] = jnp.zeros_like(col_hi)
    col_mu[...] = jnp.zeros_like(col_mu)
    imsg[...] = jnp.zeros_like(imsg)
    pad_in[...] = jnp.zeros_like(pad_in)
    opack[...] = jnp.zeros_like(opack)
    orow[...] = jnp.zeros_like(orow)
    row_no, col_no = iota((2 * LANES, 2 * LANES), 0) % LANES, iota((2 * LANES, 2 * LANES), 1)
    before = (row_no == col_no - 1) & (col_no < LANES)
    after = (row_no == col_no + 1 - LANES) & (col_no >= LANES)
    shifts[...] = (before | after).astype(F32).astype(jnp.bfloat16)
    for copy in loads[:5]:
        copy.wait()
    wet_ice = imask[...].astype(F32)
    for t in range(TILES):
        acc = jnp.zeros((SUB, LANES), F32)
        wet_t = wet_ice[t * SUB : (t + 1) * SUB]
        for k in range(CELLS):
            rows = pl.ds(k * ROWS + t * SUB, SUB)
            weight = visc[rows] * wet_t
            mu[pl.ds(SUB + k * ROWS + t * SUB, SUB)] = weight
            acc = jnp.where(pair8 == k, roll(weight, 2 * k + 1, 1), acc)
        wpack[pl.ds(t * SUB, SUB)] = acc
    wmsg[pl.ds(0, 8)] = mu[pl.ds(SUB + ROWS - 1, 8, stride=ROWS)]
    wmsg[pl.ds(8, 2)] = mu[pl.ds(SUB + 8 * ROWS + ROWS - 1, 2, stride=ROWS)]
    wmsg[pl.ds(16, 1)] = wpack[pl.ds(ROWS - 1, 1)]

    lane1 = iota((SUB, LANES), 1)
    to_row = jnp.full((SUB, LANES), -1, jnp.int32)
    from_row = jnp.full((SUB, LANES), -1, jnp.int32)
    to_col = [jnp.full((SUB, LANES), -1, jnp.int32) for _ in range(TILES)]
    from_col = [jnp.full((SUB, LANES), -1, jnp.int32) for _ in range(TILES)]
    for i in range(ROWS):
        to_row = jnp.where(lane1 == i, target[i], to_row)
        from_row = jnp.where(lane1 == i, source[i], from_row)
        to_col[i // SUB] = jnp.where(sub8 == i % SUB, target[i], to_col[i // SUB])
        from_col[i // SUB] = jnp.where(sub8 == i % SUB, source[i], from_col[i // SUB])

    def slot_of(ids):
        device = ids >> 5
        return jnp.where(ids >= 0, (device & (ny - 1)) * nx + (device >> 4), -1)

    def by_slot(row):
        slots = slot_of(row)
        return jnp.concatenate(
            [(sub8 + n * SUB == slots).astype(F32) for n in range(LANES // SUB)], axis=0
        )

    def by_device(cols):
        return jnp.concatenate(
            [((lane8 == (ids >> 5)) & (ids >= 0)).astype(F32) for ids in cols], axis=0
        )

    def pick(one_hot, values):
        return jnp.dot(one_hot, values, precision=lax.Precision.HIGHEST, preferred_element_type=F32)

    pad_in[pl.ds(0, ROWS)] = draft_ratio * thick[...]
    tbl[0] = pick(by_slot(to_row), pad_in[...])

    for copy in loads[5:]:
        copy.wait()

    def guard(ref):
        for field in range(2):
            base = FBASE + field * FSPAN
            ref[pl.ds(base, ROWS)] = ref[pl.ds(base + ROWS, ROWS)]
            ref[pl.ds(base + (ZO + 1) * ROWS, ROWS)] = ref[pl.ds(base + ZO * ROWS, ROWS)]

    def put_pack(r, field, chunk, t, acc):
        vec, lane = packed_place(field, chunk)
        rows = pl.ds(pl.multiple_of(vec * ROWS + t * SUB, SUB), SUB)
        shifted = pltpu.roll(acc, lane, 1)
        mine = (lane8 >= lane) & (lane8 < lane + 16)
        opack[r, rows] = jnp.where(mine, shifted, opack[r, rows])

    def put_rows(r, ref, field, chunk):
        base = FBASE + field * FSPAN + ROWS + chunk * (CHUNK * ROWS)
        rows = pl.ds(pl.multiple_of(field * ZO + chunk * CHUNK, SUB), SUB)
        orow[r, 0, rows] = ref[pl.ds(base, SUB, stride=ROWS)]
        orow[r, 1, rows] = ref[pl.ds(base + ROWS - 1, SUB, stride=ROWS)]

    def first_edges(chunk, carry):
        for field in range(2):
            base = FBASE + field * FSPAN + ROWS + chunk * (CHUNK * ROWS)
            for t in range(TILES):
                acc = jnp.zeros((SUB, LANES), F32)
                for j in range(CHUNK):
                    value = fa[pl.ds(pl.multiple_of(base + j * ROWS + t * SUB, SUB), SUB)]
                    acc = jnp.where(pair8 == j, roll(value, 2 * j + 1, 1), acc)
                put_pack(0, field, chunk, t, acc)
            put_rows(0, fa, field, chunk)
        return carry

    lax.fori_loop(0, ZO // CHUNK, first_edges, 0)
    guard(fa)
    wet = omask[...].astype(F32)
    diffusion = diff[...]
    orow[0, 0, pl.ds(2 * ZO, 1)] = diffusion[0:1]
    orow[0, 0, pl.ds(2 * ZO + 1, 1)] = wet[0:1]
    orow[0, 1, pl.ds(2 * ZO, 1)] = diffusion[ROWS - 1 :]
    orow[0, 1, pl.ds(2 * ZO + 1, 1)] = wet[ROWS - 1 :]
    for t in range(TILES):
        rows = pl.ds(2 * ROWS + t * SUB, SUB)
        acc = opack[0, rows]
        acc = jnp.where(pair8 == 32, roll(diffusion[t * SUB : (t + 1) * SUB], 65, 1), acc)
        acc = jnp.where(pair8 == 33, roll(wet[t * SUB : (t + 1) * SUB], 67, 1), acc)
        opack[0, rows] = acc

    pl.semaphore_wait(barrier, len(peers))

    def send_ocean(r):
        return [
            send(orow.at[r, 0], rrow.at[r, 1], o_send.at[r, 0], o_recv.at[r, 0], north),
            send(orow.at[r, 1], rrow.at[r, 0], o_send.at[r, 1], o_recv.at[r, 1], south),
            send(opack.at[r], rpack.at[r, 1], o_send.at[r, 2], o_recv.at[r, 2], west),
            send(opack.at[r], rpack.at[r, 0], o_send.at[r, 3], o_recv.at[r, 3], east),
        ]

    def scatter_first(n):
        copies = []
        for q in range(1, ny):
            peer = at(0, q)
            copies.append(
                send(
                    tbl.at[n, pl.ds(pl.multiple_of(peer[1] * nx, nx), nx)],
                    mid.at[n, pl.ds(pl.multiple_of(gy * nx, nx), nx)],
                    a_send.at[n, q], a_recv.at[n, q], peer,
                )
            )
        own = pl.ds(pl.multiple_of(gy * nx, nx), nx)
        mid[n, own] = tbl[n, own]
        return copies

    def scatter_second(n, copies):
        for copy in copies:
            copy.wait_recv()
        for p in range(nx):
            fwd[n, pl.ds(p * ny, ny)] = mid[n, pl.ds(p, ny, stride=nx)]
        copies = []
        for p in range(1, nx):
            peer = at(p, 0)
            copies.append(
                send(
                    fwd.at[n, pl.ds(pl.multiple_of(peer[0] * ny, ny), ny)],
                    got.at[n, pl.ds(pl.multiple_of(gx * ny, ny), ny)],
                    b_send.at[n, p], b_recv.at[n, p], peer,
                )
            )
        own = pl.ds(pl.multiple_of(gx * ny, ny), ny)
        got[n, own] = fwd[n, own]
        return copies

    weights = [
        send(wmsg, rwmsg, w_send.at[0], w_recv.at[0], south),
        send(wpack, rwpack, w_send.at[1], w_recv.at[1], east),
        send(wmsg.at[pl.ds(16, 8)], rwcorner, w_send.at[2], w_recv.at[2], corners[3]),
    ]
    ocean = send_ocean(0)
    coupling = scatter_first(0)

    for copy in weights:
        copy.wait_recv()
    row_mu[...] = rwmsg[pl.ds(0, 16)] * has_n
    even = (lane8 & 1) == 0
    for t in range(TILES):
        col_mu[pl.ds(SUB + t * SUB, SUB)] = jnp.where(even, rwpack[pl.ds(t * SUB, SUB)] * has_w, 0.0)
    even1 = (iota((1, LANES), 1) & 1) == 0
    col_mu[pl.ds(SUB - 1, 1)] = jnp.where(even1, rwcorner[pl.ds(0, 1)] * (has_w * has_n), 0.0)

    def put_ice_edges(r, ref):
        for c in range(2):
            for edge in range(2):
                start = c * NODES * VSPAN + edge * (ROWS - 1)
                imsg[r, edge, pl.ds(c * 16, 16)] = ref[pl.ds(start, 16, stride=VSPAN)]
        imsg[r, 0, pl.ds(32, 1)] = ipack[r, pl.ds(0, 1)]
        imsg[r, 1, pl.ds(32, 1)] = ipack[r, pl.ds(ROWS - 1, 1)]

    def send_ice(r):
        copies = [
            send(imsg.at[r, 0], rmsg.at[r, 1], i_send.at[r, 0], i_recv.at[r, 0], north),
            send(imsg.at[r, 1], rmsg.at[r, 0], i_send.at[r, 1], i_recv.at[r, 1], south),
            send(ipack.at[r], rside.at[r, 1], i_send.at[r, 2], i_recv.at[r, 2], west),
            send(ipack.at[r], rside.at[r, 0], i_send.at[r, 3], i_recv.at[r, 3], east),
        ]
        for n, device in enumerate(corners):
            src = imsg.at[r, n // 2, pl.ds(32, 8)]
            copies.append(send(src, rcorner.at[r, 3 - n], i_send.at[r, 4 + n], i_recv.at[r, 4 + n], device))
        return copies

    for t in range(TILES):
        cols = col_mu[pl.ds(SUB + t * SUB, SUB)] + col_mu[pl.ds(SUB - 1 + t * SUB, SUB)]
        cols = cols + roll(cols, 2, 1)
        acc = jnp.zeros((SUB, LANES), F32)
        below = None
        for k in range(NODES):
            layer = None
            if k < CELLS:
                start = SUB + k * ROWS + t * SUB
                up = mu[pl.ds(start - 1, SUB)]
                if t == 0:
                    up = jnp.where(sub8 == 0, row_mu[pl.ds(k, 1)], up)
                layer = mu[pl.ds(start, SUB)] + up
            total = layer if below is None else (below if layer is None else layer + below)
            below = layer
            left = jnp.where(lane8 == 0, roll(cols, -2 * k, 1), roll(total, 1, 1))
            diagonal = DIAGONAL * (total + left) + shift_term
            if k == 0:
                diagonal = diagonal + drag[pl.ds(t * SUB, SUB)]
            factor = relax_weight / diagonal
            rdiag[pl.ds(k * ROWS + t * SUB, SUB)] = factor
            for c in range(2):
                value = force[pl.ds((c * NODES + k) * ROWS + t * SUB, SUB)] * factor
                va[pl.ds((c * NODES + k) * VSPAN + t * SUB, SUB)] = value
                acc = jnp.where(pair8 == 32 * c + k, roll(value, 64 * c + 2 * k + 1, 1), acc)
        ipack[0, pl.ds(t * SUB, SUB)] = acc
    put_ice_edges(0, va)
    ice = send_ice(0)

    def take_ocean(r, copies):
        for copy in copies:
            copy.wait_recv()
        for n in range(3 * TILES):
            rows = pl.ds(n * SUB, SUB)
            from_e = roll(rpack[r, 1, rows], -1, 1)
            from_w = roll(rpack[r, 0, rows], 1, 1)
            merged[rows] = jnp.where(even, from_e, from_w)

    take_ocean(0, ocean)
    for t in range(TILES):
        rows = slice(t * SUB, (t + 1) * SUB)
        d, w = diffusion[rows], wet[rows]

        def around(mine, plane, n):
            whole = plane
            up = roll(mine, 1, 0)
            above = rrow[0, 0, pl.ds(2 * ZO + n, 1)] if t == 0 else whole[t * SUB - 1 : t * SUB]
            up = jnp.where(sub8 == 0, above, up)
            down = roll(mine, -1, 0)
            below = rrow[0, 1, pl.ds(2 * ZO + n, 1)] if t == TILES - 1 else whole[(t + 1) * SUB : (t + 1) * SUB + 1]
            down = jnp.where(sub8 == SUB - 1, below, down)
            edge = roll(merged[pl.ds(2 * ROWS + t * SUB, SUB)], 127 - 64 - 2 * n, 1)
            left = jnp.where(lane8 == 0, edge, roll(mine, 1, 1))
            right = jnp.where(lane8 == LANES - 1, edge, roll(mine, -1, 1))
            return up, down, left, right

        near_d = around(d, diffusion, 0)
        up_w, down_w, left_w, right_w = around(w, wet, 1)
        if t == 0:
            up_w = jnp.where(sub8 == 0, up_w * has_n, up_w)
        if t == TILES - 1:
            down_w = jnp.where(sub8 == SUB - 1, down_w * has_s, down_w)
        left_w = jnp.where(lane8 == 0, left_w * has_w, left_w)
        right_w = jnp.where(lane8 == LANES - 1, right_w * has_e, right_w)
        total = 2.0 * vert_mix * w
        for n, (near, near_w) in enumerate(zip(near_d, (up_w, down_w, left_w, right_w))):
            face = 0.5 * (d + near) * w * near_w
            coef[pl.ds((n + 1) * ROWS + t * SUB, SUB)] = face
            total = total + face
        coef[pl.ds(t * SUB, SUB)] = 1.0 - total
        coef[pl.ds(5 * ROWS + t * SUB, SUB)] = vert_mix * w

    def melt_of(temp_top, salt_top, t):
        freezing = freeze_slope * (salt_ref + salt_top) + freeze_base - freeze_depth * draft[pl.ds(t * SUB, SUB)]
        return heat_gamma * (temp_top - freezing) * (10.0 * coef[pl.ds(5 * ROWS + t * SUB, SUB)])

    def ocean_chunk(s, chunk, src, dst, top):
        for field in range(2):
            base = FBASE + field * FSPAN + ROWS + chunk * (CHUNK * ROWS)
            if not isinstance(base, int):
                base = pl.multiple_of(base, SUB)
            values = src[pl.ds(base, CHUNK * ROWS)]
            high = values.astype(jnp.bfloat16)
            rest = (values - high.astype(F32)).astype(jnp.bfloat16)
            both = jnp.concatenate([high, rest], axis=1)
            sides[pl.ds(field * CHUNK * ROWS, CHUNK * ROWS)] = jnp.dot(
                both, shifts[...], preferred_element_type=F32
            )
        for t in range(TILES):
            cs = [coef[pl.ds(n * ROWS + t * SUB, SUB)] for n in range(6)]
            first = []
            for field in range(2):
                base = FBASE + field * FSPAN + ROWS + chunk * (CHUNK * ROWS) + t * SUB
                if not isinstance(base, int):
                    base = pl.multiple_of(base, SUB)
                vec, lane = packed_place(field, chunk)
                packed = merged[pl.ds(pl.multiple_of(vec * ROWS + t * SUB, SUB), SUB)]
                packed = pltpu.roll(packed, lax.rem(LANES - lane, LANES), 1)
                acc = jnp.zeros((SUB, LANES), F32)
                prev = src[pl.ds(base - ROWS, SUB)]
                cur = src[pl.ds(base, SUB)]
                news = []
                for j in range(CHUNK):
                    row = base + j * ROWS
                    nxt = src[pl.ds(row + ROWS, SUB)]
                    up = src[pl.ds(row - 1, SUB)]
                    down = src[pl.ds(row + 1, SUB)]
                    level = field * ZO + chunk * CHUNK + j
                    if t == 0:
                        up = jnp.where(sub8 == 0, rrow[s, 0, pl.ds(level, 1)], up)
                    if t == TILES - 1:
                        down = jnp.where(sub8 == SUB - 1, rrow[s, 1, pl.ds(level, 1)], down)
                    edge = roll(packed, 127 - 2 * j, 1)
                    beside = pl.ds(field * CHUNK * ROWS + j * ROWS + t * SUB, SUB)
                    left = jnp.where(lane8 == 0, edge, sides[beside, :LANES])
                    right = jnp.where(lane8 == LANES - 1, edge, sides[beside, LANES:])
                    new = (
                        cs[0] * cur
                        + (cs[1] * up + cs[2] * down)
                        + (cs[3] * left + cs[4] * right)
                        + cs[5] * (prev + nxt)
                    )
                    news.append(new)
                    prev, cur = cur, nxt
                first.append(news)
            if top:
                temp_top, salt_top = first[0][0], first[1][0]
                rate = melt_of(temp_top, salt_top, t)
                first[0][0] = temp_top - heat_factor * rate
                first[1][0] = salt_top - salt_factor * rate * (salt_ref + salt_top) / salt_ref
            for field in range(2):
                acc = jnp.zeros((SUB, LANES), F32)
                for j in range(CHUNK):
                    new = first[field][j]
                    if s < STEPS - 1:
                        row = FBASE + field * FSPAN + ROWS + chunk * (CHUNK * ROWS) + t * SUB + j * ROWS
                        if not isinstance(row, int):
                            row = pl.multiple_of(row, SUB)
                        dst[pl.ds(row, SUB)] = new
                        acc = jnp.where(pair8 == j, roll(new, 2 * j + 1, 1), acc)
                    else:
                        row = chunk * (CHUNK * ROWS) + j * ROWS + t * SUB
                        if not isinstance(row, int):
                            row = pl.multiple_of(row, SUB)
                        dst[field][pl.ds(row, SUB)] = new
                if s < STEPS - 1:
                    put_pack(s + 1, field, chunk, t, acc)
        if s < STEPS - 1:
            for field in range(2):
                put_rows(s + 1, dst, field, chunk)

    def ocean_rest(s, src, dst):
        def body(chunk, carry):
            ocean_chunk(s, chunk, src, dst, False)
            return carry

        lax.fori_loop(1, ZO // CHUNK, body, 0)

    def ice_sweep(r, copies, src, dst):
        last = r == SWEEPS - 1
        for copy in copies:
            copy.wait_recv()
        for c in range(2):
            for k in range(NODES):
                src[pl.ds((c * NODES + k) * VSPAN + ROWS, 1)] = rmsg[r, 1, pl.ds(c * 16 + k, 1)] * has_s
        for t in range(TILES):
            rows = pl.ds(t * SUB, SUB)
            edge_e[rows] = rside[r, 1, rows] * has_e
            col_lo[pl.ds(SUB + t * SUB, SUB)] = rside[r, 0, rows] * has_w
            col_hi[pl.ds(SUB + t * SUB, SUB)] = roll(ipack[r, rows], -1, 1)
        edge_e[pl.ds(ROWS, 1)] = rcorner[r, 3, pl.ds(0, 1)] * (has_e * has_s)
        col_lo[pl.ds(SUB - 1, 1)] = rcorner[r, 0, pl.ds(0, 1)] * (has_w * has_n)
        col_lo[pl.ds(SUB + ROWS, 1)] = rcorner[r, 2, pl.ds(0, 1)] * (has_w * has_s)
        col_hi[pl.ds(SUB - 1, 1)] = roll(rmsg[r, 0, pl.ds(32, 1)] * has_n, -1, 1)
        col_hi[pl.ds(SUB + ROWS, 1)] = roll(rmsg[r, 1, pl.ds(32, 1)] * has_s, -1, 1)
        for t in range(TILES + 1):
            start = SUB - 1 + t * SUB
            if t == TILES:
                start = ROWS
            lo0, lo1 = col_lo[pl.ds(start, SUB)], col_lo[pl.ds(start + 1, SUB)]
            hi0, hi1 = col_hi[pl.ds(start, SUB)], col_hi[pl.ds(start + 1, SUB)]
            planes = []
            for c in range(2):
                parts = [roll(value, 64 * c, 1) for value in (lo0, hi0, lo1, hi1)]
                low = plane_sums(*parts)
                planes += [low, {key: roll(value, -2, 1) for key, value in low.items()}]
            fu, fv = element_forces(*planes, col_mu[pl.ds(start, SUB)])
            for c, f in enumerate((fu, fv)):
                low, high = lower_part(f), upper_part(f)
                node = {key: low[key] + roll(high[key], 2, 1) for key in low}
                behind = {x: node[x + "s"] + node[x + "d"] for x in "sd"}
                col_q[2 * c, pl.ds(start - SUB + 1, SUB)] = behind["s"] - behind["d"]
                col_q[2 * c + 1, pl.ds(start - SUB + 1, SUB)] = behind["s"] + behind["d"]
        lane16, sub16 = iota((16, LANES), 1), iota((16, LANES), 0)

        def upright(row, offset):
            chosen = jnp.where(lane16 == 2 * sub16 + offset, row, 0.0)
            return jnp.sum(chosen, axis=1, keepdims=True)

        planes = []
        for c in range(2):
            lo = rmsg[r, 0, pl.ds(c * 16, 16)]
            hi = imsg[r, 0, pl.ds(c * 16, 16)]
            lo_end = upright(rcorner[r, 1, pl.ds(0, 1)] * (has_e * has_n), 64 * c + 1)
            hi_end = upright(edge_e[pl.ds(0, 1)], 64 * c + 1)
            lo_right = jnp.where(lane16 == LANES - 1, lo_end, roll(lo, -1, 1))
            hi_right = jnp.where(lane16 == LANES - 1, hi_end, roll(hi, -1, 1))
            low = plane_sums(lo, lo_right, hi, hi_right)
            planes += [low, {key: roll(value, -1, 0) for key, value in low.items()}]
        fu, fv = element_forces(*planes, row_mu[...])
        for c, f in enumerate((fu, fv)):
            low, high = lower_part(f), upper_part(f)
            node = {key: low[key] + roll(high[key], 1, 0) for key in low}
            for n, sign in enumerate((-1.0, 1.0)):
                parts = [node[x + "s"] + sign * node[x + "d"] for x in "sd"]
                row_q[pl.ds((2 * n + c) * 16, 16)] = parts[0] + parts[1]
        for c in range(2):
            for k in range(NODES):
                shift = 127 - (64 * c + 2 * k + 1)
                for t in range(TILES + 1):
                    rows = pl.ds((c * NODES + k) * VSPAN + t * SUB, SUB)
                    edge = roll(edge_e[pl.ds(t * SUB, SUB)], shift, 1)
                    vright[rows] = jnp.where(lane8 == LANES - 1, edge, roll(src[rows], -1, 1))
        pass_down = {}
        for t in range(TILES):
            below, carried = None, None
            for k in range(NODES + 1):
                planes = None
                if k < NODES:
                    planes = []
                    for c in range(2):
                        start = (c * NODES + k) * VSPAN + t * SUB
                        lo, hi = pl.ds(start, SUB), pl.ds(start + 1, SUB)
                        planes.append(plane_sums(src[lo], vright[lo], src[hi], vright[hi]))
                if k >= 1:
                    level = k - 1
                    nodes, ups = [None, None], [None, None]
                    if level < CELLS:
                        weight = mu[pl.ds(SUB + level * ROWS + t * SUB, SUB)]
                        forces = element_forces(below[0], planes[0], below[1], planes[1], weight)
                        for c in range(2):
                            nodes[c], ups[c] = lower_part(forces[c]), upper_part(forces[c])
                            if carried is not None:
                                nodes[c] = {key: nodes[c][key] + carried[c][key] for key in nodes[c]}
                    else:
                        nodes = carried
                    carried = ups
                    for c in range(2):
                        node = nodes[c]
                        row = pl.ds((c * NODES + level) * ROWS + t * SUB, SUB)
                        for n, (sign, place) in enumerate(((-1.0, low_y), (1.0, high_y))):
                            parts = [node[x + "s"] + sign * node[x + "d"] for x in "sd"]
                            down = roll(parts[0] + parts[1], 1, 0)
                            if t == 0:
                                over = row_q[pl.ds((2 * n + c) * 16 + level, 1)]
                            else:
                                over = pass_down[n, c, level]
                            pass_down[n, c, level] = down[0:1]
                            place[row] = parts[0] - parts[1] + jnp.where(sub8 == 0, over, down)
                below = planes
        for c in range(2):
            for t in range(TILES):
                strip = col_q[2 * c, pl.ds(1 + t * SUB, SUB)] + col_q[2 * c + 1, pl.ds(t * SUB, SUB)]
                for level in range(NODES):
                    at_row = (c * NODES + level) * ROWS + t * SUB
                    row = pl.ds(at_row, SUB)
                    before = jnp.where(lane8 == 0, roll(strip, -2 * level, 1), roll(high_y[row], 1, 1))
                    value = src[pl.ds((c * NODES + level) * VSPAN + t * SUB, SUB)]
                    extra = shift_term
                    if level == 0:
                        extra = shift_term + drag[pl.ds(t * SUB, SUB)]
                    applied = low_y[row] + before + extra * value
                    value = value + (force[row] - applied) * rdiag[pl.ds(level * ROWS + t * SUB, SUB)]
                    if last:
                        dst[row] = value
                    else:
                        dst[pl.ds((c * NODES + level) * VSPAN + t * SUB, SUB)] = value
        if last:
            return None
        for t in range(TILES):
            acc = jnp.zeros((SUB, LANES), F32)
            for c in range(2):
                for level in range(NODES):
                    value = dst[pl.ds((c * NODES + level) * VSPAN + t * SUB, SUB)]
                    acc = jnp.where(pair8 == 32 * c + level, roll(value, 64 * c + 2 * level + 1, 1), acc)
            ipack[r + 1, pl.ds(t * SUB, SUB)] = acc
        put_ice_edges(r + 1, dst)
        return send_ice(r + 1)

    coupling = scatter_second(0, coupling)
    ocean_rest(0, fa, fb)
    for copy in coupling:
        copy.wait_recv()
    draft[...] = pick(by_device(from_col), got[0])
    ocean_chunk(0, 0, fa, fb, True)
    guard(fb)
    ocean = send_ocean(1)
    ice = ice_sweep(0, ice, va, vb)

    take_ocean(1, ocean)
    ocean_chunk(1, 0, fb, fa, True)
    ocean_rest(1, fb, fa)
    guard(fa)
    ocean = send_ocean(2)
    ice = ice_sweep(1, ice, vb, va)

    take_ocean(2, ocean)
    ocean_chunk(2, 0, fa, fb, True)
    ocean_rest(2, fa, fb)
    guard(fb)
    ocean = send_ocean(3)
    take_ocean(3, ocean)
    ocean_chunk(3, 0, fb, (temp_out, salt_out), True)
    for t in range(TILES):
        rows = pl.ds(t * SUB, SUB)
        pad_in[rows] = melt_of(temp_out[rows], salt_out[rows], t)
    tbl[1] = pick(by_slot(from_row), pad_in[...])
    coupling = scatter_first(1)
    ice_sweep(2, ice, va, vel_out)
    coupling = scatter_second(1, coupling)
    ocean_rest(3, fb, (temp_out, salt_out))
    for copy in coupling:
        copy.wait_recv()
    melt = pick(by_device(to_col), got[1])
    thick_out[...] = thick[...] - melt_factor * melt * wet_ice
    for copy in sends:
        copy.wait_send()


def per_device(
    ice_force, ice_visc, ice_drag, ice_mask, ice_thick, ice_target,
    ocean_temp, ocean_salt, ocean_diff, ocean_mask, ocean_source,
):
    def flat(array):
        return pltpu.with_memory_space_constraint(array.reshape(-1, LANES), pltpu.HBM)

    def held(array):
        return pltpu.with_memory_space_constraint(array, pltpu.HBM)

    vmem = pl.BlockSpec(memory_space=pltpu.VMEM)
    hbm = pl.BlockSpec(memory_space=pltpu.HBM)
    dma = pltpu.SemaphoreType.DMA

    def buf(*shape):
        return pltpu.VMEM((*shape, LANES), F32)

    nx, ny = lax.axis_size("gx"), lax.axis_size("gy")
    whole = pltpu.VMEM((ROWS, LANES), jnp.int32)
    ids = pltpu.SMEM((ROWS,), jnp.int32)
    scratch = [
        buf(2 * NODES * ROWS), buf(CELLS * ROWS), buf(ROWS), whole, buf(ROWS), ids, buf(ROWS), whole, ids,
        buf(FROWS), buf(FROWS), buf(6 * ROWS), buf(STEPS, 3 * ROWS), buf(STEPS, 2, 2 * ZO + SUB),
        buf(STEPS, 2, 3 * ROWS), buf(STEPS, 2, 2 * ZO + SUB), buf(3 * ROWS),
        buf(VROWS), buf(VROWS), buf(2 * SUB + CELLS * ROWS), buf(NODES * ROWS),
        buf(SWEEPS, ROWS), buf(SWEEPS, 2, 40), buf(SWEEPS, 2, ROWS), buf(SWEEPS, 2, 40), buf(SWEEPS, 4, SUB),
        buf(VROWS), buf(2 * NODES * ROWS), buf(2 * NODES * ROWS),
        pltpu.VMEM((2 * LANES, 2 * LANES), jnp.bfloat16), pltpu.VMEM((2 * CHUNK * ROWS, 2 * LANES), F32),
        buf(ROWS + SUB), buf(ROWS + 2 * SUB), buf(ROWS + 2 * SUB), buf(ROWS + 2 * SUB),
        buf(4, ROWS + SUB), buf(64), buf(16),
        buf(ROWS), buf(24), buf(ROWS), buf(24), buf(SUB),
        buf(LANES), buf(ROWS), buf(2, LANES), buf(2, LANES), buf(2, LANES), buf(2, LANES),
        dma((11,)), dma((STEPS, 4)), dma((STEPS, 4)), dma((SWEEPS, 8)), dma((SWEEPS, 8)),
        dma((3,)), dma((3,)), dma((2, ny)), dma((2, ny)), dma((2, nx)), dma((2, nx)),
    ]
    velocity, thickness, temp, salt = pl.pallas_call(
        kernel,
        out_shape=[
            jax.ShapeDtypeStruct((2 * NODES * ROWS, LANES), F32),
            jax.ShapeDtypeStruct((ROWS, LANES), F32),
            jax.ShapeDtypeStruct((ZO * ROWS, LANES), F32),
            jax.ShapeDtypeStruct((ZO * ROWS, LANES), F32),
        ],
        in_specs=[hbm] * 11,
        out_specs=[vmem] * 4,
        scratch_shapes=scratch,
        compiler_params=pltpu.CompilerParams(
            collective_id=0, has_side_effects=True, vmem_limit_bytes=40 * 1024 * 1024
        ),
    )(
        flat(ice_force), flat(ice_visc), held(ice_drag), held(ice_mask), held(ice_thick), held(ice_target),
        flat(ocean_temp), flat(ocean_salt), held(ocean_diff), held(ocean_mask), held(ocean_source),
    )
    return (
        velocity.reshape(ice_force.shape),
        thickness,
        temp.reshape(ocean_temp.shape),
        salt.reshape(ocean_salt.shape),
    )


def solution(mesh):
    in_specs = (
        P(None, None, "gx", "gy"),
        P(None, "gx", "gy"),
        P("gx", "gy"),
        P("gx", "gy"),
        P("gx", "gy"),
        P(("gx", "gy")),
        P(None, "gx", "gy"),
        P(None, "gx", "gy"),
        P("gx", "gy"),
        P("gx", "gy"),
        P(("gx", "gy")),
    )
    out_specs = (P(None, None, "gx", "gy"), P("gx", "gy"), P(None, "gx", "gy"), P(None, "gx", "gy"))
    return jax.shard_map(per_device, mesh=mesh, in_specs=in_specs, out_specs=out_specs, check_vma=False)
```

```python
import jax
import jax.numpy as jnp
from jax import lax
from jax.experimental import pallas as pl
from jax.experimental.pallas import tpu as pltpu
from jax.sharding import PartitionSpec as P

MESH = pl.DeviceIdType.MESH
F32 = jnp.float32

LANES = 128
SUB = 8
ROWS = 32
TILES = ROWS // SUB
ZO = 80
NODES = 11
CELLS = 10
STEPS = 4
SWEEPS = 3
CHUNK = 8
FBASE = 8
FSPAN = (ZO + 2) * ROWS
FROWS = 2 * FBASE + 2 * FSPAN
VSPAN = 40
VROWS = (NODES + 16) * VSPAN

relax_weight = 0.6
shift_term = 0.2
vert_mix = 0.1
heat_gamma = 0.5
heat_factor = 0.05
salt_factor = 0.05
salt_ref = 34.5
freeze_slope = -0.0573
freeze_base = 0.0832
freeze_depth = 0.761
melt_factor = 0.2
draft_ratio = 0.89

MASS = {"s": 1.0 / 4.0, "d": 1.0 / 12.0}


def same_weight(z, x, y, along):
    wx, wy = (4.0, 1.0) if along == 0 else (1.0, 4.0)
    total = 0.0
    if x == "d":
        total += wx * MASS[y] * MASS[z]
    if y == "d":
        total += wy * MASS[x] * MASS[z]
    if z == "d":
        total += MASS[x] * MASS[y]
    return total


DIAGONAL = 2.0 / 3.0


def iota(shape, axis):
    return lax.broadcasted_iota(jnp.int32, shape, axis)


def roll(value, shift, axis):
    size = value.shape[axis]
    if isinstance(shift, int):
        shift = shift % size
        if shift == 0:
            return value
    return pltpu.roll(value, shift, axis)


def plane_sums(lo, lo_right, hi, hi_right):
    ls, ld = lo + lo_right, lo_right - lo
    hs, hd = hi + hi_right, hi_right - hi
    return {"ss": ls + hs, "sd": ld + hd, "ds": hs - ls, "dd": hd - ld}


def element_forces(u_low, u_high, v_low, v_high, mu):
    u, v = {}, {}
    for xy in ("ss", "sd", "ds", "dd"):
        if xy != "ss":
            u["s" + xy] = u_low[xy] + u_high[xy]
            v["s" + xy] = v_low[xy] + v_high[xy]
        u["d" + xy] = u_high[xy] - u_low[xy]
        v["d" + xy] = v_high[xy] - v_low[xy]
    scaled = {}

    def times_mu(factor):
        if factor not in scaled:
            scaled[factor] = mu * factor
        return scaled[factor]

    fu, fv = {}, {}
    for key in u:
        z, xy = key[0], key[1:]
        for along, mine, other, out in ((0, u, v, fu), (1, v, u, fv)):
            own = same_weight(z, xy[0], xy[1], along)
            if xy in ("ds", "sd"):
                first = xy == "ds"
                double = first if along == 0 else not first
                cross = MASS[z] * (2.0 if double else 1.0) / 4.0
                swapped = z + ("sd" if first else "ds")
                out[key] = times_mu(own) * (mine[key] + (cross / own) * other[swapped])
            else:
                out[key] = times_mu(own) * mine[key]
    return fu, fv


def lower_part(f):
    out = {xy: f["s" + xy] - f["d" + xy] for xy in ("sd", "ds", "dd")}
    out["ss"] = -f["dss"]
    return out


def upper_part(f):
    out = {xy: f["s" + xy] + f["d" + xy] for xy in ("sd", "ds", "dd")}
    out["ss"] = f["dss"]
    return out


GROUPS = {
    "top": ((0, 1), (128, 32), (144, 24), (144, 8)),
    "mid": ((1, 5), (0, 64), (0, 64), (0, 32)),
    "low": ((5, 10), (64, 64), (64, 80), (64, 40)),
}
ORDER = ("top", "mid", "low")
PACK_ROWS = 160
STATIC_ROW = 160


def packed_place(group, field, chunk):
    first = GROUPS[group][0][0]
    if group == "top":
        return 4 * ROWS, 16 * field
    return (field + (2 if group == "low" else 0)) * ROWS, (chunk - first) * 16


def level_row(group, field, chunk):
    start, span = GROUPS[group][3]
    return start + field * span + (chunk - GROUPS[group][0][0]) * CHUNK


def kernel(
    force_in, visc_in, drag_in, imask_in, thick_in, target_in, temp_in, salt_in, diff_in, omask_in, source_in,
    vel_out, thick_out, temp_out, salt_out,
    force, visc, drag, imask, thick, target, diff, omask, source,
    fa, fb, coef, opack, orow, rpack, rrow, merged,
    va, vb, mu, rdiag, ipack, imsg, rside, rmsg, rcorner,
    vright, low_y, high_y, shifts, sides,
    edge_e, col_lo, col_hi, col_mu, col_q, row_q, row_mu,
    wpack, wmsg, rwpack, rwmsg, rwcorner,
    pad_in, draft, tbl, mid, fwd, got,
    in_sem, o_send, o_recv, i_send, i_recv, w_send, w_recv, a_send, a_recv, b_send, b_recv,
):
    gx, gy = lax.axis_index("gx"), lax.axis_index("gy")
    nx, ny = lax.axis_size("gx"), lax.axis_size("gy")

    def at(dx, dy):
        return (lax.rem(gx + (dx + nx), nx), lax.rem(gy + (dy + ny), ny))

    north, south, west, east = at(-1, 0), at(1, 0), at(0, -1), at(0, 1)
    corners = (at(-1, -1), at(-1, 1), at(1, -1), at(1, 1))

    lane8 = iota((SUB, LANES), 1)
    sub8 = iota((SUB, LANES), 0)
    pair8 = lane8 // 2

    pairs = [(visc_in, visc), (imask_in, imask), (thick_in, thick), (target_in, target), (source_in, source)]
    for field, ref in ((0, temp_in), (1, salt_in)):
        start = FBASE + field * FSPAN + ROWS
        pairs.append((ref, fa.at[pl.ds(start, ZO * ROWS)]))
    pairs += [(diff_in, diff), (omask_in, omask), (drag_in, drag), (force_in, force)]
    loads = [pltpu.make_async_copy(src, dst, in_sem.at[n]) for n, (src, dst) in enumerate(pairs)]
    for copy in loads:
        copy.start()
    barrier = pltpu.get_barrier_semaphore()
    peers = [north, south, *corners]
    peers += [at(0, q) for q in range(1, ny)] + [at(p, 0) for p in range(2, nx - 1)]
    for peer in peers:
        pl.semaphore_signal(barrier, inc=1, device_id=peer, device_id_type=MESH)

    has_n = (gx > 0).astype(F32)
    has_s = (gx < nx - 1).astype(F32)
    has_w = (gy > 0).astype(F32)
    has_e = (gy < ny - 1).astype(F32)

    sends = []

    def send(src, dst, ssem, rsem, device):
        copy = pltpu.make_async_remote_copy(
            src_ref=src, dst_ref=dst, send_sem=ssem, recv_sem=rsem, device_id=device, device_id_type=MESH
        )
        copy.start()
        sends.append(copy)
        return copy

    wmsg[...] = jnp.zeros_like(wmsg)
    va[...] = jnp.zeros_like(va)
    vb[...] = jnp.zeros_like(vb)
    edge_e[...] = jnp.zeros_like(edge_e)
    col_lo[...] = jnp.zeros_like(col_lo)
    col_hi[...] = jnp.zeros_like(col_hi)
    col_mu[...] = jnp.zeros_like(col_mu)
    imsg[...] = jnp.zeros_like(imsg)
    pad_in[...] = jnp.zeros_like(pad_in)
    opack[...] = jnp.zeros_like(opack)
    orow[...] = jnp.zeros_like(orow)
    row_no, col_no = iota((2 * LANES, 2 * LANES), 0) % LANES, iota((2 * LANES, 2 * LANES), 1)
    before = (row_no == col_no - 1) & (col_no < LANES)
    after = (row_no == col_no + 1 - LANES) & (col_no >= LANES)
    shifts[...] = (before | after).astype(F32).astype(jnp.bfloat16)
    for copy in loads[:5]:
        copy.wait()
    wet_ice = imask[...].astype(F32)
    for t in range(TILES):
        acc = jnp.zeros((SUB, LANES), F32)
        wet_t = wet_ice[t * SUB : (t + 1) * SUB]
        for k in range(CELLS):
            rows = pl.ds(k * ROWS + t * SUB, SUB)
            weight = visc[rows] * wet_t
            mu[pl.ds(SUB + k * ROWS + t * SUB, SUB)] = weight
            acc = jnp.where(pair8 == k, roll(weight, 2 * k + 1, 1), acc)
        wpack[pl.ds(t * SUB, SUB)] = acc
    wmsg[pl.ds(0, 8)] = mu[pl.ds(SUB + ROWS - 1, 8, stride=ROWS)]
    wmsg[pl.ds(8, 2)] = mu[pl.ds(SUB + 8 * ROWS + ROWS - 1, 2, stride=ROWS)]
    wmsg[pl.ds(16, 1)] = wpack[pl.ds(ROWS - 1, 1)]

    lane1 = iota((SUB, LANES), 1)
    to_row = jnp.full((SUB, LANES), -1, jnp.int32)
    from_row = jnp.full((SUB, LANES), -1, jnp.int32)
    to_col = [jnp.full((SUB, LANES), -1, jnp.int32) for _ in range(TILES)]
    from_col = [jnp.full((SUB, LANES), -1, jnp.int32) for _ in range(TILES)]
    for i in range(ROWS):
        to_row = jnp.where(lane1 == i, target[i], to_row)
        from_row = jnp.where(lane1 == i, source[i], from_row)
        to_col[i // SUB] = jnp.where(sub8 == i % SUB, target[i], to_col[i // SUB])
        from_col[i // SUB] = jnp.where(sub8 == i % SUB, source[i], from_col[i // SUB])

    def slot_of(ids):
        device = ids >> 5
        return jnp.where(ids >= 0, (device & (ny - 1)) * nx + (device >> 4), -1)

    def by_slot(row):
        slots = slot_of(row)
        return jnp.concatenate(
            [(sub8 + n * SUB == slots).astype(F32) for n in range(LANES // SUB)], axis=0
        )

    def by_device(cols):
        return jnp.concatenate(
            [((lane8 == (ids >> 5)) & (ids >= 0)).astype(F32) for ids in cols], axis=0
        )

    def pick(one_hot, values):
        return jnp.dot(one_hot, values, precision=lax.Precision.HIGHEST, preferred_element_type=F32)

    pad_in[pl.ds(0, ROWS)] = draft_ratio * thick[...]
    tbl[0] = pick(by_slot(to_row), pad_in[...])

    pl.semaphore_wait(barrier, len(peers))

    def scatter_first(n):
        copies = []
        for q in range(1, ny):
            peer = at(0, q)
            copies.append(
                send(
                    tbl.at[n, pl.ds(pl.multiple_of(peer[1] * nx, nx), nx)],
                    mid.at[n, pl.ds(pl.multiple_of(gy * nx, nx), nx)],
                    a_send.at[n, q], a_recv.at[n, q], peer,
                )
            )
        own = pl.ds(pl.multiple_of(gy * nx, nx), nx)
        mid[n, own] = tbl[n, own]
        return copies

    def scatter_second(n, copies):
        for copy in copies:
            copy.wait_recv()
        for p in range(nx):
            fwd[n, pl.ds(p * ny, ny)] = mid[n, pl.ds(p, ny, stride=nx)]
        copies = []
        for p in range(1, nx):
            peer = at(p, 0)
            copies.append(
                send(
                    fwd.at[n, pl.ds(pl.multiple_of(peer[0] * ny, ny), ny)],
                    got.at[n, pl.ds(pl.multiple_of(gx * ny, ny), ny)],
                    b_send.at[n, p], b_recv.at[n, p], peer,
                )
            )
        own = pl.ds(pl.multiple_of(gx * ny, ny), ny)
        got[n, own] = fwd[n, own]
        return copies

    weights = [
        send(wmsg, rwmsg, w_send.at[0], w_recv.at[0], south),
        send(wpack, rwpack, w_send.at[1], w_recv.at[1], east),
        send(wmsg.at[pl.ds(16, 8)], rwcorner, w_send.at[2], w_recv.at[2], corners[3]),
    ]
    coupling = scatter_first(0)

    for copy in loads[5:]:
        copy.wait()

    def guard(ref, ends):
        for field in range(2):
            base = FBASE + field * FSPAN
            if "top" in ends:
                ref[pl.ds(base, ROWS)] = ref[pl.ds(base + ROWS, ROWS)]
            if "low" in ends:
                ref[pl.ds(base + (ZO + 1) * ROWS, ROWS)] = ref[pl.ds(base + ZO * ROWS, ROWS)]

    def put_pack(r, group, field, chunk, t, acc):
        first, lane = packed_place(group, field, chunk)
        rows = pl.ds(first + t * SUB, SUB)
        shifted = roll(acc, lane, 1)
        mine = (lane8 >= lane) & (lane8 < lane + 16)
        opack[r, rows] = jnp.where(mine, shifted, opack[r, rows])

    def put_rows(r, ref, group, field, chunk):
        base = FBASE + field * FSPAN + ROWS + chunk * (CHUNK * ROWS)
        start = level_row(group, field, chunk)
        rows = pl.ds(start if isinstance(start, int) else pl.multiple_of(start, SUB), SUB)
        orow[r, 0, rows] = ref[pl.ds(base, SUB, stride=ROWS)]
        orow[r, 1, rows] = ref[pl.ds(base + ROWS - 1, SUB, stride=ROWS)]

    def first_edges(group, chunk):
        for field in range(2):
            base = FBASE + field * FSPAN + ROWS + chunk * (CHUNK * ROWS)
            if not isinstance(base, int):
                base = pl.multiple_of(base, SUB)
            for t in range(TILES):
                acc = jnp.zeros((SUB, LANES), F32)
                for j in range(CHUNK):
                    value = fa[pl.ds(base + j * ROWS + t * SUB, SUB)]
                    acc = jnp.where(pair8 == j, roll(value, 2 * j + 1, 1), acc)
                put_pack(0, group, field, chunk, t, acc)
            put_rows(0, fa, group, field, chunk)

    def over_chunks(group, step):
        def body(chunk, carry):
            step(group, chunk)
            return carry

        if group == "top":
            step(group, 0)
        else:
            lax.fori_loop(*GROUPS[group][0], body, 0)

    def send_ocean(r, group):
        n = ORDER.index(group)
        cols, rows = (pl.ds(*GROUPS[group][m]) for m in (1, 2))
        return [
            send(orow.at[r, 0, rows], rrow.at[r, 1, rows], o_send.at[r, n, 0], o_recv.at[r, n, 0], north),
            send(orow.at[r, 1, rows], rrow.at[r, 0, rows], o_send.at[r, n, 1], o_recv.at[r, n, 1], south),
            send(opack.at[r, cols], rpack.at[r, 1, cols], o_send.at[r, n, 2], o_recv.at[r, n, 2], west),
            send(opack.at[r, cols], rpack.at[r, 0, cols], o_send.at[r, n, 3], o_recv.at[r, n, 3], east),
        ]

    ocean = {}
    guard(fa, ("top", "low"))
    wet = omask[...].astype(F32)
    diffusion = diff[...]
    orow[0, 0, pl.ds(STATIC_ROW, 1)] = diffusion[0:1]
    orow[0, 0, pl.ds(STATIC_ROW + 1, 1)] = wet[0:1]
    orow[0, 1, pl.ds(STATIC_ROW, 1)] = diffusion[ROWS - 1 :]
    orow[0, 1, pl.ds(STATIC_ROW + 1, 1)] = wet[ROWS - 1 :]
    for t in range(TILES):
        rows = pl.ds(4 * ROWS + t * SUB, SUB)
        acc = opack[0, rows]
        acc = jnp.where(pair8 == 32, roll(diffusion[t * SUB : (t + 1) * SUB], 65, 1), acc)
        acc = jnp.where(pair8 == 33, roll(wet[t * SUB : (t + 1) * SUB], 67, 1), acc)
        opack[0, rows] = acc
    for group in ("low", "top", "mid"):
        over_chunks(group, first_edges)
        ocean[group] = send_ocean(0, group)

    for copy in weights:
        copy.wait_recv()
    row_mu[...] = rwmsg[pl.ds(0, 16)] * has_n
    even = (lane8 & 1) == 0
    for t in range(TILES):
        col_mu[pl.ds(SUB + t * SUB, SUB)] = jnp.where(even, rwpack[pl.ds(t * SUB, SUB)] * has_w, 0.0)
    even1 = (iota((1, LANES), 1) & 1) == 0
    col_mu[pl.ds(SUB - 1, 1)] = jnp.where(even1, rwcorner[pl.ds(0, 1)] * (has_w * has_n), 0.0)

    def put_ice_edges(r, ref):
        for c in range(2):
            for edge in range(2):
                start = c * NODES * VSPAN + edge * (ROWS - 1)
                imsg[r, edge, pl.ds(c * 16, 16)] = ref[pl.ds(start, 16, stride=VSPAN)]
        imsg[r, 0, pl.ds(32, 1)] = ipack[r, pl.ds(0, 1)]
        imsg[r, 1, pl.ds(32, 1)] = ipack[r, pl.ds(ROWS - 1, 1)]

    def send_ice(r):
        copies = [
            send(imsg.at[r, 0], rmsg.at[r, 1], i_send.at[r, 0], i_recv.at[r, 0], north),
            send(imsg.at[r, 1], rmsg.at[r, 0], i_send.at[r, 1], i_recv.at[r, 1], south),
            send(ipack.at[r], rside.at[r, 1], i_send.at[r, 2], i_recv.at[r, 2], west),
            send(ipack.at[r], rside.at[r, 0], i_send.at[r, 3], i_recv.at[r, 3], east),
        ]
        for n, device in enumerate(corners):
            src = imsg.at[r, n // 2, pl.ds(32, 8)]
            copies.append(send(src, rcorner.at[r, 3 - n], i_send.at[r, 4 + n], i_recv.at[r, 4 + n], device))
        return copies

    for t in range(TILES):
        cols = col_mu[pl.ds(SUB + t * SUB, SUB)] + col_mu[pl.ds(SUB - 1 + t * SUB, SUB)]
        cols = cols + roll(cols, 2, 1)
        acc = jnp.zeros((SUB, LANES), F32)
        below = None
        for k in range(NODES):
            layer = None
            if k < CELLS:
                start = SUB + k * ROWS + t * SUB
                up = mu[pl.ds(start - 1, SUB)]
                if t == 0:
                    up = jnp.where(sub8 == 0, row_mu[pl.ds(k, 1)], up)
                layer = mu[pl.ds(start, SUB)] + up
            total = layer if below is None else (below if layer is None else layer + below)
            below = layer
            left = jnp.where(lane8 == 0, roll(cols, -2 * k, 1), roll(total, 1, 1))
            diagonal = DIAGONAL * (total + left) + shift_term
            if k == 0:
                diagonal = diagonal + drag[pl.ds(t * SUB, SUB)]
            factor = relax_weight / diagonal
            rdiag[pl.ds(k * ROWS + t * SUB, SUB)] = factor
            for c in range(2):
                value = force[pl.ds((c * NODES + k) * ROWS + t * SUB, SUB)] * factor
                va[pl.ds((c * NODES + k) * VSPAN + t * SUB, SUB)] = value
                acc = jnp.where(pair8 == 32 * c + k, roll(value, 64 * c + 2 * k + 1, 1), acc)
        ipack[0, pl.ds(t * SUB, SUB)] = acc
    put_ice_edges(0, va)
    ice = send_ice(0)

    def take_ocean(r, group):
        for copy in ocean[group]:
            copy.wait_recv()
        first, count = GROUPS[group][1]
        for n in range(count // SUB):
            rows = pl.ds(first + n * SUB, SUB)
            from_e = roll(rpack[r, 1, rows], -1, 1)
            from_w = roll(rpack[r, 0, rows], 1, 1)
            merged[rows] = jnp.where(even, from_e, from_w)

    coupling = scatter_second(0, coupling)
    take_ocean(0, "top")
    for t in range(TILES):
        rows = slice(t * SUB, (t + 1) * SUB)
        d, w = diffusion[rows], wet[rows]

        def around(mine, plane, n):
            whole = plane
            up = roll(mine, 1, 0)
            above = rrow[0, 0, pl.ds(STATIC_ROW + n, 1)] if t == 0 else whole[t * SUB - 1 : t * SUB]
            up = jnp.where(sub8 == 0, above, up)
            down = roll(mine, -1, 0)
            below = rrow[0, 1, pl.ds(STATIC_ROW + n, 1)] if t == TILES - 1 else whole[(t + 1) * SUB : (t + 1) * SUB + 1]
            down = jnp.where(sub8 == SUB - 1, below, down)
            edge = roll(merged[pl.ds(4 * ROWS + t * SUB, SUB)], 127 - 64 - 2 * n, 1)
            left = jnp.where(lane8 == 0, edge, roll(mine, 1, 1))
            right = jnp.where(lane8 == LANES - 1, edge, roll(mine, -1, 1))
            return up, down, left, right

        near_d = around(d, diffusion, 0)
        up_w, down_w, left_w, right_w = around(w, wet, 1)
        if t == 0:
            up_w = jnp.where(sub8 == 0, up_w * has_n, up_w)
        if t == TILES - 1:
            down_w = jnp.where(sub8 == SUB - 1, down_w * has_s, down_w)
        left_w = jnp.where(lane8 == 0, left_w * has_w, left_w)
        right_w = jnp.where(lane8 == LANES - 1, right_w * has_e, right_w)
        total = 2.0 * vert_mix * w
        for n, (near, near_w) in enumerate(zip(near_d, (up_w, down_w, left_w, right_w))):
            face = 0.5 * (d + near) * w * near_w
            coef[pl.ds((n + 1) * ROWS + t * SUB, SUB)] = face
            total = total + face
        coef[pl.ds(t * SUB, SUB)] = 1.0 - total
        coef[pl.ds(5 * ROWS + t * SUB, SUB)] = vert_mix * w

    def melt_of(temp_top, salt_top, t):
        freezing = freeze_slope * (salt_ref + salt_top) + freeze_base - freeze_depth * draft[pl.ds(t * SUB, SUB)]
        return heat_gamma * (temp_top - freezing) * (10.0 * coef[pl.ds(5 * ROWS + t * SUB, SUB)])

    def ocean_chunk(s, group, chunk, src, dst):
        for field in range(2):
            base = FBASE + field * FSPAN + ROWS + chunk * (CHUNK * ROWS)
            if not isinstance(base, int):
                base = pl.multiple_of(base, SUB)
            values = src[pl.ds(base, CHUNK * ROWS)]
            high = values.astype(jnp.bfloat16)
            rest = (values - high.astype(F32)).astype(jnp.bfloat16)
            both = jnp.concatenate([high, rest], axis=1)
            sides[pl.ds(field * CHUNK * ROWS, CHUNK * ROWS)] = jnp.dot(
                both, shifts[...], preferred_element_type=F32
            )
        for t in range(TILES):
            cs = [coef[pl.ds(n * ROWS + t * SUB, SUB)] for n in range(6)]
            first = []
            for field in range(2):
                base = FBASE + field * FSPAN + ROWS + chunk * (CHUNK * ROWS) + t * SUB
                if not isinstance(base, int):
                    base = pl.multiple_of(base, SUB)
                vec, lane = packed_place(group, field, chunk)
                packed = merged[pl.ds(vec + t * SUB, SUB)]
                packed = roll(packed, -lane if isinstance(lane, int) else lax.rem(LANES - lane, LANES), 1)
                acc = jnp.zeros((SUB, LANES), F32)
                prev = src[pl.ds(base - ROWS, SUB)]
                cur = src[pl.ds(base, SUB)]
                news = []
                for j in range(CHUNK):
                    row = base + j * ROWS
                    nxt = src[pl.ds(row + ROWS, SUB)]
                    up = src[pl.ds(row - 1, SUB)]
                    down = src[pl.ds(row + 1, SUB)]
                    level = level_row(group, field, chunk) + j
                    if t == 0:
                        up = jnp.where(sub8 == 0, rrow[s, 0, pl.ds(level, 1)], up)
                    if t == TILES - 1:
                        down = jnp.where(sub8 == SUB - 1, rrow[s, 1, pl.ds(level, 1)], down)
                    edge = roll(packed, 127 - 2 * j, 1)
                    beside = pl.ds(field * CHUNK * ROWS + j * ROWS + t * SUB, SUB)
                    left = jnp.where(lane8 == 0, edge, sides[beside, :LANES])
                    right = jnp.where(lane8 == LANES - 1, edge, sides[beside, LANES:])
                    new = (
                        cs[0] * cur
                        + (cs[1] * up + cs[2] * down)
                        + (cs[3] * left + cs[4] * right)
                        + cs[5] * (prev + nxt)
                    )
                    news.append(new)
                    prev, cur = cur, nxt
                first.append(news)
            if group == "top":
                temp_top, salt_top = first[0][0], first[1][0]
                rate = melt_of(temp_top, salt_top, t)
                first[0][0] = temp_top - heat_factor * rate
                first[1][0] = salt_top - salt_factor * rate * (salt_ref + salt_top) / salt_ref
            for field in range(2):
                acc = jnp.zeros((SUB, LANES), F32)
                for j in range(CHUNK):
                    new = first[field][j]
                    if s < STEPS - 1:
                        row = FBASE + field * FSPAN + ROWS + chunk * (CHUNK * ROWS) + t * SUB + j * ROWS
                        if not isinstance(row, int):
                            row = pl.multiple_of(row, SUB)
                        dst[pl.ds(row, SUB)] = new
                        acc = jnp.where(pair8 == j, roll(new, 2 * j + 1, 1), acc)
                    else:
                        row = chunk * (CHUNK * ROWS) + j * ROWS + t * SUB
                        if not isinstance(row, int):
                            row = pl.multiple_of(row, SUB)
                        dst[field][pl.ds(row, SUB)] = new
                if s < STEPS - 1:
                    put_pack(s + 1, group, field, chunk, t, acc)
        if s < STEPS - 1:
            for field in range(2):
                put_rows(s + 1, dst, group, field, chunk)

    def ocean_part(s, group, src, dst, taken=False):
        if not taken:
            take_ocean(s, group)
        over_chunks(group, lambda part, chunk: ocean_chunk(s, part, chunk, src, dst))
        if s < STEPS - 1:
            guard(dst, (group,))
            ocean[group] = send_ocean(s + 1, group)

    def ice_sweep(r, copies, src, dst):
        last = r == SWEEPS - 1
        for copy in copies:
            copy.wait_recv()
        for c in range(2):
            for k in range(NODES):
                src[pl.ds((c * NODES + k) * VSPAN + ROWS, 1)] = rmsg[r, 1, pl.ds(c * 16 + k, 1)] * has_s
        for t in range(TILES):
            rows = pl.ds(t * SUB, SUB)
            edge_e[rows] = rside[r, 1, rows] * has_e
            col_lo[pl.ds(SUB + t * SUB, SUB)] = rside[r, 0, rows] * has_w
            col_hi[pl.ds(SUB + t * SUB, SUB)] = roll(ipack[r, rows], -1, 1)
        edge_e[pl.ds(ROWS, 1)] = rcorner[r, 3, pl.ds(0, 1)] * (has_e * has_s)
        col_lo[pl.ds(SUB - 1, 1)] = rcorner[r, 0, pl.ds(0, 1)] * (has_w * has_n)
        col_lo[pl.ds(SUB + ROWS, 1)] = rcorner[r, 2, pl.ds(0, 1)] * (has_w * has_s)
        col_hi[pl.ds(SUB - 1, 1)] = roll(rmsg[r, 0, pl.ds(32, 1)] * has_n, -1, 1)
        col_hi[pl.ds(SUB + ROWS, 1)] = roll(rmsg[r, 1, pl.ds(32, 1)] * has_s, -1, 1)
        for t in range(TILES + 1):
            start = SUB - 1 + t * SUB
            if t == TILES:
                start = ROWS
            lo0, lo1 = col_lo[pl.ds(start, SUB)], col_lo[pl.ds(start + 1, SUB)]
            hi0, hi1 = col_hi[pl.ds(start, SUB)], col_hi[pl.ds(start + 1, SUB)]
            planes = []
            for c in range(2):
                parts = [roll(value, 64 * c, 1) for value in (lo0, hi0, lo1, hi1)]
                low = plane_sums(*parts)
                planes += [low, {key: roll(value, -2, 1) for key, value in low.items()}]
            fu, fv = element_forces(*planes, col_mu[pl.ds(start, SUB)])
            for c, f in enumerate((fu, fv)):
                low, high = lower_part(f), upper_part(f)
                node = {key: low[key] + roll(high[key], 2, 1) for key in low}
                behind = {x: node[x + "s"] + node[x + "d"] for x in "sd"}
                col_q[2 * c, pl.ds(start - SUB + 1, SUB)] = behind["s"] - behind["d"]
                col_q[2 * c + 1, pl.ds(start - SUB + 1, SUB)] = behind["s"] + behind["d"]
        lane16, sub16 = iota((16, LANES), 1), iota((16, LANES), 0)

        def upright(row, offset):
            chosen = jnp.where(lane16 == 2 * sub16 + offset, row, 0.0)
            return jnp.sum(chosen, axis=1, keepdims=True)

        planes = []
        for c in range(2):
            lo = rmsg[r, 0, pl.ds(c * 16, 16)]
            hi = imsg[r, 0, pl.ds(c * 16, 16)]
            lo_end = upright(rcorner[r, 1, pl.ds(0, 1)] * (has_e * has_n), 64 * c + 1)
            hi_end = upright(edge_e[pl.ds(0, 1)], 64 * c + 1)
            lo_right = jnp.where(lane16 == LANES - 1, lo_end, roll(lo, -1, 1))
            hi_right = jnp.where(lane16 == LANES - 1, hi_end, roll(hi, -1, 1))
            low = plane_sums(lo, lo_right, hi, hi_right)
            planes += [low, {key: roll(value, -1, 0) for key, value in low.items()}]
        fu, fv = element_forces(*planes, row_mu[...])
        for c, f in enumerate((fu, fv)):
            low, high = lower_part(f), upper_part(f)
            node = {key: low[key] + roll(high[key], 1, 0) for key in low}
            for n, sign in enumerate((-1.0, 1.0)):
                parts = [node[x + "s"] + sign * node[x + "d"] for x in "sd"]
                row_q[pl.ds((2 * n + c) * 16, 16)] = parts[0] + parts[1]
        for c in range(2):
            for k in range(NODES):
                shift = 127 - (64 * c + 2 * k + 1)
                for t in range(TILES + 1):
                    rows = pl.ds((c * NODES + k) * VSPAN + t * SUB, SUB)
                    edge = roll(edge_e[pl.ds(t * SUB, SUB)], shift, 1)
                    vright[rows] = jnp.where(lane8 == LANES - 1, edge, roll(src[rows], -1, 1))
        pass_down = {}
        for t in range(TILES):
            below, carried = None, None
            for k in range(NODES + 1):
                planes = None
                if k < NODES:
                    planes = []
                    for c in range(2):
                        start = (c * NODES + k) * VSPAN + t * SUB
                        lo, hi = pl.ds(start, SUB), pl.ds(start + 1, SUB)
                        planes.append(plane_sums(src[lo], vright[lo], src[hi], vright[hi]))
                if k >= 1:
                    level = k - 1
                    nodes, ups = [None, None], [None, None]
                    if level < CELLS:
                        weight = mu[pl.ds(SUB + level * ROWS + t * SUB, SUB)]
                        forces = element_forces(below[0], planes[0], below[1], planes[1], weight)
                        for c in range(2):
                            nodes[c], ups[c] = lower_part(forces[c]), upper_part(forces[c])
                            if carried is not None:
                                nodes[c] = {key: nodes[c][key] + carried[c][key] for key in nodes[c]}
                    else:
                        nodes = carried
                    carried = ups
                    for c in range(2):
                        node = nodes[c]
                        row = pl.ds((c * NODES + level) * ROWS + t * SUB, SUB)
                        for n, (sign, place) in enumerate(((-1.0, low_y), (1.0, high_y))):
                            parts = [node[x + "s"] + sign * node[x + "d"] for x in "sd"]
                            down = roll(parts[0] + parts[1], 1, 0)
                            if t == 0:
                                over = row_q[pl.ds((2 * n + c) * 16 + level, 1)]
                            else:
                                over = pass_down[n, c, level]
                            pass_down[n, c, level] = down[0:1]
                            place[row] = parts[0] - parts[1] + jnp.where(sub8 == 0, over, down)
                below = planes
        for c in range(2):
            for t in range(TILES):
                strip = col_q[2 * c, pl.ds(1 + t * SUB, SUB)] + col_q[2 * c + 1, pl.ds(t * SUB, SUB)]
                for level in range(NODES):
                    at_row = (c * NODES + level) * ROWS + t * SUB
                    row = pl.ds(at_row, SUB)
                    before = jnp.where(lane8 == 0, roll(strip, -2 * level, 1), roll(high_y[row], 1, 1))
                    value = src[pl.ds((c * NODES + level) * VSPAN + t * SUB, SUB)]
                    extra = shift_term
                    if level == 0:
                        extra = shift_term + drag[pl.ds(t * SUB, SUB)]
                    applied = low_y[row] + before + extra * value
                    value = value + (force[row] - applied) * rdiag[pl.ds(level * ROWS + t * SUB, SUB)]
                    if last:
                        dst[row] = value
                    else:
                        dst[pl.ds((c * NODES + level) * VSPAN + t * SUB, SUB)] = value
        if last:
            return None
        for t in range(TILES):
            acc = jnp.zeros((SUB, LANES), F32)
            for c in range(2):
                for level in range(NODES):
                    value = dst[pl.ds((c * NODES + level) * VSPAN + t * SUB, SUB)]
                    acc = jnp.where(pair8 == 32 * c + level, roll(value, 64 * c + 2 * level + 1, 1), acc)
            ipack[r + 1, pl.ds(t * SUB, SUB)] = acc
        put_ice_edges(r + 1, dst)
        return send_ice(r + 1)

    ocean_part(0, "low", fa, fb)
    ocean_part(0, "mid", fa, fb)
    for copy in coupling:
        copy.wait_recv()
    draft[...] = pick(by_device(from_col), got[0])
    ocean_part(0, "top", fa, fb, True)
    ice = ice_sweep(0, ice, va, vb)
    ocean_part(1, "low", fb, fa)
    ocean_part(1, "top", fb, fa)
    ocean_part(1, "mid", fb, fa)
    ice = ice_sweep(1, ice, vb, va)
    ocean_part(2, "top", fa, fb)
    ocean_part(2, "low", fa, fb)
    ocean_part(2, "mid", fa, fb)
    ocean_part(3, "top", fb, (temp_out, salt_out))
    for t in range(TILES):
        rows = pl.ds(t * SUB, SUB)
        pad_in[rows] = melt_of(temp_out[rows], salt_out[rows], t)
    tbl[1] = pick(by_slot(from_row), pad_in[...])
    coupling = scatter_first(1)
    ice_sweep(2, ice, va, vel_out)
    ocean_part(3, "mid", fb, (temp_out, salt_out))
    coupling = scatter_second(1, coupling)
    ocean_part(3, "low", fb, (temp_out, salt_out))
    for copy in coupling:
        copy.wait_recv()
    melt = pick(by_device(to_col), got[1])
    thick_out[...] = thick[...] - melt_factor * melt * wet_ice
    for copy in sends:
        copy.wait_send()


def per_device(
    ice_force, ice_visc, ice_drag, ice_mask, ice_thick, ice_target,
    ocean_temp, ocean_salt, ocean_diff, ocean_mask, ocean_source,
):
    def flat(array):
        return pltpu.with_memory_space_constraint(array.reshape(-1, LANES), pltpu.HBM)

    def held(array):
        return pltpu.with_memory_space_constraint(array, pltpu.HBM)

    vmem = pl.BlockSpec(memory_space=pltpu.VMEM)
    hbm = pl.BlockSpec(memory_space=pltpu.HBM)
    dma = pltpu.SemaphoreType.DMA

    def buf(*shape):
        return pltpu.VMEM((*shape, LANES), F32)

    nx, ny = lax.axis_size("gx"), lax.axis_size("gy")
    whole = pltpu.VMEM((ROWS, LANES), jnp.int32)
    ids = pltpu.SMEM((ROWS,), jnp.int32)
    scratch = [
        buf(2 * NODES * ROWS), buf(CELLS * ROWS), buf(ROWS), whole, buf(ROWS), ids, buf(ROWS), whole, ids,
        buf(FROWS), buf(FROWS), buf(6 * ROWS), buf(STEPS, PACK_ROWS), buf(STEPS, 2, 2 * ZO + SUB),
        buf(STEPS, 2, PACK_ROWS), buf(STEPS, 2, 2 * ZO + SUB), buf(PACK_ROWS),
        buf(VROWS), buf(VROWS), buf(2 * SUB + CELLS * ROWS), buf(NODES * ROWS),
        buf(SWEEPS, ROWS), buf(SWEEPS, 2, 40), buf(SWEEPS, 2, ROWS), buf(SWEEPS, 2, 40), buf(SWEEPS, 4, SUB),
        buf(VROWS), buf(2 * NODES * ROWS), buf(2 * NODES * ROWS),
        pltpu.VMEM((2 * LANES, 2 * LANES), jnp.bfloat16), pltpu.VMEM((2 * CHUNK * ROWS, 2 * LANES), F32),
        buf(ROWS + SUB), buf(ROWS + 2 * SUB), buf(ROWS + 2 * SUB), buf(ROWS + 2 * SUB),
        buf(4, ROWS + SUB), buf(64), buf(16),
        buf(ROWS), buf(24), buf(ROWS), buf(24), buf(SUB),
        buf(LANES), buf(ROWS), buf(2, LANES), buf(2, LANES), buf(2, LANES), buf(2, LANES),
        dma((11,)), dma((STEPS, 3, 4)), dma((STEPS, 3, 4)), dma((SWEEPS, 8)), dma((SWEEPS, 8)),
        dma((3,)), dma((3,)), dma((2, ny)), dma((2, ny)), dma((2, nx)), dma((2, nx)),
    ]
    velocity, thickness, temp, salt = pl.pallas_call(
        kernel,
        out_shape=[
            jax.ShapeDtypeStruct((2 * NODES * ROWS, LANES), F32),
            jax.ShapeDtypeStruct((ROWS, LANES), F32),
            jax.ShapeDtypeStruct((ZO * ROWS, LANES), F32),
            jax.ShapeDtypeStruct((ZO * ROWS, LANES), F32),
        ],
        in_specs=[hbm] * 11,
        out_specs=[vmem] * 4,
        scratch_shapes=scratch,
        compiler_params=pltpu.CompilerParams(
            collective_id=0, has_side_effects=True, vmem_limit_bytes=40 * 1024 * 1024
        ),
    )(
        flat(ice_force), flat(ice_visc), held(ice_drag), held(ice_mask), held(ice_thick), held(ice_target),
        flat(ocean_temp), flat(ocean_salt), held(ocean_diff), held(ocean_mask), held(ocean_source),
    )
    return (
        velocity.reshape(ice_force.shape),
        thickness,
        temp.reshape(ocean_temp.shape),
        salt.reshape(ocean_salt.shape),
    )


def solution(mesh):
    in_specs = (
        P(None, None, "gx", "gy"),
        P(None, "gx", "gy"),
        P("gx", "gy"),
        P("gx", "gy"),
        P("gx", "gy"),
        P(("gx", "gy")),
        P(None, "gx", "gy"),
        P(None, "gx", "gy"),
        P("gx", "gy"),
        P("gx", "gy"),
        P(("gx", "gy")),
    )
    out_specs = (P(None, None, "gx", "gy"), P("gx", "gy"), P(None, "gx", "gy"), P(None, "gx", "gy"))
    return jax.shard_map(per_device, mesh=mesh, in_specs=in_specs, out_specs=out_specs, check_vma=False)
```

```python
import jax
import jax.numpy as jnp
from jax import lax
from jax.experimental import pallas as pl
from jax.experimental.pallas import tpu as pltpu
from jax.sharding import PartitionSpec as P

MESH = pl.DeviceIdType.MESH
F32 = jnp.float32

LANES = 128
SUB = 8
ROWS = 32
TILES = ROWS // SUB
ZO = 80
NODES = 11
CELLS = 10
STEPS = 4
SWEEPS = 3
CHUNK = 8
FBASE = 8
FSPAN = (ZO + 2) * ROWS
FROWS = 2 * FBASE + 2 * FSPAN
VSPAN = 40
VROWS = (NODES + 16) * VSPAN

relax_weight = 0.6
shift_term = 0.2
vert_mix = 0.1
heat_gamma = 0.5
heat_factor = 0.05
salt_factor = 0.05
salt_ref = 34.5
freeze_slope = -0.0573
freeze_base = 0.0832
freeze_depth = 0.761
melt_factor = 0.2
draft_ratio = 0.89

MASS = {"s": 1.0 / 4.0, "d": 1.0 / 12.0}


def same_weight(z, x, y, along):
    wx, wy = (4.0, 1.0) if along == 0 else (1.0, 4.0)
    total = 0.0
    if x == "d":
        total += wx * MASS[y] * MASS[z]
    if y == "d":
        total += wy * MASS[x] * MASS[z]
    if z == "d":
        total += MASS[x] * MASS[y]
    return total


DIAGONAL = 2.0 / 3.0


def iota(shape, axis):
    return lax.broadcasted_iota(jnp.int32, shape, axis)


def roll(value, shift, axis):
    size = value.shape[axis]
    if isinstance(shift, int):
        shift = shift % size
        if shift == 0:
            return value
    return pltpu.roll(value, shift, axis)


def plane_sums(lo, lo_right, hi, hi_right):
    ls, ld = lo + lo_right, lo_right - lo
    hs, hd = hi + hi_right, hi_right - hi
    return {"ss": ls + hs, "sd": ld + hd, "ds": hs - ls, "dd": hd - ld}


def element_forces(u_low, u_high, v_low, v_high, mu):
    u, v = {}, {}
    for xy in ("ss", "sd", "ds", "dd"):
        if xy != "ss":
            u["s" + xy] = u_low[xy] + u_high[xy]
            v["s" + xy] = v_low[xy] + v_high[xy]
        u["d" + xy] = u_high[xy] - u_low[xy]
        v["d" + xy] = v_high[xy] - v_low[xy]
    scaled = {}

    def times_mu(factor):
        if factor not in scaled:
            scaled[factor] = mu * factor
        return scaled[factor]

    fu, fv = {}, {}
    for key in u:
        z, xy = key[0], key[1:]
        for along, mine, other, out in ((0, u, v, fu), (1, v, u, fv)):
            own = same_weight(z, xy[0], xy[1], along)
            if xy in ("ds", "sd"):
                first = xy == "ds"
                double = first if along == 0 else not first
                cross = MASS[z] * (2.0 if double else 1.0) / 4.0
                swapped = z + ("sd" if first else "ds")
                out[key] = times_mu(own) * (mine[key] + (cross / own) * other[swapped])
            else:
                out[key] = times_mu(own) * mine[key]
    return fu, fv


def lower_part(f):
    out = {xy: f["s" + xy] - f["d" + xy] for xy in ("sd", "ds", "dd")}
    out["ss"] = -f["dss"]
    return out


def upper_part(f):
    out = {xy: f["s" + xy] + f["d" + xy] for xy in ("sd", "ds", "dd")}
    out["ss"] = f["dss"]
    return out


GROUPS = {
    "top": ((0, 1), (128, 32), (144, 24), (144, 8)),
    "mid": ((1, 5), (0, 64), (0, 64), (0, 32)),
    "low": ((5, 10), (64, 64), (64, 80), (64, 40)),
}
ORDER = ("top", "mid", "low")
PACK_ROWS = 160
STATIC_ROW = 160


def packed_place(group, field, chunk):
    first = GROUPS[group][0][0]
    if group == "top":
        return 4 * ROWS, 16 * field
    return (field + (2 if group == "low" else 0)) * ROWS, (chunk - first) * 16


def level_row(group, field, chunk):
    start, span = GROUPS[group][3]
    return start + field * span + (chunk - GROUPS[group][0][0]) * CHUNK


def kernel(
    force_in, visc_in, drag_in, imask_in, thick_in, target_in, temp_in, salt_in, diff_in, omask_in, source_in,
    vel_out, thick_out, temp_out, salt_out,
    force, visc, drag, imask, thick, target, diff, omask, source,
    fa, fb, coef, opack, orow, rpack, rrow, merged,
    va, vb, mu, rdiag, ipack, imsg, rside, rmsg, rcorner,
    vright, low_y, high_y, shifts, sides,
    edge_e, col_lo, col_hi, col_mu, col_q, row_q, row_mu,
    wpack, wmsg, rwpack, rwmsg, rwcorner,
    pad_in, draft, tbl, mid, fwd, got,
    in_sem, o_send, o_recv, i_send, i_recv, w_send, w_recv, a_send, a_recv, b_send, b_recv,
):
    gx, gy = lax.axis_index("gx"), lax.axis_index("gy")
    nx, ny = lax.axis_size("gx"), lax.axis_size("gy")

    def at(dx, dy):
        return (lax.rem(gx + (dx + nx), nx), lax.rem(gy + (dy + ny), ny))

    north, south, west, east = at(-1, 0), at(1, 0), at(0, -1), at(0, 1)
    corners = (at(-1, -1), at(-1, 1), at(1, -1), at(1, 1))

    lane8 = iota((SUB, LANES), 1)
    sub8 = iota((SUB, LANES), 0)
    pair8 = lane8 // 2

    pairs = [(visc_in, visc), (imask_in, imask), (thick_in, thick), (target_in, target), (source_in, source)]
    for field, ref in ((0, temp_in), (1, salt_in)):
        start = FBASE + field * FSPAN + ROWS
        pairs.append((ref, fa.at[pl.ds(start, ZO * ROWS)]))
    pairs += [(diff_in, diff), (omask_in, omask), (drag_in, drag), (force_in, force)]
    loads = [pltpu.make_async_copy(src, dst, in_sem.at[n]) for n, (src, dst) in enumerate(pairs)]
    for copy in loads:
        copy.start()
    barrier = pltpu.get_barrier_semaphore()
    peers = [north, south, *corners]
    peers += [at(0, q) for q in range(1, ny)] + [at(p, 0) for p in range(2, nx - 1)]
    for peer in peers:
        pl.semaphore_signal(barrier, inc=1, device_id=peer, device_id_type=MESH)

    has_n = (gx > 0).astype(F32)
    has_s = (gx < nx - 1).astype(F32)
    has_w = (gy > 0).astype(F32)
    has_e = (gy < ny - 1).astype(F32)

    sends = []

    def send(src, dst, ssem, rsem, device):
        copy = pltpu.make_async_remote_copy(
            src_ref=src, dst_ref=dst, send_sem=ssem, recv_sem=rsem, device_id=device, device_id_type=MESH
        )
        copy.start()
        sends.append(copy)
        return copy

    wmsg[...] = jnp.zeros_like(wmsg)
    va[...] = jnp.zeros_like(va)
    vb[...] = jnp.zeros_like(vb)
    edge_e[...] = jnp.zeros_like(edge_e)
    col_lo[...] = jnp.zeros_like(col_lo)
    col_hi[...] = jnp.zeros_like(col_hi)
    col_mu[...] = jnp.zeros_like(col_mu)
    imsg[...] = jnp.zeros_like(imsg)
    pad_in[...] = jnp.zeros_like(pad_in)
    opack[...] = jnp.zeros_like(opack)
    orow[...] = jnp.zeros_like(orow)
    row_no, col_no = iota((2 * LANES, 2 * LANES), 0) % LANES, iota((2 * LANES, 2 * LANES), 1)
    before = (row_no == col_no - 1) & (col_no < LANES)
    after = (row_no == col_no + 1 - LANES) & (col_no >= LANES)
    shifts[...] = (before | after).astype(F32).astype(jnp.bfloat16)
    for copy in loads[:5]:
        copy.wait()
    wet_ice = imask[...].astype(F32)
    for t in range(TILES):
        acc = jnp.zeros((SUB, LANES), F32)
        wet_t = wet_ice[t * SUB : (t + 1) * SUB]
        for k in range(CELLS):
            rows = pl.ds(k * ROWS + t * SUB, SUB)
            weight = visc[rows] * wet_t
            mu[pl.ds(SUB + k * ROWS + t * SUB, SUB)] = weight
            acc = jnp.where(pair8 == k, roll(weight, 2 * k + 1, 1), acc)
        wpack[pl.ds(t * SUB, SUB)] = acc
    wmsg[pl.ds(0, 8)] = mu[pl.ds(SUB + ROWS - 1, 8, stride=ROWS)]
    wmsg[pl.ds(8, 2)] = mu[pl.ds(SUB + 8 * ROWS + ROWS - 1, 2, stride=ROWS)]
    wmsg[pl.ds(16, 1)] = wpack[pl.ds(ROWS - 1, 1)]

    lane1 = iota((SUB, LANES), 1)
    to_row = jnp.full((SUB, LANES), -1, jnp.int32)
    from_row = jnp.full((SUB, LANES), -1, jnp.int32)
    to_col = [jnp.full((SUB, LANES), -1, jnp.int32) for _ in range(TILES)]
    from_col = [jnp.full((SUB, LANES), -1, jnp.int32) for _ in range(TILES)]
    for i in range(ROWS):
        to_row = jnp.where(lane1 == i, target[i], to_row)
        from_row = jnp.where(lane1 == i, source[i], from_row)
        to_col[i // SUB] = jnp.where(sub8 == i % SUB, target[i], to_col[i // SUB])
        from_col[i // SUB] = jnp.where(sub8 == i % SUB, source[i], from_col[i // SUB])

    def slot_of(ids):
        device = ids >> 5
        return jnp.where(ids >= 0, (device & (ny - 1)) * nx + (device >> 4), -1)

    def by_slot(row):
        slots = slot_of(row)
        return jnp.concatenate(
            [(sub8 + n * SUB == slots).astype(F32) for n in range(LANES // SUB)], axis=0
        )

    def by_device(cols):
        return jnp.concatenate(
            [((lane8 == (ids >> 5)) & (ids >= 0)).astype(F32) for ids in cols], axis=0
        )

    def pick(one_hot, values):
        return jnp.dot(one_hot, values, precision=lax.Precision.HIGHEST, preferred_element_type=F32)

    pad_in[pl.ds(0, ROWS)] = draft_ratio * thick[...]
    tbl[0] = pick(by_slot(to_row), pad_in[...])

    pl.semaphore_wait(barrier, len(peers))

    def scatter_first(n):
        copies = []
        for q in range(1, ny):
            peer = at(0, q)
            copies.append(
                send(
                    tbl.at[n, pl.ds(pl.multiple_of(peer[1] * nx, nx), nx)],
                    mid.at[n, pl.ds(pl.multiple_of(gy * nx, nx), nx)],
                    a_send.at[n, q], a_recv.at[n, q], peer,
                )
            )
        own = pl.ds(pl.multiple_of(gy * nx, nx), nx)
        mid[n, own] = tbl[n, own]
        return copies

    def scatter_second(n, copies):
        for copy in copies:
            copy.wait_recv()
        for p in range(nx):
            fwd[n, pl.ds(p * ny, ny)] = mid[n, pl.ds(p, ny, stride=nx)]
        copies = []
        for p in range(1, nx):
            peer = at(p, 0)
            copies.append(
                send(
                    fwd.at[n, pl.ds(pl.multiple_of(peer[0] * ny, ny), ny)],
                    got.at[n, pl.ds(pl.multiple_of(gx * ny, ny), ny)],
                    b_send.at[n, p], b_recv.at[n, p], peer,
                )
            )
        own = pl.ds(pl.multiple_of(gx * ny, ny), ny)
        got[n, own] = fwd[n, own]
        return copies

    weights = [
        send(wmsg, rwmsg, w_send.at[0], w_recv.at[0], south),
        send(wpack, rwpack, w_send.at[1], w_recv.at[1], east),
        send(wmsg.at[pl.ds(16, 8)], rwcorner, w_send.at[2], w_recv.at[2], corners[3]),
    ]
    coupling = scatter_first(0)

    for copy in loads[5:]:
        copy.wait()

    def guard(ref, ends):
        for field in range(2):
            base = FBASE + field * FSPAN
            if "top" in ends:
                ref[pl.ds(base, ROWS)] = ref[pl.ds(base + ROWS, ROWS)]
            if "low" in ends:
                ref[pl.ds(base + (ZO + 1) * ROWS, ROWS)] = ref[pl.ds(base + ZO * ROWS, ROWS)]

    def put_pack(r, group, field, chunk, t, acc):
        first, lane = packed_place(group, field, chunk)
        rows = pl.ds(first + t * SUB, SUB)
        shifted = roll(acc, lane, 1)
        mine = (lane8 >= lane) & (lane8 < lane + 16)
        opack[r, rows] = jnp.where(mine, shifted, opack[r, rows])

    def put_rows(r, ref, group, field, chunk):
        base = FBASE + field * FSPAN + ROWS + chunk * (CHUNK * ROWS)
        start = level_row(group, field, chunk)
        rows = pl.ds(start if isinstance(start, int) else pl.multiple_of(start, SUB), SUB)
        orow[r, 0, rows] = ref[pl.ds(base, SUB, stride=ROWS)]
        orow[r, 1, rows] = ref[pl.ds(base + ROWS - 1, SUB, stride=ROWS)]

    def first_edges(group, chunk):
        for field in range(2):
            base = FBASE + field * FSPAN + ROWS + chunk * (CHUNK * ROWS)
            if not isinstance(base, int):
                base = pl.multiple_of(base, SUB)
            for t in range(TILES):
                acc = jnp.zeros((SUB, LANES), F32)
                for j in range(CHUNK):
                    value = fa[pl.ds(base + j * ROWS + t * SUB, SUB)]
                    acc = jnp.where(pair8 == j, roll(value, 2 * j + 1, 1), acc)
                put_pack(0, group, field, chunk, t, acc)
            put_rows(0, fa, group, field, chunk)

    def over_chunks(group, step):
        def body(chunk, carry):
            step(group, chunk)
            return carry

        if group == "top":
            step(group, 0)
        else:
            lax.fori_loop(*GROUPS[group][0], body, 0)

    def send_ocean(r, group):
        n = ORDER.index(group)
        cols, rows = (pl.ds(*GROUPS[group][m]) for m in (1, 2))
        return [
            send(orow.at[r, 0, rows], rrow.at[r, 1, rows], o_send.at[r, n, 0], o_recv.at[r, n, 0], north),
            send(orow.at[r, 1, rows], rrow.at[r, 0, rows], o_send.at[r, n, 1], o_recv.at[r, n, 1], south),
            send(opack.at[r, cols], rpack.at[r, 1, cols], o_send.at[r, n, 2], o_recv.at[r, n, 2], west),
            send(opack.at[r, cols], rpack.at[r, 0, cols], o_send.at[r, n, 3], o_recv.at[r, n, 3], east),
        ]

    ocean = {}
    guard(fa, ("top", "low"))
    wet = omask[...].astype(F32)
    diffusion = diff[...]
    orow[0, 0, pl.ds(STATIC_ROW, 1)] = diffusion[0:1]
    orow[0, 0, pl.ds(STATIC_ROW + 1, 1)] = wet[0:1]
    orow[0, 1, pl.ds(STATIC_ROW, 1)] = diffusion[ROWS - 1 :]
    orow[0, 1, pl.ds(STATIC_ROW + 1, 1)] = wet[ROWS - 1 :]
    for t in range(TILES):
        rows = pl.ds(4 * ROWS + t * SUB, SUB)
        acc = opack[0, rows]
        acc = jnp.where(pair8 == 32, roll(diffusion[t * SUB : (t + 1) * SUB], 65, 1), acc)
        acc = jnp.where(pair8 == 33, roll(wet[t * SUB : (t + 1) * SUB], 67, 1), acc)
        opack[0, rows] = acc
    for group in ("low", "top", "mid"):
        over_chunks(group, first_edges)
        ocean[group] = send_ocean(0, group)

    for copy in weights:
        copy.wait_recv()
    row_mu[...] = rwmsg[pl.ds(0, 16)] * has_n
    even = (lane8 & 1) == 0
    for t in range(TILES):
        col_mu[pl.ds(SUB + t * SUB, SUB)] = jnp.where(even, rwpack[pl.ds(t * SUB, SUB)] * has_w, 0.0)
    even1 = (iota((1, LANES), 1) & 1) == 0
    col_mu[pl.ds(SUB - 1, 1)] = jnp.where(even1, rwcorner[pl.ds(0, 1)] * (has_w * has_n), 0.0)

    def put_ice_edges(r, ref):
        for c in range(2):
            for edge in range(2):
                start = c * NODES * VSPAN + edge * (ROWS - 1)
                imsg[r, edge, pl.ds(c * 16, 16)] = ref[pl.ds(start, 16, stride=VSPAN)]
        imsg[r, 0, pl.ds(32, 1)] = ipack[r, pl.ds(0, 1)]
        imsg[r, 1, pl.ds(32, 1)] = ipack[r, pl.ds(ROWS - 1, 1)]

    def send_ice(r):
        copies = [
            send(imsg.at[r, 0], rmsg.at[r, 1], i_send.at[r, 0], i_recv.at[r, 0], north),
            send(imsg.at[r, 1], rmsg.at[r, 0], i_send.at[r, 1], i_recv.at[r, 1], south),
            send(ipack.at[r], rside.at[r, 1], i_send.at[r, 2], i_recv.at[r, 2], west),
            send(ipack.at[r], rside.at[r, 0], i_send.at[r, 3], i_recv.at[r, 3], east),
        ]
        for n, device in enumerate(corners):
            src = imsg.at[r, n // 2, pl.ds(32, 8)]
            copies.append(send(src, rcorner.at[r, 3 - n], i_send.at[r, 4 + n], i_recv.at[r, 4 + n], device))
        return copies

    for t in range(TILES):
        cols = col_mu[pl.ds(SUB + t * SUB, SUB)] + col_mu[pl.ds(SUB - 1 + t * SUB, SUB)]
        cols = cols + roll(cols, 2, 1)
        acc = jnp.zeros((SUB, LANES), F32)
        below = None
        for k in range(NODES):
            layer = None
            if k < CELLS:
                start = SUB + k * ROWS + t * SUB
                up = mu[pl.ds(start - 1, SUB)]
                if t == 0:
                    up = jnp.where(sub8 == 0, row_mu[pl.ds(k, 1)], up)
                layer = mu[pl.ds(start, SUB)] + up
            total = layer if below is None else (below if layer is None else layer + below)
            below = layer
            left = jnp.where(lane8 == 0, roll(cols, -2 * k, 1), roll(total, 1, 1))
            diagonal = DIAGONAL * (total + left) + shift_term
            if k == 0:
                diagonal = diagonal + drag[pl.ds(t * SUB, SUB)]
            factor = relax_weight / diagonal
            rdiag[pl.ds(k * ROWS + t * SUB, SUB)] = factor
            for c in range(2):
                value = force[pl.ds((c * NODES + k) * ROWS + t * SUB, SUB)] * factor
                va[pl.ds((c * NODES + k) * VSPAN + t * SUB, SUB)] = value
                acc = jnp.where(pair8 == 32 * c + k, roll(value, 64 * c + 2 * k + 1, 1), acc)
        ipack[0, pl.ds(t * SUB, SUB)] = acc
    put_ice_edges(0, va)
    ice = send_ice(0)

    def take_ocean(r, group):
        for copy in ocean[group]:
            copy.wait_recv()
        first, count = GROUPS[group][1]
        for n in range(count // SUB):
            rows = pl.ds(first + n * SUB, SUB)
            from_e = roll(rpack[r, 1, rows], -1, 1)
            from_w = roll(rpack[r, 0, rows], 1, 1)
            merged[rows] = jnp.where(even, from_e, from_w)

    coupling = scatter_second(0, coupling)
    take_ocean(0, "top")
    for t in range(TILES):
        rows = slice(t * SUB, (t + 1) * SUB)
        d, w = diffusion[rows], wet[rows]

        def around(mine, plane, n):
            whole = plane
            up = roll(mine, 1, 0)
            above = rrow[0, 0, pl.ds(STATIC_ROW + n, 1)] if t == 0 else whole[t * SUB - 1 : t * SUB]
            up = jnp.where(sub8 == 0, above, up)
            down = roll(mine, -1, 0)
            below = rrow[0, 1, pl.ds(STATIC_ROW + n, 1)] if t == TILES - 1 else whole[(t + 1) * SUB : (t + 1) * SUB + 1]
            down = jnp.where(sub8 == SUB - 1, below, down)
            edge = roll(merged[pl.ds(4 * ROWS + t * SUB, SUB)], 127 - 64 - 2 * n, 1)
            left = jnp.where(lane8 == 0, edge, roll(mine, 1, 1))
            right = jnp.where(lane8 == LANES - 1, edge, roll(mine, -1, 1))
            return up, down, left, right

        near_d = around(d, diffusion, 0)
        up_w, down_w, left_w, right_w = around(w, wet, 1)
        if t == 0:
            up_w = jnp.where(sub8 == 0, up_w * has_n, up_w)
        if t == TILES - 1:
            down_w = jnp.where(sub8 == SUB - 1, down_w * has_s, down_w)
        left_w = jnp.where(lane8 == 0, left_w * has_w, left_w)
        right_w = jnp.where(lane8 == LANES - 1, right_w * has_e, right_w)
        total = 2.0 * vert_mix * w
        for n, (near, near_w) in enumerate(zip(near_d, (up_w, down_w, left_w, right_w))):
            face = 0.5 * (d + near) * w * near_w
            coef[pl.ds((n + 1) * ROWS + t * SUB, SUB)] = face
            total = total + face
        coef[pl.ds(t * SUB, SUB)] = 1.0 - total
        coef[pl.ds(5 * ROWS + t * SUB, SUB)] = vert_mix * w

    def melt_of(temp_top, salt_top, t):
        freezing = freeze_slope * (salt_ref + salt_top) + freeze_base - freeze_depth * draft[pl.ds(t * SUB, SUB)]
        return heat_gamma * (temp_top - freezing) * (10.0 * coef[pl.ds(5 * ROWS + t * SUB, SUB)])

    def ocean_chunk(s, group, chunk, src, dst):
        for field in range(2):
            base = FBASE + field * FSPAN + ROWS + chunk * (CHUNK * ROWS)
            if not isinstance(base, int):
                base = pl.multiple_of(base, SUB)
            values = src[pl.ds(base, CHUNK * ROWS)]
            high = values.astype(jnp.bfloat16)
            rest = (values - high.astype(F32)).astype(jnp.bfloat16)
            both = jnp.concatenate([high, rest], axis=1)
            sides[pl.ds(field * CHUNK * ROWS, CHUNK * ROWS)] = jnp.dot(
                both, shifts[...], preferred_element_type=F32
            )
        for t in range(TILES):
            cs = [coef[pl.ds(n * ROWS + t * SUB, SUB)] for n in range(6)]
            first = []
            for field in range(2):
                base = FBASE + field * FSPAN + ROWS + chunk * (CHUNK * ROWS) + t * SUB
                if not isinstance(base, int):
                    base = pl.multiple_of(base, SUB)
                vec, lane = packed_place(group, field, chunk)
                packed = merged[pl.ds(vec + t * SUB, SUB)]
                packed = roll(packed, -lane if isinstance(lane, int) else lax.rem(LANES - lane, LANES), 1)
                acc = jnp.zeros((SUB, LANES), F32)
                prev = src[pl.ds(base - ROWS, SUB)]
                cur = src[pl.ds(base, SUB)]
                news = []
                for j in range(CHUNK):
                    row = base + j * ROWS
                    nxt = src[pl.ds(row + ROWS, SUB)]
                    up = src[pl.ds(row - 1, SUB)]
                    down = src[pl.ds(row + 1, SUB)]
                    level = level_row(group, field, chunk) + j
                    if t == 0:
                        up = jnp.where(sub8 == 0, rrow[s, 0, pl.ds(level, 1)], up)
                    if t == TILES - 1:
                        down = jnp.where(sub8 == SUB - 1, rrow[s, 1, pl.ds(level, 1)], down)
                    edge = roll(packed, 127 - 2 * j, 1)
                    beside = pl.ds(field * CHUNK * ROWS + j * ROWS + t * SUB, SUB)
                    left = jnp.where(lane8 == 0, edge, sides[beside, :LANES])
                    right = jnp.where(lane8 == LANES - 1, edge, sides[beside, LANES:])
                    new = (
                        cs[0] * cur
                        + (cs[1] * up + cs[2] * down)
                        + (cs[3] * left + cs[4] * right)
                        + cs[5] * (prev + nxt)
                    )
                    news.append(new)
                    prev, cur = cur, nxt
                first.append(news)
            if group == "top":
                temp_top, salt_top = first[0][0], first[1][0]
                rate = melt_of(temp_top, salt_top, t)
                first[0][0] = temp_top - heat_factor * rate
                first[1][0] = salt_top - salt_factor * rate * (salt_ref + salt_top) / salt_ref
            for field in range(2):
                acc = jnp.zeros((SUB, LANES), F32)
                for j in range(CHUNK):
                    new = first[field][j]
                    if s < STEPS - 1:
                        row = FBASE + field * FSPAN + ROWS + chunk * (CHUNK * ROWS) + t * SUB + j * ROWS
                        if not isinstance(row, int):
                            row = pl.multiple_of(row, SUB)
                        dst[pl.ds(row, SUB)] = new
                        acc = jnp.where(pair8 == j, roll(new, 2 * j + 1, 1), acc)
                    else:
                        row = chunk * (CHUNK * ROWS) + j * ROWS + t * SUB
                        if not isinstance(row, int):
                            row = pl.multiple_of(row, SUB)
                        dst[field][pl.ds(row, SUB)] = new
                if s < STEPS - 1:
                    put_pack(s + 1, group, field, chunk, t, acc)
        if s < STEPS - 1:
            for field in range(2):
                put_rows(s + 1, dst, group, field, chunk)

    def ocean_part(s, group, src, dst, taken=False):
        if not taken:
            take_ocean(s, group)
        over_chunks(group, lambda part, chunk: ocean_chunk(s, part, chunk, src, dst))
        if s < STEPS - 1:
            guard(dst, (group,))
            ocean[group] = send_ocean(s + 1, group)

    def ice_sweep(r, copies, src, dst):
        last = r == SWEEPS - 1
        for copy in copies:
            copy.wait_recv()
        for c in range(2):
            for k in range(NODES):
                src[pl.ds((c * NODES + k) * VSPAN + ROWS, 1)] = rmsg[r, 1, pl.ds(c * 16 + k, 1)] * has_s
        for t in range(TILES):
            rows = pl.ds(t * SUB, SUB)
            edge_e[rows] = rside[r, 1, rows] * has_e
            col_lo[pl.ds(SUB + t * SUB, SUB)] = rside[r, 0, rows] * has_w
            col_hi[pl.ds(SUB + t * SUB, SUB)] = roll(ipack[r, rows], -1, 1)
        edge_e[pl.ds(ROWS, 1)] = rcorner[r, 3, pl.ds(0, 1)] * (has_e * has_s)
        col_lo[pl.ds(SUB - 1, 1)] = rcorner[r, 0, pl.ds(0, 1)] * (has_w * has_n)
        col_lo[pl.ds(SUB + ROWS, 1)] = rcorner[r, 2, pl.ds(0, 1)] * (has_w * has_s)
        col_hi[pl.ds(SUB - 1, 1)] = roll(rmsg[r, 0, pl.ds(32, 1)] * has_n, -1, 1)
        col_hi[pl.ds(SUB + ROWS, 1)] = roll(rmsg[r, 1, pl.ds(32, 1)] * has_s, -1, 1)
        for t in range(TILES + 1):
            start = SUB - 1 + t * SUB
            if t == TILES:
                start = ROWS
            lo0, lo1 = col_lo[pl.ds(start, SUB)], col_lo[pl.ds(start + 1, SUB)]
            hi0, hi1 = col_hi[pl.ds(start, SUB)], col_hi[pl.ds(start + 1, SUB)]
            planes = []
            for c in range(2):
                parts = [roll(value, 64 * c, 1) for value in (lo0, hi0, lo1, hi1)]
                low = plane_sums(*parts)
                planes += [low, {key: roll(value, -2, 1) for key, value in low.items()}]
            fu, fv = element_forces(*planes, col_mu[pl.ds(start, SUB)])
            for c, f in enumerate((fu, fv)):
                low, high = lower_part(f), upper_part(f)
                node = {key: low[key] + roll(high[key], 2, 1) for key in low}
                behind = {x: node[x + "s"] + node[x + "d"] for x in "sd"}
                col_q[2 * c, pl.ds(start - SUB + 1, SUB)] = behind["s"] - behind["d"]
                col_q[2 * c + 1, pl.ds(start - SUB + 1, SUB)] = behind["s"] + behind["d"]
        lane16, sub16 = iota((16, LANES), 1), iota((16, LANES), 0)

        def upright(row, offset):
            chosen = jnp.where(lane16 == 2 * sub16 + offset, row, 0.0)
            return jnp.sum(chosen, axis=1, keepdims=True)

        planes = []
        for c in range(2):
            lo = rmsg[r, 0, pl.ds(c * 16, 16)]
            hi = imsg[r, 0, pl.ds(c * 16, 16)]
            lo_end = upright(rcorner[r, 1, pl.ds(0, 1)] * (has_e * has_n), 64 * c + 1)
            hi_end = upright(edge_e[pl.ds(0, 1)], 64 * c + 1)
            lo_right = jnp.where(lane16 == LANES - 1, lo_end, roll(lo, -1, 1))
            hi_right = jnp.where(lane16 == LANES - 1, hi_end, roll(hi, -1, 1))
            low = plane_sums(lo, lo_right, hi, hi_right)
            planes += [low, {key: roll(value, -1, 0) for key, value in low.items()}]
        fu, fv = element_forces(*planes, row_mu[...])
        for c, f in enumerate((fu, fv)):
            low, high = lower_part(f), upper_part(f)
            node = {key: low[key] + roll(high[key], 1, 0) for key in low}
            for n, sign in enumerate((-1.0, 1.0)):
                parts = [node[x + "s"] + sign * node[x + "d"] for x in "sd"]
                row_q[pl.ds((2 * n + c) * 16, 16)] = parts[0] + parts[1]
        for c in range(2):
            for k in range(NODES):
                shift = 127 - (64 * c + 2 * k + 1)
                for t in range(TILES + 1):
                    rows = pl.ds((c * NODES + k) * VSPAN + t * SUB, SUB)
                    edge = roll(edge_e[pl.ds(t * SUB, SUB)], shift, 1)
                    vright[rows] = jnp.where(lane8 == LANES - 1, edge, roll(src[rows], -1, 1))
        pass_down = {}
        for t in range(TILES):
            below, carried = None, None
            for k in range(NODES + 1):
                planes = None
                if k < NODES:
                    planes = []
                    for c in range(2):
                        start = (c * NODES + k) * VSPAN + t * SUB
                        lo, hi = pl.ds(start, SUB), pl.ds(start + 1, SUB)
                        planes.append(plane_sums(src[lo], vright[lo], src[hi], vright[hi]))
                if k >= 1:
                    level = k - 1
                    nodes, ups = [None, None], [None, None]
                    if level < CELLS:
                        weight = mu[pl.ds(SUB + level * ROWS + t * SUB, SUB)]
                        forces = element_forces(below[0], planes[0], below[1], planes[1], weight)
                        for c in range(2):
                            nodes[c], ups[c] = lower_part(forces[c]), upper_part(forces[c])
                            if carried is not None:
                                nodes[c] = {key: nodes[c][key] + carried[c][key] for key in nodes[c]}
                    else:
                        nodes = carried
                    carried = ups
                    for c in range(2):
                        node = nodes[c]
                        row = pl.ds((c * NODES + level) * ROWS + t * SUB, SUB)
                        for n, (sign, place) in enumerate(((-1.0, low_y), (1.0, high_y))):
                            parts = [node[x + "s"] + sign * node[x + "d"] for x in "sd"]
                            down = roll(parts[0] + parts[1], 1, 0)
                            if t == 0:
                                over = row_q[pl.ds((2 * n + c) * 16 + level, 1)]
                            else:
                                over = pass_down[n, c, level]
                            pass_down[n, c, level] = down[0:1]
                            place[row] = parts[0] - parts[1] + jnp.where(sub8 == 0, over, down)
                below = planes
        for c in range(2):
            for t in range(TILES):
                strip = col_q[2 * c, pl.ds(1 + t * SUB, SUB)] + col_q[2 * c + 1, pl.ds(t * SUB, SUB)]
                for level in range(NODES):
                    at_row = (c * NODES + level) * ROWS + t * SUB
                    row = pl.ds(at_row, SUB)
                    before = jnp.where(lane8 == 0, roll(strip, -2 * level, 1), roll(high_y[row], 1, 1))
                    value = src[pl.ds((c * NODES + level) * VSPAN + t * SUB, SUB)]
                    extra = shift_term
                    if level == 0:
                        extra = shift_term + drag[pl.ds(t * SUB, SUB)]
                    applied = low_y[row] + before + extra * value
                    value = value + (force[row] - applied) * rdiag[pl.ds(level * ROWS + t * SUB, SUB)]
                    if last:
                        dst[row] = value
                    else:
                        dst[pl.ds((c * NODES + level) * VSPAN + t * SUB, SUB)] = value
        if last:
            return None
        for t in range(TILES):
            acc = jnp.zeros((SUB, LANES), F32)
            for c in range(2):
                for level in range(NODES):
                    value = dst[pl.ds((c * NODES + level) * VSPAN + t * SUB, SUB)]
                    acc = jnp.where(pair8 == 32 * c + level, roll(value, 64 * c + 2 * level + 1, 1), acc)
            ipack[r + 1, pl.ds(t * SUB, SUB)] = acc
        put_ice_edges(r + 1, dst)
        return send_ice(r + 1)

    ocean_part(0, "low", fa, fb)
    ocean_part(0, "mid", fa, fb)
    for copy in coupling:
        copy.wait_recv()
    draft[...] = pick(by_device(from_col), got[0])
    ocean_part(0, "top", fa, fb, True)
    ice = ice_sweep(0, ice, va, vb)
    ocean_part(1, "low", fb, fa)
    ocean_part(1, "top", fb, fa)
    ocean_part(1, "mid", fb, fa)
    ice = ice_sweep(1, ice, vb, va)
    ocean_part(2, "top", fa, fb)
    ocean_part(2, "low", fa, fb)
    ocean_part(2, "mid", fa, fb)
    ocean_part(3, "top", fb, (temp_out, salt_out))
    for t in range(TILES):
        rows = pl.ds(t * SUB, SUB)
        pad_in[rows] = melt_of(temp_out[rows], salt_out[rows], t)
    tbl[1] = pick(by_slot(from_row), pad_in[...])
    coupling = scatter_first(1)
    ice_sweep(2, ice, va, vel_out)
    ocean_part(3, "low", fb, (temp_out, salt_out))
    coupling = scatter_second(1, coupling)
    ocean_part(3, "mid", fb, (temp_out, salt_out))
    for copy in coupling:
        copy.wait_recv()
    melt = pick(by_device(to_col), got[1])
    thick_out[...] = thick[...] - melt_factor * melt * wet_ice
    for copy in sends:
        copy.wait_send()


def write_out(*refs):
    srcs, dsts, sem = refs[:4], refs[4:8], refs[8]
    copies = [pltpu.make_async_copy(src, dst, sem.at[n]) for n, (src, dst) in enumerate(zip(srcs, dsts))]
    for copy in copies:
        copy.start()
    for copy in copies:
        copy.wait()


def per_device(
    ice_force, ice_visc, ice_drag, ice_mask, ice_thick, ice_target,
    ocean_temp, ocean_salt, ocean_diff, ocean_mask, ocean_source,
):
    def flat(array):
        return pltpu.with_memory_space_constraint(array.reshape(-1, LANES), pltpu.HBM)

    def held(array):
        return pltpu.with_memory_space_constraint(array, pltpu.HBM)

    vmem = pl.BlockSpec(memory_space=pltpu.VMEM)
    hbm = pl.BlockSpec(memory_space=pltpu.HBM)
    dma = pltpu.SemaphoreType.DMA

    def buf(*shape):
        return pltpu.VMEM((*shape, LANES), F32)

    nx, ny = lax.axis_size("gx"), lax.axis_size("gy")
    whole = pltpu.VMEM((ROWS, LANES), jnp.int32)
    ids = pltpu.SMEM((ROWS,), jnp.int32)
    scratch = [
        buf(2 * NODES * ROWS), buf(CELLS * ROWS), buf(ROWS), whole, buf(ROWS), ids, buf(ROWS), whole, ids,
        buf(FROWS), buf(FROWS), buf(6 * ROWS), buf(STEPS, PACK_ROWS), buf(STEPS, 2, 2 * ZO + SUB),
        buf(STEPS, 2, PACK_ROWS), buf(STEPS, 2, 2 * ZO + SUB), buf(PACK_ROWS),
        buf(VROWS), buf(VROWS), buf(2 * SUB + CELLS * ROWS), buf(NODES * ROWS),
        buf(SWEEPS, ROWS), buf(SWEEPS, 2, 40), buf(SWEEPS, 2, ROWS), buf(SWEEPS, 2, 40), buf(SWEEPS, 4, SUB),
        buf(VROWS), buf(2 * NODES * ROWS), buf(2 * NODES * ROWS),
        pltpu.VMEM((2 * LANES, 2 * LANES), jnp.bfloat16), pltpu.VMEM((2 * CHUNK * ROWS, 2 * LANES), F32),
        buf(ROWS + SUB), buf(ROWS + 2 * SUB), buf(ROWS + 2 * SUB), buf(ROWS + 2 * SUB),
        buf(4, ROWS + SUB), buf(64), buf(16),
        buf(ROWS), buf(24), buf(ROWS), buf(24), buf(SUB),
        buf(LANES), buf(ROWS), buf(2, LANES), buf(2, LANES), buf(2, LANES), buf(2, LANES),
        dma((11,)), dma((STEPS, 3, 4)), dma((STEPS, 3, 4)), dma((SWEEPS, 8)), dma((SWEEPS, 8)),
        dma((3,)), dma((3,)), dma((2, ny)), dma((2, ny)), dma((2, nx)), dma((2, nx)),
    ]
    shapes = [
        jax.ShapeDtypeStruct((2 * NODES * ROWS, LANES), F32),
        jax.ShapeDtypeStruct((ROWS, LANES), F32),
        jax.ShapeDtypeStruct((ZO * ROWS, LANES), F32),
        jax.ShapeDtypeStruct((ZO * ROWS, LANES), F32),
    ]
    results = pl.pallas_call(
        kernel,
        out_shape=shapes,
        in_specs=[hbm] * 11,
        out_specs=[vmem] * 4,
        scratch_shapes=scratch,
        compiler_params=pltpu.CompilerParams(
            collective_id=0, has_side_effects=True, vmem_limit_bytes=40 * 1024 * 1024
        ),
    )(
        flat(ice_force), flat(ice_visc), held(ice_drag), held(ice_mask), held(ice_thick), held(ice_target),
        flat(ocean_temp), flat(ocean_salt), held(ocean_diff), held(ocean_mask), held(ocean_source),
    )
    velocity, thickness, temp, salt = pl.pallas_call(
        write_out,
        out_shape=shapes,
        in_specs=[pl.BlockSpec(memory_space=pl.ANY)] * 4,
        out_specs=[pl.BlockSpec(memory_space=pl.ANY)] * 4,
        scratch_shapes=[dma((4,))],
        compiler_params=pltpu.CompilerParams(vmem_limit_bytes=1024 * 1024),
    )(*results)
    return (
        velocity.reshape(ice_force.shape),
        thickness,
        temp.reshape(ocean_temp.shape),
        salt.reshape(ocean_salt.shape),
    )


def solution(mesh):
    in_specs = (
        P(None, None, "gx", "gy"),
        P(None, "gx", "gy"),
        P("gx", "gy"),
        P("gx", "gy"),
        P("gx", "gy"),
        P(("gx", "gy")),
        P(None, "gx", "gy"),
        P(None, "gx", "gy"),
        P("gx", "gy"),
        P("gx", "gy"),
        P(("gx", "gy")),
    )
    out_specs = (P(None, None, "gx", "gy"), P("gx", "gy"), P(None, "gx", "gy"), P(None, "gx", "gy"))
    return jax.shard_map(per_device, mesh=mesh, in_specs=in_specs, out_specs=out_specs, check_vma=False)
```

```python
import jax
import jax.numpy as jnp
from jax import lax
from jax.experimental import pallas as pl
from jax.experimental.pallas import tpu as pltpu
from jax.sharding import PartitionSpec as P

MESH = pl.DeviceIdType.MESH
F32 = jnp.float32

LANES = 128
SUB = 8
ROWS = 32
TILES = ROWS // SUB
ZO = 80
NODES = 11
CELLS = 10
STEPS = 4
SWEEPS = 3
CHUNK = 8
FBASE = 8
FSPAN = (ZO + 2) * ROWS
FROWS = 2 * FBASE + 2 * FSPAN
VSPAN = 40
VROWS = (NODES + 16) * VSPAN

relax_weight = 0.6
shift_term = 0.2
vert_mix = 0.1
heat_gamma = 0.5
heat_factor = 0.05
salt_factor = 0.05
salt_ref = 34.5
freeze_slope = -0.0573
freeze_base = 0.0832
freeze_depth = 0.761
melt_factor = 0.2
draft_ratio = 0.89

MASS = {"s": 1.0 / 4.0, "d": 1.0 / 12.0}


def same_weight(z, x, y, along):
    wx, wy = (4.0, 1.0) if along == 0 else (1.0, 4.0)
    total = 0.0
    if x == "d":
        total += wx * MASS[y] * MASS[z]
    if y == "d":
        total += wy * MASS[x] * MASS[z]
    if z == "d":
        total += MASS[x] * MASS[y]
    return total


DIAGONAL = 2.0 / 3.0


def iota(shape, axis):
    return lax.broadcasted_iota(jnp.int32, shape, axis)


def roll(value, shift, axis):
    size = value.shape[axis]
    if isinstance(shift, int):
        shift = shift % size
        if shift == 0:
            return value
    return pltpu.roll(value, shift, axis)


def plane_sums(lo, lo_right, hi, hi_right):
    ls, ld = lo + lo_right, lo_right - lo
    hs, hd = hi + hi_right, hi_right - hi
    return {"ss": ls + hs, "sd": ld + hd, "ds": hs - ls, "dd": hd - ld}


def element_forces(u_low, u_high, v_low, v_high, mu):
    u, v = {}, {}
    for xy in ("ss", "sd", "ds", "dd"):
        if xy != "ss":
            u["s" + xy] = u_low[xy] + u_high[xy]
            v["s" + xy] = v_low[xy] + v_high[xy]
        u["d" + xy] = u_high[xy] - u_low[xy]
        v["d" + xy] = v_high[xy] - v_low[xy]
    scaled = {}

    def times_mu(factor):
        if factor not in scaled:
            scaled[factor] = mu * factor
        return scaled[factor]

    fu, fv = {}, {}
    for key in u:
        z, xy = key[0], key[1:]
        for along, mine, other, out in ((0, u, v, fu), (1, v, u, fv)):
            own = same_weight(z, xy[0], xy[1], along)
            if xy in ("ds", "sd"):
                first = xy == "ds"
                double = first if along == 0 else not first
                cross = MASS[z] * (2.0 if double else 1.0) / 4.0
                swapped = z + ("sd" if first else "ds")
                out[key] = times_mu(own) * (mine[key] + (cross / own) * other[swapped])
            else:
                out[key] = times_mu(own) * mine[key]
    return fu, fv


def lower_part(f):
    out = {xy: f["s" + xy] - f["d" + xy] for xy in ("sd", "ds", "dd")}
    out["ss"] = -f["dss"]
    return out


def upper_part(f):
    out = {xy: f["s" + xy] + f["d" + xy] for xy in ("sd", "ds", "dd")}
    out["ss"] = f["dss"]
    return out


GROUPS = {
    "top": ((0, 1), (128, 32), (144, 24), (144, 8)),
    "mid": ((1, 5), (0, 64), (0, 64), (0, 32)),
    "low": ((5, 10), (64, 64), (64, 80), (64, 40)),
}
ORDER = ("top", "mid", "low")
PACK_ROWS = 160
STATIC_ROW = 160


def packed_place(group, field, chunk):
    first = GROUPS[group][0][0]
    if group == "top":
        return 4 * ROWS, 16 * field
    return (field + (2 if group == "low" else 0)) * ROWS, (chunk - first) * 16


def level_row(group, field, chunk):
    start, span = GROUPS[group][3]
    return start + field * span + (chunk - GROUPS[group][0][0]) * CHUNK


def kernel(
    force_in, visc_in, drag_in, imask_in, thick_in, target_in, temp_in, salt_in, diff_in, omask_in, source_in,
    vel_out, thick_out, temp_out, salt_out,
    force, visc, drag, imask, thick, target, diff, omask, source,
    fa, fb, coef, opack, orow, rpack, rrow, merged,
    va, vb, mu, rdiag, ipack, imsg, rside, rmsg, rcorner,
    vright, low_y, high_y, shifts, sides,
    edge_e, col_lo, col_hi, col_mu, col_q, row_q, row_mu,
    wpack, wmsg, rwpack, rwmsg, rwcorner,
    pad_in, draft, tbl, mid, fwd, got,
    in_sem, o_send, o_recv, i_send, i_recv, w_send, w_recv, a_send, a_recv, b_send, b_recv,
):
    gx, gy = lax.axis_index("gx"), lax.axis_index("gy")
    nx, ny = lax.axis_size("gx"), lax.axis_size("gy")

    def at(dx, dy):
        return (lax.rem(gx + (dx + nx), nx), lax.rem(gy + (dy + ny), ny))

    north, south, west, east = at(-1, 0), at(1, 0), at(0, -1), at(0, 1)
    corners = (at(-1, -1), at(-1, 1), at(1, -1), at(1, 1))

    lane8 = iota((SUB, LANES), 1)
    sub8 = iota((SUB, LANES), 0)
    pair8 = lane8 // 2

    pairs = [(visc_in, visc), (imask_in, imask), (thick_in, thick), (target_in, target), (source_in, source)]
    for field, ref in ((0, temp_in), (1, salt_in)):
        start = FBASE + field * FSPAN + ROWS
        pairs.append((ref, fa.at[pl.ds(start, ZO * ROWS)]))
    pairs += [(diff_in, diff), (omask_in, omask), (drag_in, drag), (force_in, force)]
    loads = [pltpu.make_async_copy(src, dst, in_sem.at[n]) for n, (src, dst) in enumerate(pairs)]
    for copy in loads:
        copy.start()
    barrier = pltpu.get_barrier_semaphore()
    peers = [north, south, *corners]
    peers += [at(0, q) for q in range(1, ny)] + [at(p, 0) for p in range(2, nx - 1)]
    for peer in peers:
        pl.semaphore_signal(barrier, inc=1, device_id=peer, device_id_type=MESH)

    has_n = (gx > 0).astype(F32)
    has_s = (gx < nx - 1).astype(F32)
    has_w = (gy > 0).astype(F32)
    has_e = (gy < ny - 1).astype(F32)

    sends = []

    def send(src, dst, ssem, rsem, device):
        copy = pltpu.make_async_remote_copy(
            src_ref=src, dst_ref=dst, send_sem=ssem, recv_sem=rsem, device_id=device, device_id_type=MESH
        )
        copy.start()
        sends.append(copy)
        return copy

    wmsg[...] = jnp.zeros_like(wmsg)
    va[...] = jnp.zeros_like(va)
    vb[...] = jnp.zeros_like(vb)
    edge_e[...] = jnp.zeros_like(edge_e)
    col_lo[...] = jnp.zeros_like(col_lo)
    col_hi[...] = jnp.zeros_like(col_hi)
    col_mu[...] = jnp.zeros_like(col_mu)
    imsg[...] = jnp.zeros_like(imsg)
    pad_in[...] = jnp.zeros_like(pad_in)
    opack[...] = jnp.zeros_like(opack)
    orow[...] = jnp.zeros_like(orow)
    row_no, col_no = iota((2 * LANES, 2 * LANES), 0) % LANES, iota((2 * LANES, 2 * LANES), 1)
    before = (row_no == col_no - 1) & (col_no < LANES)
    after = (row_no == col_no + 1 - LANES) & (col_no >= LANES)
    shifts[...] = (before | after).astype(F32).astype(jnp.bfloat16)
    for copy in loads[:5]:
        copy.wait()
    wet_ice = imask[...].astype(F32)
    for t in range(TILES):
        acc = jnp.zeros((SUB, LANES), F32)
        wet_t = wet_ice[t * SUB : (t + 1) * SUB]
        for k in range(CELLS):
            rows = pl.ds(k * ROWS + t * SUB, SUB)
            weight = visc[rows] * wet_t
            mu[pl.ds(SUB + k * ROWS + t * SUB, SUB)] = weight
            acc = jnp.where(pair8 == k, roll(weight, 2 * k + 1, 1), acc)
        wpack[pl.ds(t * SUB, SUB)] = acc
    wmsg[pl.ds(0, 8)] = mu[pl.ds(SUB + ROWS - 1, 8, stride=ROWS)]
    wmsg[pl.ds(8, 2)] = mu[pl.ds(SUB + 8 * ROWS + ROWS - 1, 2, stride=ROWS)]
    wmsg[pl.ds(16, 1)] = wpack[pl.ds(ROWS - 1, 1)]

    lane1 = iota((SUB, LANES), 1)
    to_row = jnp.full((SUB, LANES), -1, jnp.int32)
    from_row = jnp.full((SUB, LANES), -1, jnp.int32)
    to_col = [jnp.full((SUB, LANES), -1, jnp.int32) for _ in range(TILES)]
    from_col = [jnp.full((SUB, LANES), -1, jnp.int32) for _ in range(TILES)]
    for i in range(ROWS):
        to_row = jnp.where(lane1 == i, target[i], to_row)
        from_row = jnp.where(lane1 == i, source[i], from_row)
        to_col[i // SUB] = jnp.where(sub8 == i % SUB, target[i], to_col[i // SUB])
        from_col[i // SUB] = jnp.where(sub8 == i % SUB, source[i], from_col[i // SUB])

    def slot_of(ids):
        device = ids >> 5
        return jnp.where(ids >= 0, (device & (ny - 1)) * nx + (device >> 4), -1)

    def by_slot(row):
        slots = slot_of(row)
        return jnp.concatenate(
            [(sub8 + n * SUB == slots).astype(F32) for n in range(LANES // SUB)], axis=0
        )

    def by_device(cols):
        return jnp.concatenate(
            [((lane8 == (ids >> 5)) & (ids >= 0)).astype(F32) for ids in cols], axis=0
        )

    def pick(one_hot, values):
        return jnp.dot(one_hot, values, precision=lax.Precision.HIGHEST, preferred_element_type=F32)

    pad_in[pl.ds(0, ROWS)] = draft_ratio * thick[...]
    tbl[0] = pick(by_slot(to_row), pad_in[...])

    pl.semaphore_wait(barrier, len(peers))

    def scatter_first(n):
        copies = []
        for q in range(1, ny):
            peer = at(0, q)
            copies.append(
                send(
                    tbl.at[n, pl.ds(pl.multiple_of(peer[1] * nx, nx), nx)],
                    mid.at[n, pl.ds(pl.multiple_of(gy * nx, nx), nx)],
                    a_send.at[n, q], a_recv.at[n, q], peer,
                )
            )
        own = pl.ds(pl.multiple_of(gy * nx, nx), nx)
        mid[n, own] = tbl[n, own]
        return copies

    def scatter_second(n, copies):
        for copy in copies:
            copy.wait_recv()
        for p in range(nx):
            fwd[n, pl.ds(p * ny, ny)] = mid[n, pl.ds(p, ny, stride=nx)]
        copies = []
        for p in range(1, nx):
            peer = at(p, 0)
            copies.append(
                send(
                    fwd.at[n, pl.ds(pl.multiple_of(peer[0] * ny, ny), ny)],
                    got.at[n, pl.ds(pl.multiple_of(gx * ny, ny), ny)],
                    b_send.at[n, p], b_recv.at[n, p], peer,
                )
            )
        own = pl.ds(pl.multiple_of(gx * ny, ny), ny)
        got[n, own] = fwd[n, own]
        return copies

    weights = [
        send(wmsg, rwmsg, w_send.at[0], w_recv.at[0], south),
        send(wpack, rwpack, w_send.at[1], w_recv.at[1], east),
        send(wmsg.at[pl.ds(16, 8)], rwcorner, w_send.at[2], w_recv.at[2], corners[3]),
    ]
    coupling = scatter_first(0)

    for copy in loads[5:]:
        copy.wait()

    def guard(ref, ends):
        for field in range(2):
            base = FBASE + field * FSPAN
            if "top" in ends:
                ref[pl.ds(base, ROWS)] = ref[pl.ds(base + ROWS, ROWS)]
            if "low" in ends:
                ref[pl.ds(base + (ZO + 1) * ROWS, ROWS)] = ref[pl.ds(base + ZO * ROWS, ROWS)]

    def put_pack(r, group, field, chunk, t, values):
        first, lane = packed_place(group, field, chunk)
        rows = pl.ds(first + t * SUB, SUB)
        pair = pair8 - lane // 2
        acc = opack[r, rows]
        for j, value in enumerate(values):
            acc = jnp.where(pair == j, roll(value, lane + 2 * j + 1, 1), acc)
        opack[r, rows] = acc

    def put_rows(r, ref, group, field, chunk):
        base = FBASE + field * FSPAN + ROWS + chunk * (CHUNK * ROWS)
        start = level_row(group, field, chunk)
        rows = pl.ds(start if isinstance(start, int) else pl.multiple_of(start, SUB), SUB)
        orow[r, 0, rows] = ref[pl.ds(base, SUB, stride=ROWS)]
        orow[r, 1, rows] = ref[pl.ds(base + ROWS - 1, SUB, stride=ROWS)]

    def first_edges(group, chunk):
        for field in range(2):
            base = FBASE + field * FSPAN + ROWS + chunk * (CHUNK * ROWS)
            if not isinstance(base, int):
                base = pl.multiple_of(base, SUB)
            for t in range(TILES):
                values = [fa[pl.ds(base + j * ROWS + t * SUB, SUB)] for j in range(CHUNK)]
                put_pack(0, group, field, chunk, t, values)
            put_rows(0, fa, group, field, chunk)

    def over_chunks(group, step):
        def body(chunk, carry):
            step(group, chunk)
            return carry

        if group == "top":
            step(group, 0)
        else:
            lax.fori_loop(*GROUPS[group][0], body, 0)

    def send_ocean(r, group):
        n = ORDER.index(group)
        cols, rows = (pl.ds(*GROUPS[group][m]) for m in (1, 2))
        return [
            send(orow.at[r, 0, rows], rrow.at[r, 1, rows], o_send.at[r, n, 0], o_recv.at[r, n, 0], north),
            send(orow.at[r, 1, rows], rrow.at[r, 0, rows], o_send.at[r, n, 1], o_recv.at[r, n, 1], south),
            send(opack.at[r, cols], rpack.at[r, 1, cols], o_send.at[r, n, 2], o_recv.at[r, n, 2], west),
            send(opack.at[r, cols], rpack.at[r, 0, cols], o_send.at[r, n, 3], o_recv.at[r, n, 3], east),
        ]

    ocean = {}
    guard(fa, ("top", "low"))
    wet = omask[...].astype(F32)
    diffusion = diff[...]
    orow[0, 0, pl.ds(STATIC_ROW, 1)] = diffusion[0:1]
    orow[0, 0, pl.ds(STATIC_ROW + 1, 1)] = wet[0:1]
    orow[0, 1, pl.ds(STATIC_ROW, 1)] = diffusion[ROWS - 1 :]
    orow[0, 1, pl.ds(STATIC_ROW + 1, 1)] = wet[ROWS - 1 :]
    for t in range(TILES):
        rows = pl.ds(4 * ROWS + t * SUB, SUB)
        acc = opack[0, rows]
        acc = jnp.where(pair8 == 32, roll(diffusion[t * SUB : (t + 1) * SUB], 65, 1), acc)
        acc = jnp.where(pair8 == 33, roll(wet[t * SUB : (t + 1) * SUB], 67, 1), acc)
        opack[0, rows] = acc
    for group in ("low", "top", "mid"):
        over_chunks(group, first_edges)
        ocean[group] = send_ocean(0, group)

    for copy in weights:
        copy.wait_recv()
    row_mu[...] = rwmsg[pl.ds(0, 16)] * has_n
    even = (lane8 & 1) == 0
    for t in range(TILES):
        col_mu[pl.ds(SUB + t * SUB, SUB)] = jnp.where(even, rwpack[pl.ds(t * SUB, SUB)] * has_w, 0.0)
    even1 = (iota((1, LANES), 1) & 1) == 0
    col_mu[pl.ds(SUB - 1, 1)] = jnp.where(even1, rwcorner[pl.ds(0, 1)] * (has_w * has_n), 0.0)

    def put_ice_edges(r, ref):
        for c in range(2):
            for edge in range(2):
                start = c * NODES * VSPAN + edge * (ROWS - 1)
                imsg[r, edge, pl.ds(c * 16, 16)] = ref[pl.ds(start, 16, stride=VSPAN)]
        imsg[r, 0, pl.ds(32, 1)] = ipack[r, pl.ds(0, 1)]
        imsg[r, 1, pl.ds(32, 1)] = ipack[r, pl.ds(ROWS - 1, 1)]

    def send_ice(r):
        copies = [
            send(imsg.at[r, 0], rmsg.at[r, 1], i_send.at[r, 0], i_recv.at[r, 0], north),
            send(imsg.at[r, 1], rmsg.at[r, 0], i_send.at[r, 1], i_recv.at[r, 1], south),
            send(ipack.at[r], rside.at[r, 1], i_send.at[r, 2], i_recv.at[r, 2], west),
            send(ipack.at[r], rside.at[r, 0], i_send.at[r, 3], i_recv.at[r, 3], east),
        ]
        for n, device in enumerate(corners):
            src = imsg.at[r, n // 2, pl.ds(32, 8)]
            copies.append(send(src, rcorner.at[r, 3 - n], i_send.at[r, 4 + n], i_recv.at[r, 4 + n], device))
        return copies

    for t in range(TILES):
        cols = col_mu[pl.ds(SUB + t * SUB, SUB)] + col_mu[pl.ds(SUB - 1 + t * SUB, SUB)]
        cols = cols + roll(cols, 2, 1)
        acc = jnp.zeros((SUB, LANES), F32)
        below = None
        for k in range(NODES):
            layer = None
            if k < CELLS:
                start = SUB + k * ROWS + t * SUB
                up = mu[pl.ds(start - 1, SUB)]
                if t == 0:
                    up = jnp.where(sub8 == 0, row_mu[pl.ds(k, 1)], up)
                layer = mu[pl.ds(start, SUB)] + up
            total = layer if below is None else (below if layer is None else layer + below)
            below = layer
            left = jnp.where(lane8 == 0, roll(cols, -2 * k, 1), roll(total, 1, 1))
            diagonal = DIAGONAL * (total + left) + shift_term
            if k == 0:
                diagonal = diagonal + drag[pl.ds(t * SUB, SUB)]
            factor = relax_weight / diagonal
            rdiag[pl.ds(k * ROWS + t * SUB, SUB)] = factor
            for c in range(2):
                value = force[pl.ds((c * NODES + k) * ROWS + t * SUB, SUB)] * factor
                va[pl.ds((c * NODES + k) * VSPAN + t * SUB, SUB)] = value
                acc = jnp.where(pair8 == 32 * c + k, roll(value, 64 * c + 2 * k + 1, 1), acc)
        ipack[0, pl.ds(t * SUB, SUB)] = acc
    put_ice_edges(0, va)
    ice = send_ice(0)

    def take_ocean(r, group):
        for copy in ocean[group]:
            copy.wait_recv()
        first, count = GROUPS[group][1]
        for n in range(count // SUB):
            rows = pl.ds(first + n * SUB, SUB)
            from_e = roll(rpack[r, 1, rows], -1, 1)
            from_w = roll(rpack[r, 0, rows], 1, 1)
            merged[rows] = jnp.where(even, from_e, from_w)

    coupling = scatter_second(0, coupling)
    take_ocean(0, "top")
    for t in range(TILES):
        rows = slice(t * SUB, (t + 1) * SUB)
        d, w = diffusion[rows], wet[rows]

        def around(mine, plane, n):
            whole = plane
            up = roll(mine, 1, 0)
            above = rrow[0, 0, pl.ds(STATIC_ROW + n, 1)] if t == 0 else whole[t * SUB - 1 : t * SUB]
            up = jnp.where(sub8 == 0, above, up)
            down = roll(mine, -1, 0)
            below = rrow[0, 1, pl.ds(STATIC_ROW + n, 1)] if t == TILES - 1 else whole[(t + 1) * SUB : (t + 1) * SUB + 1]
            down = jnp.where(sub8 == SUB - 1, below, down)
            edge = roll(merged[pl.ds(4 * ROWS + t * SUB, SUB)], 127 - 64 - 2 * n, 1)
            left = jnp.where(lane8 == 0, edge, roll(mine, 1, 1))
            right = jnp.where(lane8 == LANES - 1, edge, roll(mine, -1, 1))
            return up, down, left, right

        near_d = around(d, diffusion, 0)
        up_w, down_w, left_w, right_w = around(w, wet, 1)
        if t == 0:
            up_w = jnp.where(sub8 == 0, up_w * has_n, up_w)
        if t == TILES - 1:
            down_w = jnp.where(sub8 == SUB - 1, down_w * has_s, down_w)
        left_w = jnp.where(lane8 == 0, left_w * has_w, left_w)
        right_w = jnp.where(lane8 == LANES - 1, right_w * has_e, right_w)
        total = 2.0 * vert_mix * w
        for n, (near, near_w) in enumerate(zip(near_d, (up_w, down_w, left_w, right_w))):
            face = 0.5 * (d + near) * w * near_w
            coef[pl.ds((n + 1) * ROWS + t * SUB, SUB)] = face
            total = total + face
        coef[pl.ds(t * SUB, SUB)] = 1.0 - total
        coef[pl.ds(5 * ROWS + t * SUB, SUB)] = vert_mix * w

    def melt_of(temp_top, salt_top, t):
        freezing = freeze_slope * (salt_ref + salt_top) + freeze_base - freeze_depth * draft[pl.ds(t * SUB, SUB)]
        return heat_gamma * (temp_top - freezing) * (10.0 * coef[pl.ds(5 * ROWS + t * SUB, SUB)])

    def ocean_chunk(s, group, chunk, src, dst):
        for field in range(2):
            base = FBASE + field * FSPAN + ROWS + chunk * (CHUNK * ROWS)
            if not isinstance(base, int):
                base = pl.multiple_of(base, SUB)
            values = src[pl.ds(base, CHUNK * ROWS)]
            high = values.astype(jnp.bfloat16)
            rest = (values - high.astype(F32)).astype(jnp.bfloat16)
            both = jnp.concatenate([high, rest], axis=1)
            sides[pl.ds(field * CHUNK * ROWS, CHUNK * ROWS)] = jnp.dot(
                both, shifts[...], preferred_element_type=F32
            )
        for t in range(TILES):
            cs = [coef[pl.ds(n * ROWS + t * SUB, SUB)] for n in range(6)]
            first = []
            for field in range(2):
                base = FBASE + field * FSPAN + ROWS + chunk * (CHUNK * ROWS) + t * SUB
                if not isinstance(base, int):
                    base = pl.multiple_of(base, SUB)
                vec, lane = packed_place(group, field, chunk)
                packed = merged[pl.ds(vec + t * SUB, SUB)]
                prev = src[pl.ds(base - ROWS, SUB)]
                cur = src[pl.ds(base, SUB)]
                news = []
                for j in range(CHUNK):
                    row = base + j * ROWS
                    nxt = src[pl.ds(row + ROWS, SUB)]
                    up = src[pl.ds(row - 1, SUB)]
                    down = src[pl.ds(row + 1, SUB)]
                    level = level_row(group, field, chunk) + j
                    if t == 0:
                        up = jnp.where(sub8 == 0, rrow[s, 0, pl.ds(level, 1)], up)
                    if t == TILES - 1:
                        down = jnp.where(sub8 == SUB - 1, rrow[s, 1, pl.ds(level, 1)], down)
                    edge = roll(packed, 127 - 2 * j - lane, 1)
                    beside = pl.ds(field * CHUNK * ROWS + j * ROWS + t * SUB, SUB)
                    left = jnp.where(lane8 == 0, edge, sides[beside, :LANES])
                    right = jnp.where(lane8 == LANES - 1, edge, sides[beside, LANES:])
                    new = (
                        cs[0] * cur
                        + (cs[1] * up + cs[2] * down)
                        + (cs[3] * left + cs[4] * right)
                        + cs[5] * (prev + nxt)
                    )
                    news.append(new)
                    prev, cur = cur, nxt
                first.append(news)
            if group == "top":
                temp_top, salt_top = first[0][0], first[1][0]
                rate = melt_of(temp_top, salt_top, t)
                first[0][0] = temp_top - heat_factor * rate
                first[1][0] = salt_top - salt_factor * rate * (salt_ref + salt_top) / salt_ref
            for field in range(2):
                for j in range(CHUNK):
                    new = first[field][j]
                    if s < STEPS - 1:
                        row = FBASE + field * FSPAN + ROWS + chunk * (CHUNK * ROWS) + t * SUB + j * ROWS
                        if not isinstance(row, int):
                            row = pl.multiple_of(row, SUB)
                        dst[pl.ds(row, SUB)] = new
                    else:
                        row = chunk * (CHUNK * ROWS) + j * ROWS + t * SUB
                        if not isinstance(row, int):
                            row = pl.multiple_of(row, SUB)
                        dst[field][pl.ds(row, SUB)] = new
                if s < STEPS - 1:
                    put_pack(s + 1, group, field, chunk, t, first[field])
        if s < STEPS - 1:
            for field in range(2):
                put_rows(s + 1, dst, group, field, chunk)

    def ocean_part(s, group, src, dst, taken=False):
        if not taken:
            take_ocean(s, group)
        over_chunks(group, lambda part, chunk: ocean_chunk(s, part, chunk, src, dst))
        if s < STEPS - 1:
            guard(dst, (group,))
            ocean[group] = send_ocean(s + 1, group)

    def ice_sweep(r, copies, src, dst):
        last = r == SWEEPS - 1
        for copy in copies:
            copy.wait_recv()
        for c in range(2):
            for k in range(NODES):
                src[pl.ds((c * NODES + k) * VSPAN + ROWS, 1)] = rmsg[r, 1, pl.ds(c * 16 + k, 1)] * has_s
        for t in range(TILES):
            rows = pl.ds(t * SUB, SUB)
            edge_e[rows] = rside[r, 1, rows] * has_e
            col_lo[pl.ds(SUB + t * SUB, SUB)] = rside[r, 0, rows] * has_w
            col_hi[pl.ds(SUB + t * SUB, SUB)] = roll(ipack[r, rows], -1, 1)
        edge_e[pl.ds(ROWS, 1)] = rcorner[r, 3, pl.ds(0, 1)] * (has_e * has_s)
        col_lo[pl.ds(SUB - 1, 1)] = rcorner[r, 0, pl.ds(0, 1)] * (has_w * has_n)
        col_lo[pl.ds(SUB + ROWS, 1)] = rcorner[r, 2, pl.ds(0, 1)] * (has_w * has_s)
        col_hi[pl.ds(SUB - 1, 1)] = roll(rmsg[r, 0, pl.ds(32, 1)] * has_n, -1, 1)
        col_hi[pl.ds(SUB + ROWS, 1)] = roll(rmsg[r, 1, pl.ds(32, 1)] * has_s, -1, 1)
        for t in range(TILES + 1):
            start = SUB - 1 + t * SUB
            if t == TILES:
                start = ROWS
            lo0, lo1 = col_lo[pl.ds(start, SUB)], col_lo[pl.ds(start + 1, SUB)]
            hi0, hi1 = col_hi[pl.ds(start, SUB)], col_hi[pl.ds(start + 1, SUB)]
            planes = []
            for c in range(2):
                parts = [roll(value, 64 * c, 1) for value in (lo0, hi0, lo1, hi1)]
                low = plane_sums(*parts)
                planes += [low, {key: roll(value, -2, 1) for key, value in low.items()}]
            fu, fv = element_forces(*planes, col_mu[pl.ds(start, SUB)])
            for c, f in enumerate((fu, fv)):
                low, high = lower_part(f), upper_part(f)
                node = {key: low[key] + roll(high[key], 2, 1) for key in low}
                behind = {x: node[x + "s"] + node[x + "d"] for x in "sd"}
                col_q[2 * c, pl.ds(start - SUB + 1, SUB)] = behind["s"] - behind["d"]
                col_q[2 * c + 1, pl.ds(start - SUB + 1, SUB)] = behind["s"] + behind["d"]
        lane16, sub16 = iota((16, LANES), 1), iota((16, LANES), 0)

        def upright(row, offset):
            chosen = jnp.where(lane16 == 2 * sub16 + offset, row, 0.0)
            return jnp.sum(chosen, axis=1, keepdims=True)

        planes = []
        for c in range(2):
            lo = rmsg[r, 0, pl.ds(c * 16, 16)]
            hi = imsg[r, 0, pl.ds(c * 16, 16)]
            lo_end = upright(rcorner[r, 1, pl.ds(0, 1)] * (has_e * has_n), 64 * c + 1)
            hi_end = upright(edge_e[pl.ds(0, 1)], 64 * c + 1)
            lo_right = jnp.where(lane16 == LANES - 1, lo_end, roll(lo, -1, 1))
            hi_right = jnp.where(lane16 == LANES - 1, hi_end, roll(hi, -1, 1))
            low = plane_sums(lo, lo_right, hi, hi_right)
            planes += [low, {key: roll(value, -1, 0) for key, value in low.items()}]
        fu, fv = element_forces(*planes, row_mu[...])
        for c, f in enumerate((fu, fv)):
            low, high = lower_part(f), upper_part(f)
            node = {key: low[key] + roll(high[key], 1, 0) for key in low}
            for n, sign in enumerate((-1.0, 1.0)):
                parts = [node[x + "s"] + sign * node[x + "d"] for x in "sd"]
                row_q[pl.ds((2 * n + c) * 16, 16)] = parts[0] + parts[1]
        for c in range(2):
            for k in range(NODES):
                shift = 127 - (64 * c + 2 * k + 1)
                for t in range(TILES + 1):
                    rows = pl.ds((c * NODES + k) * VSPAN + t * SUB, SUB)
                    edge = roll(edge_e[pl.ds(t * SUB, SUB)], shift, 1)
                    vright[rows] = jnp.where(lane8 == LANES - 1, edge, roll(src[rows], -1, 1))
        pass_down = {}
        for t in range(TILES):
            below, carried = None, None
            for k in range(NODES + 1):
                planes = None
                if k < NODES:
                    planes = []
                    for c in range(2):
                        start = (c * NODES + k) * VSPAN + t * SUB
                        lo, hi = pl.ds(start, SUB), pl.ds(start + 1, SUB)
                        planes.append(plane_sums(src[lo], vright[lo], src[hi], vright[hi]))
                if k >= 1:
                    level = k - 1
                    nodes, ups = [None, None], [None, None]
                    if level < CELLS:
                        weight = mu[pl.ds(SUB + level * ROWS + t * SUB, SUB)]
                        forces = element_forces(below[0], planes[0], below[1], planes[1], weight)
                        for c in range(2):
                            nodes[c], ups[c] = lower_part(forces[c]), upper_part(forces[c])
                            if carried is not None:
                                nodes[c] = {key: nodes[c][key] + carried[c][key] for key in nodes[c]}
                    else:
                        nodes = carried
                    carried = ups
                    for c in range(2):
                        node = nodes[c]
                        row = pl.ds((c * NODES + level) * ROWS + t * SUB, SUB)
                        for n, (sign, place) in enumerate(((-1.0, low_y), (1.0, high_y))):
                            parts = [node[x + "s"] + sign * node[x + "d"] for x in "sd"]
                            down = roll(parts[0] + parts[1], 1, 0)
                            if t == 0:
                                over = row_q[pl.ds((2 * n + c) * 16 + level, 1)]
                            else:
                                over = pass_down[n, c, level]
                            pass_down[n, c, level] = down[0:1]
                            place[row] = parts[0] - parts[1] + jnp.where(sub8 == 0, over, down)
                below = planes
        for c in range(2):
            for t in range(TILES):
                strip = col_q[2 * c, pl.ds(1 + t * SUB, SUB)] + col_q[2 * c + 1, pl.ds(t * SUB, SUB)]
                for level in range(NODES):
                    at_row = (c * NODES + level) * ROWS + t * SUB
                    row = pl.ds(at_row, SUB)
                    before = jnp.where(lane8 == 0, roll(strip, -2 * level, 1), roll(high_y[row], 1, 1))
                    value = src[pl.ds((c * NODES + level) * VSPAN + t * SUB, SUB)]
                    extra = shift_term
                    if level == 0:
                        extra = shift_term + drag[pl.ds(t * SUB, SUB)]
                    applied = low_y[row] + before + extra * value
                    value = value + (force[row] - applied) * rdiag[pl.ds(level * ROWS + t * SUB, SUB)]
                    if last:
                        dst[row] = value
                    else:
                        dst[pl.ds((c * NODES + level) * VSPAN + t * SUB, SUB)] = value
        if last:
            return None
        for t in range(TILES):
            acc = jnp.zeros((SUB, LANES), F32)
            for c in range(2):
                for level in range(NODES):
                    value = dst[pl.ds((c * NODES + level) * VSPAN + t * SUB, SUB)]
                    acc = jnp.where(pair8 == 32 * c + level, roll(value, 64 * c + 2 * level + 1, 1), acc)
            ipack[r + 1, pl.ds(t * SUB, SUB)] = acc
        put_ice_edges(r + 1, dst)
        return send_ice(r + 1)

    ocean_part(0, "low", fa, fb)
    ocean_part(0, "mid", fa, fb)
    for copy in coupling:
        copy.wait_recv()
    draft[...] = pick(by_device(from_col), got[0])
    ocean_part(0, "top", fa, fb, True)
    ice = ice_sweep(0, ice, va, vb)
    ocean_part(1, "low", fb, fa)
    ocean_part(1, "top", fb, fa)
    ocean_part(1, "mid", fb, fa)
    ice = ice_sweep(1, ice, vb, va)
    ocean_part(2, "top", fa, fb)
    ocean_part(2, "low", fa, fb)
    ocean_part(2, "mid", fa, fb)
    ocean_part(3, "top", fb, (temp_out, salt_out))
    for t in range(TILES):
        rows = pl.ds(t * SUB, SUB)
        pad_in[rows] = melt_of(temp_out[rows], salt_out[rows], t)
    tbl[1] = pick(by_slot(from_row), pad_in[...])
    coupling = scatter_first(1)
    ice_sweep(2, ice, va, vel_out)
    ocean_part(3, "low", fb, (temp_out, salt_out))
    coupling = scatter_second(1, coupling)
    ocean_part(3, "mid", fb, (temp_out, salt_out))
    for copy in coupling:
        copy.wait_recv()
    melt = pick(by_device(to_col), got[1])
    thick_out[...] = thick[...] - melt_factor * melt * wet_ice
    for copy in sends:
        copy.wait_send()


def write_out(*refs):
    srcs, dsts, sem = refs[:4], refs[4:8], refs[8]
    copies = [pltpu.make_async_copy(src, dst, sem.at[n]) for n, (src, dst) in enumerate(zip(srcs, dsts))]
    for copy in copies:
        copy.start()
    for copy in copies:
        copy.wait()


def per_device(
    ice_force, ice_visc, ice_drag, ice_mask, ice_thick, ice_target,
    ocean_temp, ocean_salt, ocean_diff, ocean_mask, ocean_source,
):
    def flat(array):
        return pltpu.with_memory_space_constraint(array.reshape(-1, LANES), pltpu.HBM)

    def held(array):
        return pltpu.with_memory_space_constraint(array, pltpu.HBM)

    vmem = pl.BlockSpec(memory_space=pltpu.VMEM)
    hbm = pl.BlockSpec(memory_space=pltpu.HBM)
    dma = pltpu.SemaphoreType.DMA

    def buf(*shape):
        return pltpu.VMEM((*shape, LANES), F32)

    nx, ny = lax.axis_size("gx"), lax.axis_size("gy")
    whole = pltpu.VMEM((ROWS, LANES), jnp.int32)
    ids = pltpu.SMEM((ROWS,), jnp.int32)
    scratch = [
        buf(2 * NODES * ROWS), buf(CELLS * ROWS), buf(ROWS), whole, buf(ROWS), ids, buf(ROWS), whole, ids,
        buf(FROWS), buf(FROWS), buf(6 * ROWS), buf(STEPS, PACK_ROWS), buf(STEPS, 2, 2 * ZO + SUB),
        buf(STEPS, 2, PACK_ROWS), buf(STEPS, 2, 2 * ZO + SUB), buf(PACK_ROWS),
        buf(VROWS), buf(VROWS), buf(2 * SUB + CELLS * ROWS), buf(NODES * ROWS),
        buf(SWEEPS, ROWS), buf(SWEEPS, 2, 40), buf(SWEEPS, 2, ROWS), buf(SWEEPS, 2, 40), buf(SWEEPS, 4, SUB),
        buf(VROWS), buf(2 * NODES * ROWS), buf(2 * NODES * ROWS),
        pltpu.VMEM((2 * LANES, 2 * LANES), jnp.bfloat16), pltpu.VMEM((2 * CHUNK * ROWS, 2 * LANES), F32),
        buf(ROWS + SUB), buf(ROWS + 2 * SUB), buf(ROWS + 2 * SUB), buf(ROWS + 2 * SUB),
        buf(4, ROWS + SUB), buf(64), buf(16),
        buf(ROWS), buf(24), buf(ROWS), buf(24), buf(SUB),
        buf(LANES), buf(ROWS), buf(2, LANES), buf(2, LANES), buf(2, LANES), buf(2, LANES),
        dma((11,)), dma((STEPS, 3, 4)), dma((STEPS, 3, 4)), dma((SWEEPS, 8)), dma((SWEEPS, 8)),
        dma((3,)), dma((3,)), dma((2, ny)), dma((2, ny)), dma((2, nx)), dma((2, nx)),
    ]
    shapes = [
        jax.ShapeDtypeStruct((2 * NODES * ROWS, LANES), F32),
        jax.ShapeDtypeStruct((ROWS, LANES), F32),
        jax.ShapeDtypeStruct((ZO * ROWS, LANES), F32),
        jax.ShapeDtypeStruct((ZO * ROWS, LANES), F32),
    ]
    results = pl.pallas_call(
        kernel,
        out_shape=shapes,
        in_specs=[hbm] * 11,
        out_specs=[vmem] * 4,
        scratch_shapes=scratch,
        compiler_params=pltpu.CompilerParams(
            collective_id=0, has_side_effects=True, vmem_limit_bytes=40 * 1024 * 1024
        ),
    )(
        flat(ice_force), flat(ice_visc), held(ice_drag), held(ice_mask), held(ice_thick), held(ice_target),
        flat(ocean_temp), flat(ocean_salt), held(ocean_diff), held(ocean_mask), held(ocean_source),
    )
    velocity, thickness, temp, salt = pl.pallas_call(
        write_out,
        out_shape=shapes,
        in_specs=[pl.BlockSpec(memory_space=pl.ANY)] * 4,
        out_specs=[pl.BlockSpec(memory_space=pl.ANY)] * 4,
        scratch_shapes=[dma((4,))],
        compiler_params=pltpu.CompilerParams(vmem_limit_bytes=1024 * 1024),
    )(*results)
    return (
        velocity.reshape(ice_force.shape),
        thickness,
        temp.reshape(ocean_temp.shape),
        salt.reshape(ocean_salt.shape),
    )


def solution(mesh):
    in_specs = (
        P(None, None, "gx", "gy"),
        P(None, "gx", "gy"),
        P("gx", "gy"),
        P("gx", "gy"),
        P("gx", "gy"),
        P(("gx", "gy")),
        P(None, "gx", "gy"),
        P(None, "gx", "gy"),
        P("gx", "gy"),
        P("gx", "gy"),
        P(("gx", "gy")),
    )
    out_specs = (P(None, None, "gx", "gy"), P("gx", "gy"), P(None, "gx", "gy"), P(None, "gx", "gy"))
    return jax.shard_map(per_device, mesh=mesh, in_specs=in_specs, out_specs=out_specs, check_vma=False)
```
